32 devices in a mesh: row: 16 (over z, y, x), col: 2 (over core).
Axes of the slice: x: 2, y: 2, z: 4, core: 2. Of those that a mesh axis runs over, the one named last changes fastest.
Arguments:
- hamiltonian_blocks: bfloat16 [16, 2, 64, 128, 128], P('row', 'col'), may hold values from -0.046875 to 0.046875
- block_rows: int32 [16, 2, 64], P('row', 'col'), may hold values from 0 to 1, as said below
- block_cols: int32 [16, 2, 64], P('row', 'col'), may hold values from 0 to 15
- block_counts: int32 [16, 2], P('row', 'col'), may hold values from 16 to 64, as said below
- initial: float32 [4096, 128], P(('row', 'col')), may hold values from -6 to 6
- center: float32 [1], replicated, may hold values from -0.3 to 0.3
- halfwidth: float32 [1], replicated, may hold values from 1 to 1.5
Outputs:
- filtered: float32 [4096, 128], P(('row', 'col'))
The draws below stay inside these ranges and needn't reach their ends.
Inputs may be any that keep to these rules, and one draw needn't show every extreme that they name: `block_rows`: padded slots hold arbitrary values. `block_counts`: some tile is full in every draw.
All inputs are finite; a program needn't handle non-finite values.
Results may differ from the reference program's by a relative error of at most 0.0068.
Values may be sent and summed in bfloat16 or wider, within the bound.
No kernel may reach another device: no remote copies, remote signals or barrier semaphores. Data moves between devices by JAX's collectives and lax.ppermute only.
A program may use at most 128 MiB of HBM per device.

```python
import jax
import jax.numpy as jnp
from jax import lax

ORB = 128
VECS = 128
SLAB = 1
STACK = 64
DEGREE = 3
ORDER = 4096
N_ROW = 16
N_COL = 2


def pattern_pair(key):
    folded = jax.random.fold_in(key, 7301)
    first_key, second_key = jax.random.split(folded, 2)
    shape = (N_ROW, N_COL, STACK)
    grid_row = jnp.broadcast_to(jnp.arange(N_ROW, dtype=jnp.int32)[:, None, None], shape)
    slot_index = jnp.broadcast_to(jnp.arange(STACK, dtype=jnp.int32)[None, None, :], shape)
    slot_cols = jax.random.randint(first_key, shape, 0, N_ROW * SLAB, dtype=jnp.int32)
    forced = (grid_row + N_ROW - 1) % N_ROW * SLAB + slot_cols % SLAB
    slot_cols = jnp.where(slot_index == 0, forced, slot_cols)
    slot_rows = jax.random.randint(second_key, shape, 0, N_COL * SLAB, dtype=jnp.int32)
    return (slot_rows, slot_cols)


def draw_block_rows(key, part):
    return pattern_pair(key)[0]


def draw_block_cols(key, part):
    return pattern_pair(key)[1]


def draw_block_counts(key, part):
    folded = jax.random.fold_in(key, 9127)
    count_key, full_key = jax.random.split(folded, 2)
    counts = jax.random.randint(count_key, (N_ROW * N_COL,), STACK // 4, STACK + 1, dtype=jnp.int32)
    chosen = jax.random.randint(full_key, (), 0, N_ROW * N_COL, dtype=jnp.int32)
    counts = jnp.where(jnp.arange(N_ROW * N_COL, dtype=jnp.int32) == chosen, STACK, counts)
    return counts.reshape(N_ROW, N_COL)


def block_levels(rng, shape, shards, low, largest):
    level = 1.0
    for position, blocks in shards:
        heights = jax.random.uniform(jax.random.fold_in(jax.random.fold_in(rng, 6), position), (blocks,), jnp.float32, low / len(shards), largest / len(shards))
        level = level * jnp.repeat(jnp.exp(heights), shape[position] // blocks).reshape((-1,) + (1,) * (len(shape) - 1 - position))
    return level


def gaussian(rng, shape, deviation, limit, cuts=(), held_as=jnp.bfloat16):
    drawn = jax.random.normal(rng, shape, jnp.float32) * deviation
    if len(cuts) > 0:
        drawn = block_levels(rng, shape, cuts, -0.22, 0.18) * drawn
    return jnp.clip(drawn, min=-limit, max=limit).astype(held_as)


def setup_inputs(seed: int = 0) -> dict:
    key_of = jax.random.split(jax.random.key(seed), 8)
    return {
        "hamiltonian_blocks": gaussian(key_of[0], (N_ROW, N_COL, STACK, ORB, ORB), (2 * STACK * ORB) ** -0.5, 0.046875, ((0, 16), (1, 2))),
        "block_rows": draw_block_rows(jax.random.fold_in(key_of[7], 71), 0),
        "block_cols": draw_block_cols(jax.random.fold_in(key_of[7], 71), 0),
        "block_counts": draw_block_counts(jax.random.fold_in(key_of[7], 71), 0),
        "initial": gaussian(key_of[4], (ORDER, VECS), 1.0, 6.0, ((0, 32),), jnp.float32),
        "center": jnp.clip(jax.random.uniform(key_of[5], (1,), jnp.float32, -0.3, 0.3), -0.3, 0.3),
        "halfwidth": jnp.clip(jax.random.uniform(key_of[6], (1,), jnp.float32, 1.0, 1.5), 1.0, 1.5),
    }


def reference(hamiltonian_blocks, block_rows, block_cols, block_counts, initial, center, halfwidth):
    total_blocks = SLAB * N_ROW * N_COL

    def apply_operator(panel):
        source = panel.reshape(total_blocks, ORB, VECS).astype(jnp.float32)

        def visit(carried, tile_index):
            grid_row = tile_index // N_COL
            grid_col = tile_index % N_COL
            stacked = hamiltonian_blocks[grid_row, grid_col].astype(jnp.float32)
            slot_rows = block_rows[grid_row, grid_col].astype(jnp.int32)
            slot_cols = block_cols[grid_row, grid_col].astype(jnp.int32)
            live_count = block_counts[grid_row, grid_col]
            global_rows = (grid_row * (N_COL * SLAB) + slot_rows).astype(jnp.int32)
            global_cols = (((slot_cols // SLAB) * N_COL + grid_col) * SLAB + slot_cols % SLAB).astype(jnp.int32)
            is_live = (jnp.arange(STACK, dtype=jnp.int32) < live_count).astype(jnp.float32)[:, None, None]
            forward = jnp.einsum("sab,sbv->sav", stacked, source[global_cols], precision=lax.Precision.HIGHEST) * is_live
            backward = jnp.einsum("sba,sbv->sav", stacked, source[global_rows], precision=lax.Precision.HIGHEST) * is_live
            carried = carried.at[global_rows].add(forward).at[global_cols].add(backward)
            return carried, None

        zeros = jnp.zeros((total_blocks, ORB, VECS), jnp.float32)
        result, unused = lax.scan(visit, zeros, jnp.arange(N_ROW * N_COL, dtype=jnp.int32))
        return result.reshape(total_blocks * ORB, VECS)

    previous = initial
    current = initial
    for degree_step in range(DEGREE):
        applied = apply_operator(current.astype(jnp.bfloat16))
        shifted = (applied - center[0] * current) / halfwidth[0]
        if degree_step == 0:
            following = shifted
        else:
            following = 2.0 * shifted - previous
        previous = current
        current = following
    return current
```

```python
import functools

import jax
import jax.numpy as jnp
from jax import lax
from jax.experimental import pallas as pl
from jax.experimental.pallas import tpu as pltpu
from jax.sharding import PartitionSpec as P

DEGREE = 3
RADIX = 4
CHUNK = 8


def stage_strides(size):
    found = []
    stride = 1
    while stride < size:
        radix = RADIX if size % (stride * RADIX) == 0 else size // stride
        found.append((stride, radix))
        stride *= radix
    return found[::-1]


def arrival_order(strides):
    order = [0]
    for stride, radix in strides:
        order = [k * stride ^ offset for k in range(radix) for offset in order]
    return order


def swap(x, axis, size, offset):
    return lax.ppermute(x, axis, [(source, source ^ offset) for source in range(size)])


def build_tile(rows, cols, count, stacked, grid_rows, grid_cols):
    slots, orb, _ = stacked.shape
    chunk = CHUNK if slots % CHUNK == 0 else slots
    cells = grid_rows * grid_cols

    def kernel(rows_ref, cols_ref, count_ref, stack_ref, dense_ref, acc_ref):
        step = pl.program_id(0)

        @pl.when(step == 0)
        def _():
            acc_ref[...] = jnp.zeros_like(acc_ref)

        first = step * chunk

        def add(s, carry):
            cell = cols_ref[first + s] * grid_cols + rows_ref[first + s]
            acc_ref[cell] += stack_ref[s].astype(jnp.float32)
            return carry

        lax.fori_loop(0, jnp.clip(count_ref[0] - first, 0, chunk), add, 0)

        @pl.when(step == pl.num_programs(0) - 1)
        def _():
            def put(cell, carry):
                dense_ref[cell] = acc_ref[cell].astype(jnp.bfloat16)
                return carry

            lax.fori_loop(0, cells, put, 0)

    return pl.pallas_call(
        kernel,
        grid_spec=pltpu.PrefetchScalarGridSpec(
            num_scalar_prefetch=3,
            grid=(slots // chunk,),
            in_specs=[pl.BlockSpec((chunk, orb, orb), lambda s, *_: (s, 0, 0))],
            out_specs=pl.BlockSpec((cells, orb, orb), lambda s, *_: (0, 0, 0)),
            scratch_shapes=[pltpu.VMEM((cells, orb, orb), jnp.float32)],
        ),
        out_shape=jax.ShapeDtypeStruct((cells, orb, orb), jnp.bfloat16),
        compiler_params=pltpu.CompilerParams(vmem_limit_bytes=60 * 2**20),
        name="build_tile",
    )(rows, cols, count, stacked)


def merge_tile(sources, targets, dense, received):
    cells, orb, _ = dense.shape
    grid_rows = sources.shape[0]
    grid_cols = targets.shape[0]

    def kernel(sources_ref, targets_ref, dense_ref, received_ref, tile_ref):
        first = sources_ref[pl.program_id(0)] * grid_cols
        for d in range(grid_cols):
            cell = first + targets_ref[d]
            block = dense_ref[cell].astype(jnp.float32) + received_ref[cell].astype(jnp.float32).T
            tile_ref[d * orb : (d + 1) * orb, :] = block.astype(jnp.bfloat16)

    return pl.pallas_call(
        kernel,
        grid_spec=pltpu.PrefetchScalarGridSpec(
            num_scalar_prefetch=2,
            grid=(grid_rows,),
            in_specs=[pl.BlockSpec((cells, orb, orb), lambda k, *_: (0, 0, 0))] * 2,
            out_specs=pl.BlockSpec((grid_cols * orb, orb), lambda k, *_: (0, k)),
        ),
        out_shape=jax.ShapeDtypeStruct((grid_cols * orb, grid_rows * orb), jnp.bfloat16),
        compiler_params=pltpu.CompilerParams(vmem_limit_bytes=60 * 2**20),
        name="merge_tile",
    )(sources, targets, dense, received)


def apply_tile(tile, pieces, grid_cols):
    height, width = tile.shape
    orb = height // grid_cols
    vectors = pieces[0].shape[1]

    def kernel(tile_ref, *refs):
        pieces_refs = refs[: len(pieces)]
        outs = refs[len(pieces) :]
        total = None
        at = 0
        for ref in pieces_refs:
            depth = ref.shape[0]
            part = jnp.dot(
                tile_ref[:, at : at + depth], ref[...], preferred_element_type=jnp.float32
            )
            total = part if total is None else total + part
            at += depth
        for d, out in enumerate(outs):
            out[...] = total[d * orb : (d + 1) * orb]

    return pl.pallas_call(
        kernel,
        out_shape=[jax.ShapeDtypeStruct((orb, vectors), jnp.float32)] * grid_cols,
        compiler_params=pltpu.CompilerParams(vmem_limit_bytes=60 * 2**20),
        name="apply_tile",
    )(tile, *pieces)


def body(hamiltonian_blocks, block_rows, block_cols, block_counts, initial, center, halfwidth):
    grid_rows = lax.axis_size("row")
    grid_cols = lax.axis_size("col")
    strides = stage_strides(grid_rows)

    def gather(panel):
        gathered = panel
        for index, (stride, radix) in enumerate(strides):
            parts = [gathered] + [
                swap(gathered, "row", grid_rows, k * stride) for k in range(1, radix)
            ]
            if index < len(strides) - 1:
                gathered = jnp.concatenate(parts, axis=0)
        return parts

    sources = jnp.array(arrival_order(strides), jnp.int32) ^ lax.axis_index("row")
    targets = jnp.arange(grid_cols, dtype=jnp.int32) ^ lax.axis_index("col")
    dense = build_tile(
        block_rows[0, 0], block_cols[0, 0], block_counts[0], hamiltonian_blocks[0, 0],
        grid_rows, grid_cols,
    )
    received = lax.all_to_all(dense, ("row", "col"), 0, 0)
    tile = merge_tile(sources, targets, dense, received)

    previous = initial
    current = initial
    for degree_step in range(DEGREE):
        pieces = gather(current.astype(jnp.bfloat16))
        own, *others = apply_tile(tile, pieces, grid_cols)
        applied = own
        for d, other in enumerate(others, start=1):
            applied = applied + swap(other, "col", grid_cols, d)
        shifted = (applied - center[0] * current) / halfwidth[0]
        following = shifted if degree_step == 0 else 2.0 * shifted - previous
        previous = current
        current = following
    return current


def solution(mesh):
    in_specs = (
        P("row", "col", None, None, None),
        P("row", "col", None),
        P("row", "col", None),
        P("row", "col"),
        P(("row", "col"), None),
        P(),
        P(),
    )
    out_specs = P(("row", "col"), None)
    return jax.shard_map(body, mesh=mesh, in_specs=in_specs, out_specs=out_specs, check_vma=False)
```

```python
import jax
import jax.numpy as jnp
from jax import lax
from jax.experimental import pallas as pl
from jax.experimental.pallas import tpu as pltpu
from jax.sharding import PartitionSpec as P

DEGREE = 3
RADIX = 4
CHUNK = 8
SPARE = 4 * 2**20

VMEM = pl.BlockSpec(memory_space=pltpu.VMEM)
SMEM = pl.BlockSpec(memory_space=pltpu.SMEM)
HBM = pl.BlockSpec(memory_space=pltpu.HBM)


def stage_strides(size):
    found = []
    stride = 1
    while stride < size:
        radix = RADIX if size % (stride * RADIX) == 0 else size // stride
        found.append((stride, radix))
        stride *= radix
    return found[::-1]


def arrival_order(strides):
    order = [0]
    for stride, radix in strides:
        order = [k * stride ^ offset for k in range(radix) for offset in order]
    return order


def swap(x, axis, size, offset):
    return lax.ppermute(x, axis, [(source, source ^ offset) for source in range(size)])


def build_tile(rows, cols, count, stacked, grid_rows, grid_cols):
    slots, orb, _ = stacked.shape
    chunk = CHUNK if slots % CHUNK == 0 else slots
    chunks = slots // chunk
    cells = grid_rows * grid_cols

    def kernel(rows_ref, cols_ref, count_ref, stack_ref, dense_ref, held_ref, acc_ref, sems):
        copies = [
            pltpu.make_async_copy(
                stack_ref.at[pl.ds(n * chunk, chunk)], held_ref.at[pl.ds(n * chunk, chunk)], sems.at[n]
            )
            for n in range(chunks)
        ]
        for copy in copies:
            copy.start()
        count = count_ref[0]
        acc_ref[...] = jnp.zeros_like(acc_ref)
        for n, copy in enumerate(copies):
            copy.wait()
            for s in range(n * chunk, (n + 1) * chunk):
                cell = jnp.where(s < count, cols_ref[s] * grid_cols + rows_ref[s], cells)
                acc_ref[cell] += held_ref[s].astype(jnp.float32)

        def put(cell, carry):
            dense_ref[cell] = acc_ref[cell].astype(jnp.bfloat16)
            return carry

        lax.fori_loop(0, cells, put, 0, unroll=4 if cells % 4 == 0 else 1)

    need = stacked.size * 2 + (cells + 1) * orb * orb * 4 + cells * orb * orb * 2
    return pl.pallas_call(
        kernel,
        in_specs=[SMEM, SMEM, SMEM, HBM],
        out_specs=VMEM,
        scratch_shapes=[
            pltpu.VMEM(stacked.shape, jnp.bfloat16),
            pltpu.VMEM((cells + 1, orb, orb), jnp.float32),
            pltpu.SemaphoreType.DMA((chunks,)),
        ],
        out_shape=jax.ShapeDtypeStruct((cells, orb, orb), jnp.bfloat16),
        compiler_params=pltpu.CompilerParams(vmem_limit_bytes=need + SPARE),
        name="build_tile",
    )(rows, cols, count, stacked)


def finish(total, first, orb, current_ref, previous_ref, center_ref, halfwidth_ref, outs):
    scale = (1.0 if first else 2.0) / jnp.full((1, total.shape[1]), halfwidth_ref[0])
    own = (total[:orb] - center_ref[0] * current_ref[...]) * scale
    outs[0][...] = own if first else own - previous_ref[...]
    for d in range(1, len(outs)):
        outs[d][...] = total[d * orb : (d + 1) * orb] * scale


def merge_apply(sources, targets, dense, received, pieces, current, center, halfwidth):
    cells, orb, _ = dense.shape
    grid_rows = sources.shape[0]
    grid_cols = targets.shape[0]
    vectors = current.shape[1]
    count = len(pieces)

    def kernel(sources_ref, targets_ref, center_ref, halfwidth_ref, dense_ref, received_ref, current_ref, *refs):
        piece_refs = refs[:count]
        tile_ref, *outs = refs[count:]
        total = None
        at = 0
        for ref in piece_refs:
            depth = ref.shape[0]
            for k in range(at // orb, (at + depth) // orb):
                first = sources_ref[k] * grid_cols
                for d in range(grid_cols):
                    cell = first + targets_ref[d]
                    turned = received_ref[cell].T.astype(jnp.float32)
                    block = (dense_ref[cell].astype(jnp.float32) + turned).astype(jnp.bfloat16)
                    tile_ref[d * orb : (d + 1) * orb, k * orb : (k + 1) * orb] = block
            part = jnp.dot(
                tile_ref[:, at : at + depth], ref[...], preferred_element_type=jnp.float32
            )
            total = part if total is None else total + part
            at += depth
        finish(total, True, orb, current_ref, None, center_ref, halfwidth_ref, outs)

    block = jax.ShapeDtypeStruct((orb, vectors), jnp.float32)
    return pl.pallas_call(
        kernel,
        in_specs=[SMEM] * 4 + [VMEM] * (3 + count),
        out_specs=[VMEM] * (1 + grid_cols),
        out_shape=[jax.ShapeDtypeStruct((grid_cols * orb, grid_rows * orb), jnp.bfloat16)]
        + [block] * grid_cols,
        compiler_params=pltpu.CompilerParams(vmem_limit_bytes=dense.size * 6 + 2 * SPARE),
        name="merge_apply",
    )(sources, targets, center, halfwidth, dense, received, current, *pieces)


def apply_tile(tile, pieces, current, previous, center, halfwidth, grid_cols):
    height, _ = tile.shape
    orb = height // grid_cols
    vectors = current.shape[1]
    count = len(pieces)

    def kernel(center_ref, halfwidth_ref, tile_ref, current_ref, previous_ref, *refs):
        total = None
        at = 0
        for ref in refs[:count]:
            depth = ref.shape[0]
            part = jnp.dot(
                tile_ref[:, at : at + depth], ref[...], preferred_element_type=jnp.float32
            )
            total = part if total is None else total + part
            at += depth
        finish(total, False, orb, current_ref, previous_ref, center_ref, halfwidth_ref, refs[count:])

    return pl.pallas_call(
        kernel,
        in_specs=[SMEM] * 2 + [VMEM] * (3 + count),
        out_specs=[VMEM] * grid_cols,
        out_shape=[jax.ShapeDtypeStruct((orb, vectors), jnp.float32)] * grid_cols,
        compiler_params=pltpu.CompilerParams(vmem_limit_bytes=tile.size * 2 + 2 * SPARE),
        name="apply_tile",
    )(center, halfwidth, tile, current, previous, *pieces)


def body(hamiltonian_blocks, block_rows, block_cols, block_counts, initial, center, halfwidth):
    grid_rows = lax.axis_size("row")
    grid_cols = lax.axis_size("col")
    strides = stage_strides(grid_rows)

    def gather(panel):
        gathered = panel
        for index, (stride, radix) in enumerate(strides):
            parts = [gathered] + [
                swap(gathered, "row", grid_rows, k * stride) for k in range(1, radix)
            ]
            if index < len(strides) - 1:
                gathered = jnp.concatenate(parts, axis=0)
        return parts

    sources = jnp.array(arrival_order(strides), jnp.int32) ^ lax.axis_index("row")
    targets = jnp.arange(grid_cols, dtype=jnp.int32) ^ lax.axis_index("col")
    pieces = gather(initial.astype(jnp.bfloat16))
    dense = build_tile(
        block_rows[0, 0], block_cols[0, 0], block_counts[0], hamiltonian_blocks[0, 0],
        grid_rows, grid_cols,
    )
    received = lax.all_to_all(dense, ("row", "col"), 0, 0)
    tile, base, *others = merge_apply(
        sources, targets, dense, received, pieces, initial, center, halfwidth
    )

    previous = initial
    current = initial
    for degree_step in range(DEGREE):
        if degree_step > 0:
            pieces = gather(current.astype(jnp.bfloat16))
            base, *others = apply_tile(
                tile, pieces, current, previous, center, halfwidth, grid_cols
            )
        following = base
        for d, other in enumerate(others, start=1):
            following = following + swap(other, "col", grid_cols, d)
        previous = current
        current = following
    return current


def solution(mesh):
    in_specs = (
        P("row", "col", None, None, None),
        P("row", "col", None),
        P("row", "col", None),
        P("row", "col"),
        P(("row", "col"), None),
        P(),
        P(),
    )
    out_specs = P(("row", "col"), None)
    return jax.shard_map(body, mesh=mesh, in_specs=in_specs, out_specs=out_specs, check_vma=False)
```

```python
import jax
import jax.numpy as jnp
from jax import lax
from jax.experimental import pallas as pl
from jax.experimental.pallas import tpu as pltpu
from jax.sharding import PartitionSpec as P

DEGREE = 3
RADIX = 4
CHUNK = 8
SPARE = 4 * 2**20
BUILD_VMEM = 62 * 2**20
AFTER_VMEM = 60 * 2**20

VMEM = pl.BlockSpec(memory_space=pltpu.VMEM)
SMEM = pl.BlockSpec(memory_space=pltpu.SMEM)
HBM = pl.BlockSpec(memory_space=pltpu.HBM)


def stage_strides(size):
    found = []
    stride = 1
    while stride < size:
        radix = RADIX if size % (stride * RADIX) == 0 else size // stride
        found.append((stride, radix))
        stride *= radix
    return found[::-1]


def arrival_order(strides):
    order = [0]
    for stride, radix in strides:
        order = [k * stride ^ offset for k in range(radix) for offset in order]
    return order


def swap(x, axis, size, offset):
    return lax.ppermute(x, axis, [(source, source ^ offset) for source in range(size)])


def build_tile(rows, cols, count, stacked, grid_rows, grid_cols):
    slots, orb, _ = stacked.shape
    chunk = CHUNK if slots % CHUNK == 0 else slots
    chunks = slots // chunk
    cells = grid_rows * grid_cols

    def kernel(rows_ref, cols_ref, count_ref, stack_ref, dense_ref, held_ref, acc_ref, sems):
        copies = [
            pltpu.make_async_copy(
                stack_ref.at[pl.ds(n * chunk, chunk)], held_ref.at[pl.ds(n * chunk, chunk)], sems.at[n]
            )
            for n in range(chunks)
        ]
        for copy in copies:
            copy.start()
        count = count_ref[0]
        acc_ref[...] = jnp.zeros_like(acc_ref)
        for n, copy in enumerate(copies):
            copy.wait()
            for s in range(n * chunk, (n + 1) * chunk):
                cell = jnp.where(s < count, cols_ref[s] * grid_cols + rows_ref[s], cells)
                acc_ref[cell] += held_ref[s].astype(jnp.float32)

        def put(cell, carry):
            dense_ref[cell] = acc_ref[cell].astype(jnp.bfloat16)
            return carry

        lax.fori_loop(0, cells, put, 0, unroll=4 if cells % 4 == 0 else 1)

    return pl.pallas_call(
        kernel,
        grid_spec=pltpu.PrefetchScalarGridSpec(
            num_scalar_prefetch=3,
            grid=(1,),
            in_specs=[HBM],
            out_specs=VMEM,
            scratch_shapes=[
                pltpu.VMEM(stacked.shape, jnp.bfloat16),
                pltpu.VMEM((cells + 1, orb, orb), jnp.float32),
                pltpu.SemaphoreType.DMA((chunks,)),
            ],
        ),
        out_shape=jax.ShapeDtypeStruct((cells, orb, orb), jnp.bfloat16),
        compiler_params=pltpu.CompilerParams(vmem_limit_bytes=BUILD_VMEM),
        name="build_tile",
    )(rows, cols, count, stacked)


def after(x, others):
    token = sum(other[:16] for other in others)

    def kernel(*refs):
        pass

    return pl.pallas_call(
        kernel,
        in_specs=[HBM, HBM],
        out_specs=HBM,
        out_shape=jax.ShapeDtypeStruct(x.shape, x.dtype),
        input_output_aliases={0: 0},
        compiler_params=pltpu.CompilerParams(vmem_limit_bytes=AFTER_VMEM),
        name="after",
    )(x, token)


def finish(total, first, orb, current_ref, previous_ref, center_ref, halfwidth_ref, outs):
    scale = (1.0 if first else 2.0) / jnp.full((1, total.shape[1]), halfwidth_ref[0])
    own = (total[:orb] - center_ref[0] * current_ref[...]) * scale
    outs[0][...] = own if first else own - previous_ref[...]
    for d in range(1, len(outs)):
        outs[d][...] = total[d * orb : (d + 1) * orb] * scale


def merge_apply(sources, targets, dense, received, pieces, current, center, halfwidth):
    cells, orb, _ = dense.shape
    grid_rows = sources.shape[0]
    grid_cols = targets.shape[0]
    vectors = current.shape[1]
    count = len(pieces)

    def kernel(sources_ref, targets_ref, center_ref, halfwidth_ref, dense_ref, received_ref, current_ref, *refs):
        piece_refs = refs[:count]
        tile_ref, *outs = refs[count:]
        total = None
        at = 0
        for ref in piece_refs:
            depth = ref.shape[0]
            for k in range(at // orb, (at + depth) // orb):
                first = sources_ref[k] * grid_cols
                for d in range(grid_cols):
                    cell = first + targets_ref[d]
                    turned = received_ref[cell].T.astype(jnp.float32)
                    block = (dense_ref[cell].astype(jnp.float32) + turned).astype(jnp.bfloat16)
                    tile_ref[d * orb : (d + 1) * orb, k * orb : (k + 1) * orb] = block
            part = jnp.dot(
                tile_ref[:, at : at + depth], ref[...], preferred_element_type=jnp.float32
            )
            total = part if total is None else total + part
            at += depth
        finish(total, True, orb, current_ref, None, center_ref, halfwidth_ref, outs)

    block = jax.ShapeDtypeStruct((orb, vectors), jnp.float32)
    return pl.pallas_call(
        kernel,
        in_specs=[SMEM] * 4 + [VMEM] * (3 + count),
        out_specs=[VMEM] * (1 + grid_cols),
        out_shape=[jax.ShapeDtypeStruct((grid_cols * orb, grid_rows * orb), jnp.bfloat16)]
        + [block] * grid_cols,
        compiler_params=pltpu.CompilerParams(vmem_limit_bytes=dense.size * 6 + 2 * SPARE),
        name="merge_apply",
    )(sources, targets, center, halfwidth, dense, received, current, *pieces)


def apply_tile(tile, pieces, current, previous, center, halfwidth, grid_cols):
    height, _ = tile.shape
    orb = height // grid_cols
    vectors = current.shape[1]
    count = len(pieces)

    def kernel(center_ref, halfwidth_ref, tile_ref, current_ref, previous_ref, *refs):
        total = None
        at = 0
        for ref in refs[:count]:
            depth = ref.shape[0]
            part = jnp.dot(
                tile_ref[:, at : at + depth], ref[...], preferred_element_type=jnp.float32
            )
            total = part if total is None else total + part
            at += depth
        finish(total, False, orb, current_ref, previous_ref, center_ref, halfwidth_ref, refs[count:])

    return pl.pallas_call(
        kernel,
        in_specs=[SMEM] * 2 + [VMEM] * (3 + count),
        out_specs=[VMEM] * grid_cols,
        out_shape=[jax.ShapeDtypeStruct((orb, vectors), jnp.float32)] * grid_cols,
        compiler_params=pltpu.CompilerParams(vmem_limit_bytes=tile.size * 2 + 2 * SPARE),
        name="apply_tile",
    )(center, halfwidth, tile, current, previous, *pieces)


def body(hamiltonian_blocks, block_rows, block_cols, block_counts, initial, center, halfwidth):
    grid_rows = lax.axis_size("row")
    grid_cols = lax.axis_size("col")
    strides = stage_strides(grid_rows)

    def stage(gathered, stride, radix):
        return [gathered] + [swap(gathered, "row", grid_rows, k * stride) for k in range(1, radix)]

    def gather(parts, stages):
        for stride, radix in stages:
            parts = stage(jnp.concatenate(parts, axis=0), stride, radix)
        return parts

    sources = jnp.array(arrival_order(strides), jnp.int32) ^ lax.axis_index("row")
    targets = jnp.arange(grid_cols, dtype=jnp.int32) ^ lax.axis_index("col")
    pieces = gather([initial.astype(jnp.bfloat16)], strides[:1])
    dense = build_tile(
        block_rows[0, 0], block_cols[0, 0], block_counts[0], hamiltonian_blocks[0, 0],
        grid_rows, grid_cols,
    )
    dense = after(dense, pieces[1:])
    received = lax.all_to_all(dense, ("row", "col"), 0, 0)
    pieces = gather(pieces, strides[1:])
    tile, base, *others = merge_apply(
        sources, targets, dense, received, pieces, initial, center, halfwidth
    )

    previous = initial
    current = initial
    for degree_step in range(DEGREE):
        if degree_step > 0:
            pieces = gather([current.astype(jnp.bfloat16)], strides)
            base, *others = apply_tile(
                tile, pieces, current, previous, center, halfwidth, grid_cols
            )
        following = base
        for d, other in enumerate(others, start=1):
            following = following + swap(other, "col", grid_cols, d)
        previous = current
        current = following
    return current


def solution(mesh):
    in_specs = (
        P("row", "col", None, None, None),
        P("row", "col", None),
        P("row", "col", None),
        P("row", "col"),
        P(("row", "col"), None),
        P(),
        P(),
    )
    out_specs = P(("row", "col"), None)
    return jax.shard_map(body, mesh=mesh, in_specs=in_specs, out_specs=out_specs, check_vma=False)
```

```python
import jax
import jax.numpy as jnp
from jax import lax
from jax.experimental import pallas as pl
from jax.experimental.pallas import tpu as pltpu
from jax.sharding import PartitionSpec as P

DEGREE = 3
RADIX = 4
CHUNK = 8
SPARE = 4 * 2**20
BUILD_VMEM = 62 * 2**20
AFTER_VMEM = 60 * 2**20

VMEM = pl.BlockSpec(memory_space=pltpu.VMEM)
SMEM = pl.BlockSpec(memory_space=pltpu.SMEM)
HBM = pl.BlockSpec(memory_space=pltpu.HBM)


def stage_strides(size):
    found = []
    stride = 1
    while stride < size:
        radix = RADIX if size % (stride * RADIX) == 0 else size // stride
        found.append((stride, radix))
        stride *= radix
    return found[::-1]


def arrival_order(strides):
    order = [0]
    for stride, radix in strides:
        order = [k * stride + offset for k in range(radix) for offset in order]
    return order


def spread(x, axis, size, stride, radix):
    groups = [
        [first + k * stride for k in range(radix)]
        for first in range(size)
        if first // stride % radix == 0
    ]
    copies = jnp.broadcast_to(x[None], (radix, *x.shape))
    return lax.all_to_all(copies, axis, 0, 0, axis_index_groups=groups)


def swap(x, axis, size, offset):
    return lax.ppermute(x, axis, [(source, source ^ offset) for source in range(size)])


def build_tile(rows, cols, count, stacked, grid_rows, grid_cols):
    slots, orb, _ = stacked.shape
    chunk = CHUNK if slots % CHUNK == 0 else slots
    chunks = slots // chunk
    cells = grid_rows * grid_cols

    def kernel(rows_ref, cols_ref, count_ref, stack_ref, dense_ref, held_ref, acc_ref, sems):
        copies = [
            pltpu.make_async_copy(
                stack_ref.at[pl.ds(n * chunk, chunk)], held_ref.at[pl.ds(n * chunk, chunk)], sems.at[n]
            )
            for n in range(chunks)
        ]
        for copy in copies:
            copy.start()
        count = count_ref[0]
        acc_ref[...] = jnp.zeros_like(acc_ref)
        for n, copy in enumerate(copies):
            copy.wait()
            for s in range(n * chunk, (n + 1) * chunk):
                cell = jnp.where(s < count, cols_ref[s] * grid_cols + rows_ref[s], cells)
                acc_ref[cell] += held_ref[s].astype(jnp.float32)

        def put(cell, carry):
            dense_ref[cell] = acc_ref[cell].astype(jnp.bfloat16)
            return carry

        lax.fori_loop(0, cells, put, 0, unroll=4 if cells % 4 == 0 else 1)

    return pl.pallas_call(
        kernel,
        grid_spec=pltpu.PrefetchScalarGridSpec(
            num_scalar_prefetch=3,
            grid=(1,),
            in_specs=[HBM],
            out_specs=VMEM,
            scratch_shapes=[
                pltpu.VMEM(stacked.shape, jnp.bfloat16),
                pltpu.VMEM((cells + 1, orb, orb), jnp.float32),
                pltpu.SemaphoreType.DMA((chunks,)),
            ],
        ),
        out_shape=jax.ShapeDtypeStruct((cells, orb, orb), jnp.bfloat16),
        compiler_params=pltpu.CompilerParams(vmem_limit_bytes=BUILD_VMEM),
        name="build_tile",
    )(rows, cols, count, stacked)


def after(x, other):
    token = other[:16]

    def kernel(*refs):
        pass

    return pl.pallas_call(
        kernel,
        in_specs=[HBM, HBM],
        out_specs=HBM,
        out_shape=jax.ShapeDtypeStruct(x.shape, x.dtype),
        input_output_aliases={0: 0},
        compiler_params=pltpu.CompilerParams(vmem_limit_bytes=AFTER_VMEM),
        name="after",
    )(x, token)


def finish(total, first, orb, current_ref, previous_ref, center_ref, halfwidth_ref, outs):
    scale = (1.0 if first else 2.0) / jnp.full((1, total.shape[1]), halfwidth_ref[0])
    own = (total[:orb] - center_ref[0] * current_ref[...]) * scale
    outs[0][...] = own if first else own - previous_ref[...]
    for d in range(1, len(outs)):
        outs[d][...] = total[d * orb : (d + 1) * orb] * scale


def merge_apply(sources, targets, dense, received, panel, current, center, halfwidth):
    cells, orb, _ = dense.shape
    grid_rows = len(sources)
    grid_cols = targets.shape[0]
    vectors = current.shape[1]
    step = min(4, grid_rows)

    def kernel(targets_ref, center_ref, halfwidth_ref, dense_ref, received_ref, current_ref, panel_ref, tile_ref, *outs):
        total = None
        for start in range(0, grid_rows, step):
            for k in range(start, start + step):
                for d in range(grid_cols):
                    cell = sources[k] * grid_cols + targets_ref[d]
                    turned = received_ref[cell].T.astype(jnp.float32)
                    block = (dense_ref[cell].astype(jnp.float32) + turned).astype(jnp.bfloat16)
                    tile_ref[d * orb : (d + 1) * orb, k * orb : (k + 1) * orb] = block
            held = slice(start * orb, (start + step) * orb)
            part = jnp.dot(tile_ref[:, held], panel_ref[held], preferred_element_type=jnp.float32)
            total = part if total is None else total + part
        finish(total, True, orb, current_ref, None, center_ref, halfwidth_ref, outs)

    block = jax.ShapeDtypeStruct((orb, vectors), jnp.float32)
    return pl.pallas_call(
        kernel,
        in_specs=[SMEM] * 3 + [VMEM] * 4,
        out_specs=[VMEM] * (1 + grid_cols),
        out_shape=[jax.ShapeDtypeStruct((grid_cols * orb, grid_rows * orb), jnp.bfloat16)]
        + [block] * grid_cols,
        compiler_params=pltpu.CompilerParams(vmem_limit_bytes=dense.size * 6 + 2 * SPARE),
        name="merge_apply",
    )(targets, center, halfwidth, dense, received, current, panel)


def apply_tile(tile, panel, current, previous, center, halfwidth, grid_cols):
    height, _ = tile.shape
    orb = height // grid_cols
    vectors = current.shape[1]

    def kernel(center_ref, halfwidth_ref, tile_ref, current_ref, previous_ref, panel_ref, *outs):
        total = jnp.dot(tile_ref[...], panel_ref[...], preferred_element_type=jnp.float32)
        finish(total, False, orb, current_ref, previous_ref, center_ref, halfwidth_ref, outs)

    return pl.pallas_call(
        kernel,
        in_specs=[SMEM] * 2 + [VMEM] * 4,
        out_specs=[VMEM] * grid_cols,
        out_shape=[jax.ShapeDtypeStruct((orb, vectors), jnp.float32)] * grid_cols,
        compiler_params=pltpu.CompilerParams(vmem_limit_bytes=tile.size * 2 + 2 * SPARE),
        name="apply_tile",
    )(center, halfwidth, tile, current, previous, panel)


def body(hamiltonian_blocks, block_rows, block_cols, block_counts, initial, center, halfwidth):
    grid_rows = lax.axis_size("row")
    grid_cols = lax.axis_size("col")
    strides = stage_strides(grid_rows)

    def gather(panel, stages):
        for stride, radix in stages:
            spreaded = spread(panel, "row", grid_rows, stride, radix)
            panel = spreaded.reshape(-1, panel.shape[1])
        return panel

    sources = arrival_order(strides)
    targets = jnp.arange(grid_cols, dtype=jnp.int32) ^ lax.axis_index("col")
    panel = gather(initial.astype(jnp.bfloat16), strides[:1])
    dense = build_tile(
        block_rows[0, 0], block_cols[0, 0], block_counts[0], hamiltonian_blocks[0, 0],
        grid_rows, grid_cols,
    )
    dense = after(dense, panel)
    received = lax.all_to_all(dense, ("row", "col"), 0, 0)
    panel = gather(panel, strides[1:])
    tile, base, *others = merge_apply(
        sources, targets, dense, received, panel, initial, center, halfwidth
    )

    previous = initial
    current = initial
    for degree_step in range(DEGREE):
        if degree_step > 0:
            panel = gather(current.astype(jnp.bfloat16), strides)
            base, *others = apply_tile(
                tile, panel, current, previous, center, halfwidth, grid_cols
            )
        following = base
        for d, other in enumerate(others, start=1):
            following = following + swap(other, "col", grid_cols, d)
        previous = current
        current = following
    return current


def solution(mesh):
    in_specs = (
        P("row", "col", None, None, None),
        P("row", "col", None),
        P("row", "col", None),
        P("row", "col"),
        P(("row", "col"), None),
        P(),
        P(),
    )
    out_specs = P(("row", "col"), None)
    return jax.shard_map(body, mesh=mesh, in_specs=in_specs, out_specs=out_specs, check_vma=False)
```

```python
import jax
import jax.numpy as jnp
from jax import lax
from jax.experimental import pallas as pl
from jax.experimental.pallas import tpu as pltpu
from jax.sharding import PartitionSpec as P

DEGREE = 3
RADIX = 4
CHUNK = 8
SPARE = 4 * 2**20
BUILD_VMEM = 62 * 2**20
AFTER_VMEM = 60 * 2**20

VMEM = pl.BlockSpec(memory_space=pltpu.VMEM)
SMEM = pl.BlockSpec(memory_space=pltpu.SMEM)
HBM = pl.BlockSpec(memory_space=pltpu.HBM)


def stage_strides(size):
    found = []
    stride = 1
    while stride < size:
        radix = RADIX if size % (stride * RADIX) == 0 else size // stride
        found.append((stride, radix))
        stride *= radix
    return found[::-1]


def arrival_order(strides):
    order = [0]
    for stride, radix in strides:
        order = [k * stride ^ offset for k in range(radix) for offset in order]
    return order


def swap(x, axis, size, offset):
    return lax.ppermute(x, axis, [(source, source ^ offset) for source in range(size)])


def swap_rows(x, grid_rows, grid_cols, offsets):
    pairs = [
        (row * grid_cols + col, (row ^ offsets[col % 2]) * grid_cols + col)
        for row in range(grid_rows)
        for col in range(grid_cols)
    ]
    return lax.ppermute(x, ("row", "col"), pairs)


def build_tile(rows, cols, count, stacked, grid_rows, grid_cols):
    slots, orb, _ = stacked.shape
    chunk = CHUNK if slots % CHUNK == 0 else slots
    chunks = slots // chunk
    cells = grid_rows * grid_cols

    def kernel(rows_ref, cols_ref, count_ref, stack_ref, dense_ref, held_ref, acc_ref, sems):
        copies = [
            pltpu.make_async_copy(
                stack_ref.at[pl.ds(n * chunk, chunk)], held_ref.at[pl.ds(n * chunk, chunk)], sems.at[n]
            )
            for n in range(chunks)
        ]
        for copy in copies:
            copy.start()
        count = count_ref[0]
        acc_ref[...] = jnp.zeros_like(acc_ref)
        for n, copy in enumerate(copies):
            copy.wait()
            for s in range(n * chunk, (n + 1) * chunk):
                cell = jnp.where(s < count, cols_ref[s] * grid_cols + rows_ref[s], cells)
                acc_ref[cell] += held_ref[s].astype(jnp.float32)

        def put(cell, carry):
            dense_ref[cell] = acc_ref[cell].astype(jnp.bfloat16)
            return carry

        lax.fori_loop(0, cells, put, 0, unroll=4 if cells % 4 == 0 else 1)

    return pl.pallas_call(
        kernel,
        grid_spec=pltpu.PrefetchScalarGridSpec(
            num_scalar_prefetch=3,
            grid=(1,),
            in_specs=[HBM],
            out_specs=VMEM,
            scratch_shapes=[
                pltpu.VMEM(stacked.shape, jnp.bfloat16),
                pltpu.VMEM((cells + 1, orb, orb), jnp.float32),
                pltpu.SemaphoreType.DMA((chunks,)),
            ],
        ),
        out_shape=jax.ShapeDtypeStruct((cells, orb, orb), jnp.bfloat16),
        compiler_params=pltpu.CompilerParams(vmem_limit_bytes=BUILD_VMEM),
        name="build_tile",
    )(rows, cols, count, stacked)


def after(x, others):
    token = sum(other[:16] for other in others)

    def kernel(*refs):
        pass

    return pl.pallas_call(
        kernel,
        in_specs=[HBM, HBM],
        out_specs=HBM,
        out_shape=jax.ShapeDtypeStruct(x.shape, x.dtype),
        input_output_aliases={0: 0},
        compiler_params=pltpu.CompilerParams(vmem_limit_bytes=AFTER_VMEM),
        name="after",
    )(x, token)


def finish(total, first, orb, current_ref, previous_ref, center_ref, halfwidth_ref, outs):
    scale = (1.0 if first else 2.0) / jnp.full((1, total.shape[1]), halfwidth_ref[0])
    own = (total[:orb] - center_ref[0] * current_ref[...]) * scale
    outs[0][...] = own if first else own - previous_ref[...]
    for d in range(1, len(outs)):
        outs[d][...] = total[d * orb : (d + 1) * orb] * scale


def merge_apply(sources, places, targets, dense, received, panel, current, center, halfwidth):
    cells, orb, _ = dense.shape
    grid_rows = sources.shape[0]
    grid_cols = targets.shape[0]
    vectors = current.shape[1]

    def kernel(
        sources_ref, places_ref, targets_ref, center_ref, halfwidth_ref,
        dense_ref, received_ref, panel_ref, current_ref, tile_ref, *outs,
    ):
        total = None
        for k in range(grid_rows):
            held = slice(k * orb, (k + 1) * orb)
            first = sources_ref[k] * grid_cols
            for d in range(grid_cols):
                cell = first + targets_ref[d]
                turned = received_ref[cell].T.astype(jnp.float32)
                block = (dense_ref[cell].astype(jnp.float32) + turned).astype(jnp.bfloat16)
                tile_ref[d * orb : (d + 1) * orb, held] = block
            place = pl.ds(pl.multiple_of(places_ref[k] * orb, orb), orb)
            part = jnp.dot(
                tile_ref[:, held], panel_ref[place, :], preferred_element_type=jnp.float32
            )
            total = part if total is None else total + part
        finish(total, True, orb, current_ref, None, center_ref, halfwidth_ref, outs)

    block = jax.ShapeDtypeStruct((orb, vectors), jnp.float32)
    return pl.pallas_call(
        kernel,
        in_specs=[SMEM] * 5 + [VMEM] * 4,
        out_specs=[VMEM] * (1 + grid_cols),
        out_shape=[jax.ShapeDtypeStruct((grid_cols * orb, grid_rows * orb), jnp.bfloat16)]
        + [block] * grid_cols,
        compiler_params=pltpu.CompilerParams(vmem_limit_bytes=dense.size * 6 + 2 * SPARE),
        name="merge_apply",
    )(sources, places, targets, center, halfwidth, dense, received, panel, current)


def apply_tile(tile, pieces, current, previous, center, halfwidth, grid_cols):
    height, _ = tile.shape
    orb = height // grid_cols
    vectors = current.shape[1]
    count = len(pieces)

    def kernel(center_ref, halfwidth_ref, tile_ref, current_ref, previous_ref, *refs):
        total = None
        at = 0
        for ref in refs[:count]:
            depth = ref.shape[0]
            part = jnp.dot(
                tile_ref[:, at : at + depth], ref[...], preferred_element_type=jnp.float32
            )
            total = part if total is None else total + part
            at += depth
        finish(total, False, orb, current_ref, previous_ref, center_ref, halfwidth_ref, refs[count:])

    return pl.pallas_call(
        kernel,
        in_specs=[SMEM] * 2 + [VMEM] * (3 + count),
        out_specs=[VMEM] * grid_cols,
        out_shape=[jax.ShapeDtypeStruct((orb, vectors), jnp.float32)] * grid_cols,
        compiler_params=pltpu.CompilerParams(vmem_limit_bytes=tile.size * 2 + 2 * SPARE),
        name="apply_tile",
    )(center, halfwidth, tile, current, previous, *pieces)


def body(hamiltonian_blocks, block_rows, block_cols, block_counts, initial, center, halfwidth):
    grid_rows = lax.axis_size("row")
    grid_cols = lax.axis_size("col")
    strides = stage_strides(grid_rows)
    same = [strides, strides]
    turned = [strides, strides[::-1]]
    if [radix for _, radix in turned[0]] != [radix for _, radix in turned[1]]:
        turned = same

    def gather(parts, orders, first=0, last=None):
        for (stride, radix), (odd_stride, _) in list(zip(*orders))[first:last]:
            panel = jnp.concatenate(parts, axis=0)
            parts = [panel] + [
                swap_rows(panel, grid_rows, grid_cols, (k * stride, k * odd_stride))
                for k in range(1, radix)
            ]
        return parts

    row = lax.axis_index("row")
    col = lax.axis_index("col")
    early = arrival_order(strides)
    late = [arrival_order(order) for order in turned]
    places = [[early.index(offset) for offset in order] for order in late]
    sources = jnp.array(late, jnp.int32)[col % 2] ^ row
    places = jnp.array(places, jnp.int32)[col % 2]
    targets = jnp.arange(grid_cols, dtype=jnp.int32) ^ col
    pieces = gather([initial.astype(jnp.bfloat16)], same, last=1)
    dense = build_tile(
        block_rows[0, 0], block_cols[0, 0], block_counts[0], hamiltonian_blocks[0, 0],
        grid_rows, grid_cols,
    )
    dense = after(dense, pieces[1:])
    received = lax.all_to_all(dense, ("row", "col"), 0, 0)
    panel = jnp.concatenate(gather(pieces, same, first=1), axis=0)
    tile, base, *others = merge_apply(
        sources, places, targets, dense, received, panel, initial, center, halfwidth
    )

    previous = initial
    current = initial
    for degree_step in range(DEGREE):
        if degree_step > 0:
            pieces = gather([current.astype(jnp.bfloat16)], turned)
            base, *others = apply_tile(
                tile, pieces, current, previous, center, halfwidth, grid_cols
            )
        following = base
        for d, other in enumerate(others, start=1):
            following = following + swap(other, "col", grid_cols, d)
        previous = current
        current = following
    return current


def solution(mesh):
    in_specs = (
        P("row", "col", None, None, None),
        P("row", "col", None),
        P("row", "col", None),
        P("row", "col"),
        P(("row", "col"), None),
        P(),
        P(),
    )
    out_specs = P(("row", "col"), None)
    return jax.shard_map(body, mesh=mesh, in_specs=in_specs, out_specs=out_specs, check_vma=False)
```

```python
import jax
import jax.numpy as jnp
from jax import lax
from jax.experimental import pallas as pl
from jax.experimental.pallas import tpu as pltpu
from jax.sharding import PartitionSpec as P

DEGREE = 3
CHUNK = 8
SPARE = 4 * 2**20
BUILD_VMEM = 62 * 2**20
AFTER_VMEM = 60 * 2**20

VMEM = pl.BlockSpec(memory_space=pltpu.VMEM)
SMEM = pl.BlockSpec(memory_space=pltpu.SMEM)
HBM = pl.BlockSpec(memory_space=pltpu.HBM)


def stage_strides(bits, radices):
    found = []
    for radix in radices:
        width = radix.bit_length() - 1
        found.append((1 << min(bits[:width]), radix))
        bits = bits[width:]
    return found


def arrival_order(strides):
    order = [0]
    for stride, radix in strides:
        order = [k * stride ^ offset for k in range(radix) for offset in order]
    return order


def swap(x, axis, size, offset):
    return lax.ppermute(x, axis, [(source, source ^ offset) for source in range(size)])


def swap_rows(x, grid_rows, grid_cols, offsets):
    pairs = [
        (row * grid_cols + col, (row ^ offsets[col % 2]) * grid_cols + col)
        for row in range(grid_rows)
        for col in range(grid_cols)
    ]
    return lax.ppermute(x, ("row", "col"), pairs)


def build_tile(rows, cols, count, stacked, grid_rows, grid_cols):
    slots, orb, _ = stacked.shape
    chunk = CHUNK if slots % CHUNK == 0 else slots
    chunks = slots // chunk
    cells = grid_rows * grid_cols

    def kernel(rows_ref, cols_ref, count_ref, stack_ref, dense_ref, held_ref, acc_ref, sems):
        copies = [
            pltpu.make_async_copy(
                stack_ref.at[pl.ds(n * chunk, chunk)], held_ref.at[pl.ds(n * chunk, chunk)], sems.at[n]
            )
            for n in range(chunks)
        ]
        for copy in copies:
            copy.start()
        count = count_ref[0, 0]
        acc_ref[...] = jnp.zeros_like(acc_ref)
        for n, copy in enumerate(copies):
            copy.wait()
            for s in range(n * chunk, (n + 1) * chunk):
                cell = jnp.where(s < count, cols_ref[s] * grid_cols + rows_ref[s], cells)
                acc_ref[cell] += held_ref[s].astype(jnp.float32)

        def put(cell, carry):
            dense_ref[cell] = acc_ref[cell].astype(jnp.bfloat16)
            return carry

        lax.fori_loop(0, cells, put, 0, unroll=4 if cells % 4 == 0 else 1)

    return pl.pallas_call(
        kernel,
        grid_spec=pltpu.PrefetchScalarGridSpec(
            num_scalar_prefetch=3,
            grid=(1,),
            in_specs=[HBM],
            out_specs=VMEM,
            scratch_shapes=[
                pltpu.VMEM(stacked.shape, jnp.bfloat16),
                pltpu.VMEM((cells + 1, orb, orb), jnp.float32),
                pltpu.SemaphoreType.DMA((chunks,)),
            ],
        ),
        out_shape=jax.ShapeDtypeStruct((cells, orb, orb), jnp.bfloat16),
        compiler_params=pltpu.CompilerParams(vmem_limit_bytes=BUILD_VMEM),
        name="build_tile",
    )(rows, cols, count, stacked)


def after(x, others):
    token = sum(other[:16] for other in others)

    def kernel(*refs):
        pass

    return pl.pallas_call(
        kernel,
        in_specs=[HBM, HBM],
        out_specs=HBM,
        out_shape=jax.ShapeDtypeStruct(x.shape, x.dtype),
        input_output_aliases={0: 0},
        compiler_params=pltpu.CompilerParams(vmem_limit_bytes=AFTER_VMEM),
        name="after",
    )(x, token)


def finish(total, first, orb, current_ref, previous_ref, center_ref, halfwidth_ref, outs):
    scale = (1.0 if first else 2.0) / jnp.full((1, total.shape[1]), halfwidth_ref[0])
    own = (total[:orb] - center_ref[0] * current_ref[...]) * scale
    outs[0][...] = own if first else own - previous_ref[...]
    for d in range(1, len(outs)):
        outs[d][...] = total[d * orb : (d + 1) * orb] * scale


def merge_apply(sources, places, targets, dense, received, panel, current, center, halfwidth):
    cells, orb, _ = dense.shape
    grid_rows = sources.shape[0]
    grid_cols = targets.shape[0]
    vectors = current.shape[1]

    def kernel(
        sources_ref, places_ref, targets_ref, center_ref, halfwidth_ref,
        dense_ref, received_ref, panel_ref, current_ref, tile_ref, *outs,
    ):
        total = None
        for k in range(grid_rows):
            held = slice(k * orb, (k + 1) * orb)
            first = sources_ref[k] * grid_cols
            for d in range(grid_cols):
                cell = first + targets_ref[d]
                turned = received_ref[cell].T.astype(jnp.float32)
                block = (dense_ref[cell].astype(jnp.float32) + turned).astype(jnp.bfloat16)
                tile_ref[d * orb : (d + 1) * orb, held] = block
            place = pl.ds(pl.multiple_of(places_ref[k] * orb, orb), orb)
            part = jnp.dot(
                tile_ref[:, held], panel_ref[place, :], preferred_element_type=jnp.float32
            )
            total = part if total is None else total + part
        finish(total, True, orb, current_ref, None, center_ref, halfwidth_ref, outs)

    block = jax.ShapeDtypeStruct((orb, vectors), jnp.float32)
    return pl.pallas_call(
        kernel,
        in_specs=[SMEM] * 5 + [VMEM] * 4,
        out_specs=[VMEM] * (1 + grid_cols),
        out_shape=[jax.ShapeDtypeStruct((grid_cols * orb, grid_rows * orb), jnp.bfloat16)]
        + [block] * grid_cols,
        compiler_params=pltpu.CompilerParams(vmem_limit_bytes=dense.size * 6 + 2 * SPARE),
        name="merge_apply",
    )(sources, places, targets, center, halfwidth, dense, received, panel, current)


def apply_tile(tile, pieces, current, previous, center, halfwidth, grid_cols):
    height, _ = tile.shape
    orb = height // grid_cols
    vectors = current.shape[1]
    count = len(pieces)

    def kernel(center_ref, halfwidth_ref, tile_ref, current_ref, previous_ref, *refs):
        total = None
        at = 0
        for ref in refs[:count]:
            depth = ref.shape[0]
            part = jnp.dot(
                tile_ref[:, at : at + depth], ref[...], preferred_element_type=jnp.float32
            )
            total = part if total is None else total + part
            at += depth
        finish(total, False, orb, current_ref, previous_ref, center_ref, halfwidth_ref, refs[count:])

    return pl.pallas_call(
        kernel,
        in_specs=[SMEM] * 2 + [VMEM] * (3 + count),
        out_specs=[VMEM] * grid_cols,
        out_shape=[jax.ShapeDtypeStruct((orb, vectors), jnp.float32)] * grid_cols,
        compiler_params=pltpu.CompilerParams(vmem_limit_bytes=tile.size * 2 + 2 * SPARE),
        name="apply_tile",
    )(center, halfwidth, tile, current, previous, *pieces)


def body(hamiltonian_blocks, block_rows, block_cols, block_counts, initial, center, halfwidth):
    grid_rows = lax.axis_size("row")
    grid_cols = lax.axis_size("col")
    bits = list(range(grid_rows.bit_length() - 1))
    few = [2] * (len(bits) % 2) + [4] * (len(bits) // 2)
    many = [2] * (len(bits) - 2) + [4] * (len(bits) >= 2) + [2] * (len(bits) == 1)
    same = [stage_strides(bits[::-1], few)] * 2
    turned = [stage_strides(bits[::-1], many), stage_strides(bits, many)]

    def gather(parts, orders, first=0, last=None):
        for (stride, radix), (odd_stride, _) in list(zip(*orders))[first:last]:
            panel = jnp.concatenate(parts, axis=0)
            parts = [panel] + [
                swap_rows(panel, grid_rows, grid_cols, (k * stride, k * odd_stride))
                for k in range(1, radix)
            ]
        return parts

    row = lax.axis_index("row")
    col = lax.axis_index("col")
    early = arrival_order(same[0])
    late = [arrival_order(order) for order in turned]
    places = [[early.index(offset) for offset in order] for order in late]
    sources = jnp.array(late, jnp.int32)[col % 2] ^ row
    places = jnp.array(places, jnp.int32)[col % 2]
    targets = jnp.arange(grid_cols, dtype=jnp.int32) ^ col
    pieces = gather([initial.astype(jnp.bfloat16)], same, last=1)
    dense = build_tile(
        block_rows[0, 0], block_cols[0, 0], block_counts, hamiltonian_blocks[0, 0],
        grid_rows, grid_cols,
    )
    dense = after(dense, pieces[1:])
    received = lax.all_to_all(dense, ("row", "col"), 0, 0)
    panel = jnp.concatenate(gather(pieces, same, first=1), axis=0)
    tile, base, *others = merge_apply(
        sources, places, targets, dense, received, panel, initial, center, halfwidth
    )

    previous = initial
    current = initial
    for degree_step in range(DEGREE):
        if degree_step > 0:
            pieces = gather([current.astype(jnp.bfloat16)], turned)
            base, *others = apply_tile(
                tile, pieces, current, previous, center, halfwidth, grid_cols
            )
        following = base
        for d, other in enumerate(others, start=1):
            following = following + swap(other, "col", grid_cols, d)
        previous = current
        current = following
    return current


def solution(mesh):
    in_specs = (
        P("row", "col", None, None, None),
        P("row", "col", None),
        P("row", "col", None),
        P("row", "col"),
        P(("row", "col"), None),
        P(),
        P(),
    )
    out_specs = P(("row", "col"), None)
    return jax.shard_map(body, mesh=mesh, in_specs=in_specs, out_specs=out_specs, check_vma=False)
```

```python
import jax
import jax.numpy as jnp
from jax import lax
from jax.experimental import pallas as pl
from jax.experimental.pallas import tpu as pltpu
from jax.sharding import PartitionSpec as P

DEGREE = 3
RADIX = 4
CHUNK = 8
SPARE = 4 * 2**20
BUILD_VMEM = 62 * 2**20

VMEM = pl.BlockSpec(memory_space=pltpu.VMEM)
SMEM = pl.BlockSpec(memory_space=pltpu.SMEM)
HBM = pl.BlockSpec(memory_space=pltpu.HBM)


def stage_strides(size):
    found = []
    stride = 1
    while stride < size:
        radix = RADIX if size % (stride * RADIX) == 0 else size // stride
        found.append((stride, radix))
        stride *= radix
    return found[::-1]


def arrival_order(strides):
    order = [0]
    for stride, radix in strides:
        order = [k * stride ^ offset for k in range(radix) for offset in order]
    return order


def swap(x, axis, size, offset):
    return lax.ppermute(x, axis, [(source, source ^ offset) for source in range(size)])


def swap_rows(x, grid_rows, grid_cols, offsets):
    pairs = [
        (row * grid_cols + col, (row ^ offsets[col % 2]) * grid_cols + col)
        for row in range(grid_rows)
        for col in range(grid_cols)
    ]
    return lax.ppermute(x, ("row", "col"), pairs)


def build_tile(rows, cols, count, stacked, grid_rows, grid_cols):
    slots, orb, _ = stacked.shape
    chunk = CHUNK if slots % CHUNK == 0 else slots
    chunks = slots // chunk
    cells = grid_rows * grid_cols

    def kernel(
        rows_hbm, cols_hbm, count_ref, stack_ref, dense_ref,
        held_ref, acc_ref, rows_ref, cols_ref, sems, index_sems,
    ):
        indices = [
            pltpu.make_async_copy(source, target, index_sems.at[n])
            for n, (source, target) in enumerate([(rows_hbm, rows_ref), (cols_hbm, cols_ref)])
        ]
        for copy in indices:
            copy.start()
        copies = [
            pltpu.make_async_copy(
                stack_ref.at[pl.ds(n * chunk, chunk)], held_ref.at[pl.ds(n * chunk, chunk)], sems.at[n]
            )
            for n in range(chunks)
        ]
        for copy in copies:
            copy.start()
        acc_ref[...] = jnp.zeros_like(acc_ref)
        for copy in indices:
            copy.wait()
        count = count_ref[0, 0]
        for n, copy in enumerate(copies):
            copy.wait()
            for s in range(n * chunk, (n + 1) * chunk):
                cell = jnp.where(s < count, cols_ref[0, s] * grid_cols + rows_ref[0, s], cells)
                acc_ref[cell] += held_ref[s].astype(jnp.float32)

        def put(cell, carry):
            dense_ref[cell] = acc_ref[cell].astype(jnp.bfloat16)
            return carry

        lax.fori_loop(0, cells, put, 0, unroll=4 if cells % 4 == 0 else 1)

    return pl.pallas_call(
        kernel,
        in_specs=[HBM, HBM, SMEM, HBM],
        out_specs=VMEM,
        scratch_shapes=[
            pltpu.VMEM(stacked.shape, jnp.bfloat16),
            pltpu.VMEM((cells + 1, orb, orb), jnp.float32),
            pltpu.SMEM(rows.shape, jnp.int32),
            pltpu.SMEM(cols.shape, jnp.int32),
            pltpu.SemaphoreType.DMA((chunks,)),
            pltpu.SemaphoreType.DMA((2,)),
        ],
        out_shape=jax.ShapeDtypeStruct((cells, orb, orb), jnp.bfloat16),
        compiler_params=pltpu.CompilerParams(vmem_limit_bytes=BUILD_VMEM),
        name="build_tile",
    )(
        pltpu.with_memory_space_constraint(rows, pltpu.HBM),
        pltpu.with_memory_space_constraint(cols, pltpu.HBM),
        count,
        pltpu.with_memory_space_constraint(stacked, pltpu.HBM),
    )


def after(x, others):
    def kernel(*refs):
        pass

    return pl.pallas_call(
        kernel,
        in_specs=[HBM] + [VMEM] * len(others),
        out_specs=HBM,
        out_shape=pltpu.HBM(x.shape, x.dtype),
        input_output_aliases={0: 0},
        compiler_params=pltpu.CompilerParams(vmem_limit_bytes=SPARE),
        name="after",
    )(pltpu.with_memory_space_constraint(x, pltpu.HBM), *others)


def finish(total, first, orb, current_ref, previous_ref, center_ref, halfwidth_ref, outs):
    scale = (1.0 if first else 2.0) / jnp.full((1, total.shape[1]), halfwidth_ref[0])
    own = (total[:orb] - center_ref[0] * current_ref[...]) * scale
    outs[0][...] = own if first else own - previous_ref[...]
    for d in range(1, len(outs)):
        outs[d][...] = total[d * orb : (d + 1) * orb] * scale


def merge_apply(sources, places, targets, dense, received, panel, current, center, halfwidth):
    cells, orb, _ = dense.shape
    grid_rows = sources.shape[0]
    grid_cols = targets.shape[0]
    vectors = current.shape[1]

    def kernel(
        sources_ref, places_ref, targets_ref, center_ref, halfwidth_ref,
        dense_ref, received_ref, panel_ref, current_ref, tile_ref, *outs,
    ):
        total = None
        for k in range(grid_rows):
            held = slice(k * orb, (k + 1) * orb)
            first = sources_ref[k] * grid_cols
            for d in range(grid_cols):
                cell = first + targets_ref[d]
                turned = received_ref[cell].T.astype(jnp.float32)
                block = (dense_ref[cell].astype(jnp.float32) + turned).astype(jnp.bfloat16)
                tile_ref[d * orb : (d + 1) * orb, held] = block
            place = pl.ds(pl.multiple_of(places_ref[k] * orb, orb), orb)
            part = jnp.dot(
                tile_ref[:, held], panel_ref[place, :], preferred_element_type=jnp.float32
            )
            total = part if total is None else total + part
        finish(total, True, orb, current_ref, None, center_ref, halfwidth_ref, outs)

    block = jax.ShapeDtypeStruct((orb, vectors), jnp.float32)
    return pl.pallas_call(
        kernel,
        in_specs=[SMEM] * 5 + [VMEM] * 4,
        out_specs=[VMEM] * (1 + grid_cols),
        out_shape=[jax.ShapeDtypeStruct((grid_cols * orb, grid_rows * orb), jnp.bfloat16)]
        + [block] * grid_cols,
        compiler_params=pltpu.CompilerParams(vmem_limit_bytes=dense.size * 6 + 2 * SPARE),
        name="merge_apply",
    )(sources, places, targets, center, halfwidth, dense, received, panel, current)


def apply_tile(tile, pieces, current, previous, center, halfwidth, grid_cols):
    height, _ = tile.shape
    orb = height // grid_cols
    vectors = current.shape[1]
    count = len(pieces)

    def kernel(center_ref, halfwidth_ref, tile_ref, current_ref, previous_ref, *refs):
        total = None
        at = 0
        for ref in refs[:count]:
            depth = ref.shape[0]
            part = jnp.dot(
                tile_ref[:, at : at + depth], ref[...], preferred_element_type=jnp.float32
            )
            total = part if total is None else total + part
            at += depth
        finish(total, False, orb, current_ref, previous_ref, center_ref, halfwidth_ref, refs[count:])

    return pl.pallas_call(
        kernel,
        in_specs=[SMEM] * 2 + [VMEM] * (3 + count),
        out_specs=[VMEM] * grid_cols,
        out_shape=[jax.ShapeDtypeStruct((orb, vectors), jnp.float32)] * grid_cols,
        compiler_params=pltpu.CompilerParams(vmem_limit_bytes=tile.size * 2 + 2 * SPARE),
        name="apply_tile",
    )(center, halfwidth, tile, current, previous, *pieces)


def body(hamiltonian_blocks, block_rows, block_cols, block_counts, initial, center, halfwidth):
    grid_rows = lax.axis_size("row")
    grid_cols = lax.axis_size("col")
    strides = stage_strides(grid_rows)
    same = [strides, strides]
    turned = [strides, strides[::-1]]
    if [radix for _, radix in turned[0]] != [radix for _, radix in turned[1]]:
        turned = same

    def gather(parts, orders, first=0, last=None):
        for (stride, radix), (odd_stride, _) in list(zip(*orders))[first:last]:
            panel = jnp.concatenate(parts, axis=0)
            parts = [panel] + [
                swap_rows(panel, grid_rows, grid_cols, (k * stride, k * odd_stride))
                for k in range(1, radix)
            ]
        return parts

    row = lax.axis_index("row")
    col = lax.axis_index("col")
    early = arrival_order(strides)
    late = [arrival_order(order) for order in turned]
    places = [[early.index(offset) for offset in order] for order in late]
    sources = jnp.array(late, jnp.int32)[col % 2] ^ row
    places = jnp.array(places, jnp.int32)[col % 2]
    targets = jnp.arange(grid_cols, dtype=jnp.int32) ^ col
    pieces = gather([initial.astype(jnp.bfloat16)], same, last=1)
    dense = build_tile(
        block_rows[0], block_cols[0], block_counts, hamiltonian_blocks[0, 0],
        grid_rows, grid_cols,
    )
    dense = after(dense, pieces[1:])
    received = lax.all_to_all(dense, ("row", "col"), 0, 0)
    panel = jnp.concatenate(gather(pieces, same, first=1), axis=0)
    tile, base, *others = merge_apply(
        sources, places, targets, dense, received, panel, initial, center, halfwidth
    )

    previous = initial
    current = initial
    for degree_step in range(DEGREE):
        if degree_step > 0:
            pieces = gather([current.astype(jnp.bfloat16)], turned)
            base, *others = apply_tile(
                tile, pieces, current, previous, center, halfwidth, grid_cols
            )
        following = base
        for d, other in enumerate(others, start=1):
            following = following + swap(other, "col", grid_cols, d)
        previous = current
        current = following
    return current


def solution(mesh):
    in_specs = (
        P("row", "col", None, None, None),
        P("row", "col", None),
        P("row", "col", None),
        P("row", "col"),
        P(("row", "col"), None),
        P(),
        P(),
    )
    out_specs = P(("row", "col"), None)
    return jax.shard_map(body, mesh=mesh, in_specs=in_specs, out_specs=out_specs, check_vma=False)
```

```python
import jax
import jax.numpy as jnp
from jax import lax
from jax.experimental import pallas as pl
from jax.experimental.pallas import tpu as pltpu
from jax.sharding import PartitionSpec as P

DEGREE = 3
RADIX = 4
CHUNK = 8
SPARE = 4 * 2**20
BUILD_VMEM = 62 * 2**20

VMEM = pl.BlockSpec(memory_space=pltpu.VMEM)
SMEM = pl.BlockSpec(memory_space=pltpu.SMEM)
HBM = pl.BlockSpec(memory_space=pltpu.HBM)


def stage_strides(size):
    found = []
    stride = 1
    while stride < size:
        radix = RADIX if size % (stride * RADIX) == 0 else size // stride
        found.append((stride, radix))
        stride *= radix
    return found[::-1]


def arrival_order(strides):
    order = [0]
    for stride, radix in strides:
        order = [k * stride ^ offset for k in range(radix) for offset in order]
    return order


def swap(x, axis, size, offset):
    return lax.ppermute(x, axis, [(source, source ^ offset) for source in range(size)])


def swap_rows(x, grid_rows, grid_cols, offsets):
    pairs = [
        (row * grid_cols + col, (row ^ offsets[col % 2]) * grid_cols + col)
        for row in range(grid_rows)
        for col in range(grid_cols)
    ]
    return lax.ppermute(x, ("row", "col"), pairs)


def cell_of(col_slot, row_slot, grid_rows, grid_cols, low):
    return (col_slot % low * grid_cols + row_slot) * (grid_rows // low) + col_slot // low


def build_tile(rows, cols, count, stacked, grid_rows, grid_cols, low):
    slots, orb, _ = stacked.shape
    chunk = CHUNK if slots % CHUNK == 0 else slots
    chunks = slots // chunk
    cells = grid_rows * grid_cols

    def kernel(
        rows_hbm, cols_hbm, count_ref, stack_ref, dense_ref,
        held_ref, acc_ref, rows_ref, cols_ref, sems, index_sems,
    ):
        indices = [
            pltpu.make_async_copy(source, target, index_sems.at[n])
            for n, (source, target) in enumerate([(rows_hbm, rows_ref), (cols_hbm, cols_ref)])
        ]
        for copy in indices:
            copy.start()
        copies = [
            pltpu.make_async_copy(
                stack_ref.at[pl.ds(n * chunk, chunk)], held_ref.at[pl.ds(n * chunk, chunk)], sems.at[n]
            )
            for n in range(chunks)
        ]
        for copy in copies:
            copy.start()
        acc_ref[...] = jnp.zeros_like(acc_ref)
        for copy in indices:
            copy.wait()
        count = count_ref[0, 0]
        for n, copy in enumerate(copies):
            copy.wait()
            for s in range(n * chunk, (n + 1) * chunk):
                col_slot = cols_ref[0, s]
                fast = lax.shift_right_logical(col_slot, low.bit_length() - 1)
                slow = (col_slot & (low - 1)) * grid_cols + rows_ref[0, s]
                cell = jnp.where(s < count, slow * (grid_rows // low) + fast, cells)
                acc_ref[cell] += held_ref[s].astype(jnp.float32)

        def put(cell, carry):
            dense_ref[cell] = acc_ref[cell].astype(jnp.bfloat16)
            return carry

        lax.fori_loop(0, cells, put, 0, unroll=4 if cells % 4 == 0 else 1)

    return pl.pallas_call(
        kernel,
        in_specs=[HBM, HBM, SMEM, HBM],
        out_specs=VMEM,
        scratch_shapes=[
            pltpu.VMEM(stacked.shape, jnp.bfloat16),
            pltpu.VMEM((cells + 1, orb, orb), jnp.float32),
            pltpu.SMEM(rows.shape, jnp.int32),
            pltpu.SMEM(cols.shape, jnp.int32),
            pltpu.SemaphoreType.DMA((chunks,)),
            pltpu.SemaphoreType.DMA((2,)),
        ],
        out_shape=jax.ShapeDtypeStruct((cells, orb, orb), jnp.bfloat16),
        compiler_params=pltpu.CompilerParams(vmem_limit_bytes=BUILD_VMEM),
        name="build_tile",
    )(
        pltpu.with_memory_space_constraint(rows, pltpu.HBM),
        pltpu.with_memory_space_constraint(cols, pltpu.HBM),
        count,
        pltpu.with_memory_space_constraint(stacked, pltpu.HBM),
    )


def after(x, others):
    def kernel(*refs):
        pass

    return pl.pallas_call(
        kernel,
        in_specs=[HBM] + [VMEM] * len(others),
        out_specs=HBM,
        out_shape=pltpu.HBM(x.shape, x.dtype),
        input_output_aliases={0: 0},
        compiler_params=pltpu.CompilerParams(vmem_limit_bytes=SPARE),
        name="after",
    )(pltpu.with_memory_space_constraint(x, pltpu.HBM), *others)


def finish(total, first, orb, current_ref, previous_ref, center_ref, halfwidth_ref, outs):
    scale = (1.0 if first else 2.0) / jnp.full((1, total.shape[1]), halfwidth_ref[0])
    own = (total[:orb] - center_ref[0] * current_ref[...]) * scale
    outs[0][...] = own if first else own - previous_ref[...]
    for d in range(1, len(outs)):
        outs[d][...] = total[d * orb : (d + 1) * orb] * scale


def merge_apply(cells, places, dense, received, panel, current, center, halfwidth):
    _, orb, _ = dense.shape
    grid_rows = places.shape[0]
    grid_cols = cells.shape[0] // grid_rows
    vectors = current.shape[1]

    def kernel(
        cells_ref, places_ref, center_ref, halfwidth_ref,
        dense_ref, received_ref, panel_ref, current_ref, tile_ref, *outs,
    ):
        total = None
        for k in range(grid_rows):
            held = slice(k * orb, (k + 1) * orb)
            for d in range(grid_cols):
                cell = cells_ref[k * grid_cols + d]
                turned = received_ref[cell].T.astype(jnp.float32)
                block = (dense_ref[cell].astype(jnp.float32) + turned).astype(jnp.bfloat16)
                tile_ref[d * orb : (d + 1) * orb, held] = block
            place = pl.ds(pl.multiple_of(places_ref[k] * orb, orb), orb)
            part = jnp.dot(
                tile_ref[:, held], panel_ref[place, :], preferred_element_type=jnp.float32
            )
            total = part if total is None else total + part
        finish(total, True, orb, current_ref, None, center_ref, halfwidth_ref, outs)

    block = jax.ShapeDtypeStruct((orb, vectors), jnp.float32)
    return pl.pallas_call(
        kernel,
        in_specs=[SMEM] * 4 + [VMEM] * 4,
        out_specs=[VMEM] * (1 + grid_cols),
        out_shape=[jax.ShapeDtypeStruct((grid_cols * orb, grid_rows * orb), jnp.bfloat16)]
        + [block] * grid_cols,
        compiler_params=pltpu.CompilerParams(vmem_limit_bytes=dense.size * 6 + 2 * SPARE),
        name="merge_apply",
    )(cells, places, center, halfwidth, dense, received, panel, current)


def apply_tile(tile, pieces, current, previous, center, halfwidth, grid_cols):
    height, _ = tile.shape
    orb = height // grid_cols
    vectors = current.shape[1]
    count = len(pieces)

    def kernel(center_ref, halfwidth_ref, tile_ref, current_ref, previous_ref, *refs):
        total = None
        at = 0
        for ref in refs[:count]:
            depth = ref.shape[0]
            part = jnp.dot(
                tile_ref[:, at : at + depth], ref[...], preferred_element_type=jnp.float32
            )
            total = part if total is None else total + part
            at += depth
        finish(total, False, orb, current_ref, previous_ref, center_ref, halfwidth_ref, refs[count:])

    return pl.pallas_call(
        kernel,
        in_specs=[SMEM] * 2 + [VMEM] * (3 + count),
        out_specs=[VMEM] * grid_cols,
        out_shape=[jax.ShapeDtypeStruct((orb, vectors), jnp.float32)] * grid_cols,
        compiler_params=pltpu.CompilerParams(vmem_limit_bytes=tile.size * 2 + 2 * SPARE),
        name="apply_tile",
    )(center, halfwidth, tile, current, previous, *pieces)


def body(hamiltonian_blocks, block_rows, block_cols, block_counts, initial, center, halfwidth):
    grid_rows = lax.axis_size("row")
    grid_cols = lax.axis_size("col")
    strides = stage_strides(grid_rows)
    same = [strides, strides]
    turned = [strides, strides[::-1]]
    if [radix for _, radix in turned[0]] != [radix for _, radix in turned[1]]:
        turned = same

    def gather(parts, orders, first=0, last=None):
        for (stride, radix), (odd_stride, _) in list(zip(*orders))[first:last]:
            panel = jnp.concatenate(parts, axis=0)
            parts = [panel] + [
                swap_rows(panel, grid_rows, grid_cols, (k * stride, k * odd_stride))
                for k in range(1, radix)
            ]
        return parts

    row = lax.axis_index("row")
    col = lax.axis_index("col")
    early = arrival_order(strides)
    late = [arrival_order(order) for order in turned]
    places = [[early.index(offset) for offset in order] for order in late]
    sources = jnp.array(late, jnp.int32)[col % 2] ^ row
    places = jnp.array(places, jnp.int32)[col % 2]
    targets = jnp.arange(grid_cols, dtype=jnp.int32) ^ col
    low = same[0][0][0]
    cells = cell_of(sources[:, None], targets[None, :], grid_rows, grid_cols, low).reshape(-1)
    everyone = [0] * (grid_rows * grid_cols)
    for device in range(grid_rows * grid_cols):
        cell = cell_of(device // grid_cols, device % grid_cols, grid_rows, grid_cols, low)
        everyone[cell] = device
    pieces = gather([initial.astype(jnp.bfloat16)], same, last=1)
    dense = build_tile(
        block_rows[0], block_cols[0], block_counts, hamiltonian_blocks[0, 0],
        grid_rows, grid_cols, low,
    )
    dense = after(dense, pieces[1:])
    received = lax.all_to_all(dense, ("row", "col"), 0, 0, axis_index_groups=[everyone], tiled=True)
    panel = jnp.concatenate(gather(pieces, same, first=1), axis=0)
    tile, base, *others = merge_apply(
        cells, places, dense, received, panel, initial, center, halfwidth
    )

    previous = initial
    current = initial
    for degree_step in range(DEGREE):
        if degree_step > 0:
            pieces = gather([current.astype(jnp.bfloat16)], turned)
            base, *others = apply_tile(
                tile, pieces, current, previous, center, halfwidth, grid_cols
            )
        following = base
        for d, other in enumerate(others, start=1):
            following = following + swap(other, "col", grid_cols, d)
        previous = current
        current = following
    return current


def solution(mesh):
    in_specs = (
        P("row", "col", None, None, None),
        P("row", "col", None),
        P("row", "col", None),
        P("row", "col"),
        P(("row", "col"), None),
        P(),
        P(),
    )
    out_specs = P(("row", "col"), None)
    return jax.shard_map(body, mesh=mesh, in_specs=in_specs, out_specs=out_specs, check_vma=False)
```

```python
import jax
import jax.numpy as jnp
from jax import lax
from jax.experimental import pallas as pl
from jax.experimental.pallas import tpu as pltpu
from jax.sharding import PartitionSpec as P

DEGREE = 3
RADIX = 4
CHUNK = 8
SPARE = 4 * 2**20
BUILD_VMEM = 62 * 2**20

VMEM = pl.BlockSpec(memory_space=pltpu.VMEM)
SMEM = pl.BlockSpec(memory_space=pltpu.SMEM)
HBM = pl.BlockSpec(memory_space=pltpu.HBM)


def stage_strides(size):
    found = []
    stride = 1
    while stride < size:
        radix = RADIX if size % (stride * RADIX) == 0 else size // stride
        found.append((stride, radix))
        stride *= radix
    return found[::-1]


def arrival_order(strides):
    order = [0]
    for stride, radix in strides:
        order = [k * stride ^ offset for k in range(radix) for offset in order]
    return order


def swap(x, axis, size, offset):
    return lax.ppermute(x, axis, [(source, source ^ offset) for source in range(size)])


def swap_rows(x, grid_rows, grid_cols, offsets):
    pairs = [
        (row * grid_cols + col, (row ^ offsets[col % 2]) * grid_cols + col)
        for row in range(grid_rows)
        for col in range(grid_cols)
    ]
    return lax.ppermute(x, ("row", "col"), pairs)


def build_tile(rows, cols, count, stacked, grid_rows, grid_cols):
    slots, orb, _ = stacked.shape
    chunk = CHUNK if slots % CHUNK == 0 else slots
    chunks = slots // chunk
    cells = grid_rows * grid_cols

    def kernel(
        rows_hbm, cols_hbm, count_ref, stack_ref, dense_ref,
        held_ref, acc_ref, rows_ref, cols_ref, sems, index_sems,
    ):
        indices = [
            pltpu.make_async_copy(source, target, index_sems.at[n])
            for n, (source, target) in enumerate([(rows_hbm, rows_ref), (cols_hbm, cols_ref)])
        ]
        for copy in indices:
            copy.start()
        copies = [
            pltpu.make_async_copy(
                stack_ref.at[pl.ds(n * chunk, chunk)], held_ref.at[pl.ds(n * chunk, chunk)], sems.at[n]
            )
            for n in range(chunks)
        ]
        for copy in copies:
            copy.start()
        acc_ref[...] = jnp.zeros_like(acc_ref)
        for copy in indices:
            copy.wait()
        count = count_ref[0, 0]
        for n, copy in enumerate(copies):
            copy.wait()
            for s in range(n * chunk, (n + 1) * chunk):
                cell = jnp.where(s < count, cols_ref[0, s] * grid_cols + rows_ref[0, s], cells)
                acc_ref[cell] += held_ref[s].astype(jnp.float32)

        def put(cell, carry):
            dense_ref[cell] = acc_ref[cell].astype(jnp.bfloat16)
            return carry

        lax.fori_loop(0, cells, put, 0, unroll=4 if cells % 4 == 0 else 1)

    return pl.pallas_call(
        kernel,
        in_specs=[HBM, HBM, SMEM, HBM],
        out_specs=VMEM,
        scratch_shapes=[
            pltpu.VMEM(stacked.shape, jnp.bfloat16),
            pltpu.VMEM((cells + 1, orb, orb), jnp.float32),
            pltpu.SMEM(rows.shape, jnp.int32),
            pltpu.SMEM(cols.shape, jnp.int32),
            pltpu.SemaphoreType.DMA((chunks,)),
            pltpu.SemaphoreType.DMA((2,)),
        ],
        out_shape=jax.ShapeDtypeStruct((cells, orb, orb), jnp.bfloat16),
        compiler_params=pltpu.CompilerParams(vmem_limit_bytes=BUILD_VMEM),
        name="build_tile",
    )(
        pltpu.with_memory_space_constraint(rows, pltpu.HBM),
        pltpu.with_memory_space_constraint(cols, pltpu.HBM),
        count,
        pltpu.with_memory_space_constraint(stacked, pltpu.HBM),
    )


def after(x, others):
    def kernel(*refs):
        pass

    return pl.pallas_call(
        kernel,
        in_specs=[HBM] + [VMEM] * len(others),
        out_specs=HBM,
        out_shape=pltpu.HBM(x.shape, x.dtype),
        input_output_aliases={0: 0},
        compiler_params=pltpu.CompilerParams(vmem_limit_bytes=SPARE),
        name="after",
    )(pltpu.with_memory_space_constraint(x, pltpu.HBM), *others)


def finish(own, first, current_ref, previous_ref, center_ref, halfwidth_ref):
    scale = (1.0 if first else 2.0) / jnp.full((1, own.shape[1]), halfwidth_ref[0])
    own = (own - center_ref[0] * current_ref[...]) * scale
    return own if first else own - previous_ref[...], scale


def forward_first(sources, targets, dense, panel, current, center, halfwidth):
    cells, orb, _ = dense.shape
    grid_rows = sources.shape[0]
    grid_cols = targets.shape[0]
    vectors = current.shape[1]

    def kernel(
        sources_ref, targets_ref, center_ref, halfwidth_ref,
        dense_ref, panel_ref, current_ref, *refs,
    ):
        *outs, total_ref = refs
        total = None
        for k in range(grid_rows):
            blocks = dense_ref[pl.ds(sources_ref[k] * grid_cols, grid_cols)]
            part = jnp.dot(
                blocks.reshape(grid_cols * orb, orb), panel_ref[k * orb : (k + 1) * orb],
                preferred_element_type=jnp.float32,
            )
            total = part if total is None else total + part
        total_ref[...] = total.reshape(grid_cols, orb, vectors)
        base, scale = finish(
            total_ref[targets_ref[0]], True, current_ref, None, center_ref, halfwidth_ref
        )
        outs[0][...] = base
        for d in range(1, grid_cols):
            outs[d][...] = total_ref[targets_ref[d]] * scale

    return pl.pallas_call(
        kernel,
        in_specs=[SMEM] * 4 + [VMEM] * 3,
        out_specs=[VMEM] * grid_cols,
        out_shape=[jax.ShapeDtypeStruct((orb, vectors), jnp.float32)] * grid_cols,
        scratch_shapes=[pltpu.VMEM((grid_cols, orb, vectors), jnp.float32)],
        compiler_params=pltpu.CompilerParams(vmem_limit_bytes=dense.size * 2 + 2 * SPARE),
        name="forward_first",
    )(sources, targets, center, halfwidth, dense, panel, current)


def turn_panels(sources, targets, panels, orb):
    grid_rows = sources.shape[0]
    grid_cols = targets.shape[0]
    vectors = panels[0].shape[1]

    def kernel(sources_ref, targets_ref, *refs):
        *panel_refs, turned_ref = refs
        for d, panel_ref in enumerate(panel_refs):
            for k in range(grid_rows):
                at = (sources_ref[k] * grid_cols + targets_ref[d]) * orb
                turned = panel_ref[k * orb : (k + 1) * orb].T
                turned_ref[:, pl.ds(pl.multiple_of(at, orb), orb)] = turned

    return pl.pallas_call(
        kernel,
        in_specs=[SMEM] * 2 + [VMEM] * grid_cols,
        out_specs=VMEM,
        out_shape=jax.ShapeDtypeStruct((vectors, grid_rows * grid_cols * orb), jnp.bfloat16),
        compiler_params=pltpu.CompilerParams(vmem_limit_bytes=panels[0].size * 4 * grid_cols + SPARE),
        name="turn_panels",
    )(sources, targets, *panels)


def backward_first(turned_panels, received, base, halfwidth):
    cells, orb, _ = received.shape
    vectors = base.shape[1]

    def kernel(halfwidth_ref, turned_ref, received_ref, base_ref, out_ref, panel_ref):
        blocks = received_ref[...].reshape(cells * orb, orb)
        total = jnp.dot(turned_ref[...], blocks, preferred_element_type=jnp.float32)
        out = base_ref[...] + total.T / jnp.full((1, vectors), halfwidth_ref[0])
        out_ref[...] = out
        panel_ref[...] = out.astype(jnp.bfloat16)

    return pl.pallas_call(
        kernel,
        in_specs=[SMEM] + [VMEM] * 3,
        out_specs=[VMEM] * 2,
        out_shape=[
            jax.ShapeDtypeStruct((orb, vectors), jnp.float32),
            jax.ShapeDtypeStruct((orb, vectors), jnp.bfloat16),
        ],
        compiler_params=pltpu.CompilerParams(vmem_limit_bytes=received.size * 4 + 2 * SPARE),
        name="backward_first",
    )(halfwidth, turned_panels, received, base)


def turn_blocks(targets, received, panel, grid_rows):
    _, orb, _ = received.shape
    grid_cols = targets.shape[0]

    def kernel(targets_ref, received_ref, panel_ref, *outs):
        for d, out in enumerate(outs):
            for c in range(grid_rows):
                out[c] = received_ref[c * grid_cols + targets_ref[d]].T

    return pl.pallas_call(
        kernel,
        in_specs=[SMEM, VMEM, VMEM],
        out_specs=[VMEM] * grid_cols,
        out_shape=[jax.ShapeDtypeStruct((grid_rows, orb, orb), jnp.bfloat16)] * grid_cols,
        compiler_params=pltpu.CompilerParams(vmem_limit_bytes=received.size * 4 + SPARE),
        name="turn_blocks",
    )(targets, received, panel)


def merge_tile(sources, targets, dense, stacks):
    _, orb, _ = dense.shape
    grid_rows = sources.shape[0]
    grid_cols = targets.shape[0]

    def kernel(sources_ref, targets_ref, dense_ref, *refs):
        *stack_refs, tile_ref = refs
        for k in range(grid_rows):
            source = sources_ref[k]
            for d, stack_ref in enumerate(stack_refs):
                own = dense_ref[source * grid_cols + targets_ref[d]].astype(jnp.float32)
                block = (own + stack_ref[source].astype(jnp.float32)).astype(jnp.bfloat16)
                tile_ref[d * orb : (d + 1) * orb, k * orb : (k + 1) * orb] = block

    return pl.pallas_call(
        kernel,
        in_specs=[SMEM] * 2 + [VMEM] * (1 + grid_cols),
        out_specs=VMEM,
        out_shape=jax.ShapeDtypeStruct((grid_cols * orb, grid_rows * orb), jnp.bfloat16),
        compiler_params=pltpu.CompilerParams(vmem_limit_bytes=dense.size * 6 + SPARE),
        name="merge_tile",
    )(sources, targets, dense, *stacks)


def apply_tile(tile, pieces, current, previous, center, halfwidth, grid_cols):
    height, _ = tile.shape
    orb = height // grid_cols
    vectors = current.shape[1]
    count = len(pieces)

    def kernel(center_ref, halfwidth_ref, tile_ref, current_ref, previous_ref, *refs):
        outs = refs[count:]
        total = None
        at = 0
        for ref in refs[:count]:
            depth = ref.shape[0]
            part = jnp.dot(
                tile_ref[:, at : at + depth], ref[...], preferred_element_type=jnp.float32
            )
            total = part if total is None else total + part
            at += depth
        base, scale = finish(
            total[:orb], False, current_ref, previous_ref, center_ref, halfwidth_ref
        )
        outs[0][...] = base
        for d in range(1, grid_cols):
            outs[d][...] = total[d * orb : (d + 1) * orb] * scale

    return pl.pallas_call(
        kernel,
        in_specs=[SMEM] * 2 + [VMEM] * (3 + count),
        out_specs=[VMEM] * grid_cols,
        out_shape=[jax.ShapeDtypeStruct((orb, vectors), jnp.float32)] * grid_cols,
        compiler_params=pltpu.CompilerParams(vmem_limit_bytes=tile.size * 2 + 2 * SPARE),
        name="apply_tile",
    )(center, halfwidth, tile, current, previous, *pieces)


def body(hamiltonian_blocks, block_rows, block_cols, block_counts, initial, center, halfwidth):
    grid_rows = lax.axis_size("row")
    grid_cols = lax.axis_size("col")
    strides = stage_strides(grid_rows)
    same = [strides, strides]
    turned = [strides, strides[::-1]]
    if [radix for _, radix in turned[0]] != [radix for _, radix in turned[1]]:
        turned = same

    def gather(parts, orders, first=0, last=None):
        for (stride, radix), (odd_stride, _) in list(zip(*orders))[first:last]:
            panel = jnp.concatenate(parts, axis=0)
            parts = [panel] + [
                swap_rows(panel, grid_rows, grid_cols, (k * stride, k * odd_stride))
                for k in range(1, radix)
            ]
        return parts

    row = lax.axis_index("row")
    col = lax.axis_index("col")
    early = arrival_order(strides)
    late = [arrival_order(order) for order in turned]
    early_sources = jnp.array(early, jnp.int32) ^ row
    sources = jnp.array(late, jnp.int32)[col % 2] ^ row
    targets = jnp.arange(grid_cols, dtype=jnp.int32) ^ col
    pieces = gather([initial.astype(jnp.bfloat16)], same, last=1)
    dense = build_tile(
        block_rows[0], block_cols[0], block_counts, hamiltonian_blocks[0, 0],
        grid_rows, grid_cols,
    )
    dense = after(dense, pieces[1:])
    received = lax.all_to_all(dense, "row", 0, 0, tiled=True)
    panel = jnp.concatenate(gather(pieces, same, first=1), axis=0)
    panels = [panel] + [swap(panel, "col", grid_cols, d) for d in range(1, grid_cols)]
    base, *others = forward_first(
        early_sources, targets, dense, panel, initial, center, halfwidth
    )
    for d, other in enumerate(others, start=1):
        base = base + swap(other, "col", grid_cols, d)
    turned_panels = turn_panels(early_sources, targets, panels, dense.shape[1])

    previous = initial
    current, panel = backward_first(turned_panels, received, base, halfwidth)
    stacks = turn_blocks(targets, received, panel, grid_rows)
    stacks = [stacks[0]] + [swap(stacks[d], "col", grid_cols, d) for d in range(1, grid_cols)]
    tile = merge_tile(sources, targets, dense, stacks)
    for degree_step in range(1, DEGREE):
        pieces = gather([panel], turned)
        base, *others = apply_tile(tile, pieces, current, previous, center, halfwidth, grid_cols)
        following = base
        for d, other in enumerate(others, start=1):
            following = following + swap(other, "col", grid_cols, d)
        previous = current
        current = following
        panel = current.astype(jnp.bfloat16)
    return current


def solution(mesh):
    in_specs = (
        P("row", "col", None, None, None),
        P("row", "col", None),
        P("row", "col", None),
        P("row", "col"),
        P(("row", "col"), None),
        P(),
        P(),
    )
    out_specs = P(("row", "col"), None)
    return jax.shard_map(body, mesh=mesh, in_specs=in_specs, out_specs=out_specs, check_vma=False)
```

```python
import jax
import jax.numpy as jnp
from jax import lax
from jax.experimental import pallas as pl
from jax.experimental.pallas import tpu as pltpu
from jax.sharding import PartitionSpec as P

DEGREE = 3
RADIX = 4
CHUNK = 8
SPARE = 4 * 2**20
BUILD_VMEM = 62 * 2**20

VMEM = pl.BlockSpec(memory_space=pltpu.VMEM)
SMEM = pl.BlockSpec(memory_space=pltpu.SMEM)
HBM = pl.BlockSpec(memory_space=pltpu.HBM)


def stage_strides(size):
    found = []
    stride = 1
    while stride < size:
        radix = RADIX if size % (stride * RADIX) == 0 else size // stride
        found.append((stride, radix))
        stride *= radix
    return found[::-1]


def arrival_order(strides):
    order = [0]
    for stride, radix in strides:
        order = [k * stride ^ offset for k in range(radix) for offset in order]
    return order


def swap(x, axis, size, offset):
    return lax.ppermute(x, axis, [(source, source ^ offset) for source in range(size)])


def swap_rows(x, grid_rows, grid_cols, offsets):
    pairs = [
        (row * grid_cols + col, (row ^ offsets[col % 2]) * grid_cols + col)
        for row in range(grid_rows)
        for col in range(grid_cols)
    ]
    return lax.ppermute(x, ("row", "col"), pairs)


def build_tile(rows, cols, count, stacked, grid_rows, grid_cols):
    slots, orb, _ = stacked.shape
    chunk = CHUNK if slots % CHUNK == 0 else slots
    chunks = slots // chunk
    cells = grid_rows * grid_cols

    def kernel(
        rows_hbm, cols_hbm, count_ref, stack_ref, dense_ref,
        held_ref, acc_ref, rows_ref, cols_ref, sems, index_sems,
    ):
        indices = [
            pltpu.make_async_copy(source, target, index_sems.at[n])
            for n, (source, target) in enumerate([(rows_hbm, rows_ref), (cols_hbm, cols_ref)])
        ]
        for copy in indices:
            copy.start()
        copies = [
            pltpu.make_async_copy(
                stack_ref.at[pl.ds(n * chunk, chunk)], held_ref.at[pl.ds(n * chunk, chunk)], sems.at[n]
            )
            for n in range(chunks)
        ]
        for copy in copies:
            copy.start()
        acc_ref[...] = jnp.zeros_like(acc_ref)
        for copy in indices:
            copy.wait()
        count = count_ref[0, 0]
        for n, copy in enumerate(copies):
            copy.wait()
            for s in range(n * chunk, (n + 1) * chunk):
                cell = jnp.where(s < count, cols_ref[0, s] * grid_cols + rows_ref[0, s], cells)
                acc_ref[cell] += held_ref[s].astype(jnp.float32)

        def put(cell, carry):
            dense_ref[cell] = acc_ref[cell].astype(jnp.bfloat16)
            return carry

        lax.fori_loop(0, cells, put, 0, unroll=4 if cells % 4 == 0 else 1)

    return pl.pallas_call(
        kernel,
        in_specs=[HBM, HBM, SMEM, HBM],
        out_specs=VMEM,
        scratch_shapes=[
            pltpu.VMEM(stacked.shape, jnp.bfloat16),
            pltpu.VMEM((cells + 1, orb, orb), jnp.float32),
            pltpu.SMEM(rows.shape, jnp.int32),
            pltpu.SMEM(cols.shape, jnp.int32),
            pltpu.SemaphoreType.DMA((chunks,)),
            pltpu.SemaphoreType.DMA((2,)),
        ],
        out_shape=jax.ShapeDtypeStruct((cells, orb, orb), jnp.bfloat16),
        compiler_params=pltpu.CompilerParams(vmem_limit_bytes=BUILD_VMEM),
        name="build_tile",
    )(
        pltpu.with_memory_space_constraint(rows, pltpu.HBM),
        pltpu.with_memory_space_constraint(cols, pltpu.HBM),
        count,
        pltpu.with_memory_space_constraint(stacked, pltpu.HBM),
    )


def after(x, others):
    def kernel(*refs):
        pass

    return pl.pallas_call(
        kernel,
        in_specs=[HBM] + [VMEM] * len(others),
        out_specs=HBM,
        out_shape=pltpu.HBM(x.shape, x.dtype),
        input_output_aliases={0: 0},
        compiler_params=pltpu.CompilerParams(vmem_limit_bytes=SPARE),
        name="after",
    )(pltpu.with_memory_space_constraint(x, pltpu.HBM), *others)


def finish(own, first, current_ref, previous_ref, center_ref, halfwidth_ref):
    scale = (1.0 if first else 2.0) / jnp.full((1, own.shape[1]), halfwidth_ref[0])
    own = (own - center_ref[0] * current_ref[...]) * scale
    return own if first else own - previous_ref[...], scale


def forward_first(sources, targets, dense, panel, current, center, halfwidth):
    cells, orb, _ = dense.shape
    grid_rows = sources.shape[0]
    grid_cols = targets.shape[0]
    vectors = current.shape[1]

    def kernel(
        sources_ref, targets_ref, center_ref, halfwidth_ref,
        dense_ref, panel_ref, current_ref, *refs,
    ):
        *outs, total_ref = refs
        total = None
        for k in range(grid_rows):
            blocks = dense_ref[pl.ds(sources_ref[k] * grid_cols, grid_cols)]
            part = jnp.dot(
                blocks.reshape(grid_cols * orb, orb), panel_ref[k * orb : (k + 1) * orb],
                preferred_element_type=jnp.float32,
            )
            total = part if total is None else total + part
        total_ref[...] = total.reshape(grid_cols, orb, vectors)
        base, scale = finish(
            total_ref[targets_ref[0]], True, current_ref, None, center_ref, halfwidth_ref
        )
        outs[0][...] = base
        for d in range(1, grid_cols):
            outs[d][...] = total_ref[targets_ref[d]] * scale

    return pl.pallas_call(
        kernel,
        in_specs=[SMEM] * 4 + [VMEM] * 3,
        out_specs=[VMEM] * grid_cols,
        out_shape=[jax.ShapeDtypeStruct((orb, vectors), jnp.float32)] * grid_cols,
        scratch_shapes=[pltpu.VMEM((grid_cols, orb, vectors), jnp.float32)],
        compiler_params=pltpu.CompilerParams(vmem_limit_bytes=dense.size * 2 + 2 * SPARE),
        name="forward_first",
    )(sources, targets, center, halfwidth, dense, panel, current)


def turn_panel(sources, panel, orb):
    grid_rows = sources.shape[0]
    vectors = panel.shape[1]

    def kernel(sources_ref, panel_ref, turned_ref):
        for k in range(grid_rows):
            turned = panel_ref[k * orb : (k + 1) * orb].T
            turned_ref[:, pl.ds(pl.multiple_of(sources_ref[k] * orb, orb), orb)] = turned

    return pl.pallas_call(
        kernel,
        in_specs=[SMEM, VMEM],
        out_specs=VMEM,
        out_shape=jax.ShapeDtypeStruct((vectors, grid_rows * orb), jnp.bfloat16),
        compiler_params=pltpu.CompilerParams(vmem_limit_bytes=panel.size * 4 + SPARE),
        name="turn_panel",
    )(sources, panel)


def backward_first(targets, turned_panels, received, base, halfwidth):
    cells, orb, _ = received.shape
    grid_cols = targets.shape[0]
    vectors = base.shape[1]

    def kernel(targets_ref, halfwidth_ref, received_ref, base_ref, *refs):
        turned_refs = refs[:grid_cols]
        out_ref, panel_ref = refs[grid_cols:]
        total = None
        for d, turned_ref in enumerate(turned_refs):
            blocks = jnp.concatenate(
                [received_ref[c + targets_ref[d]] for c in range(0, cells, grid_cols)], axis=0
            )
            part = jnp.dot(turned_ref[...], blocks, preferred_element_type=jnp.float32)
            total = part if total is None else total + part
        out = base_ref[...] + total.T / jnp.full((1, vectors), halfwidth_ref[0])
        out_ref[...] = out
        panel_ref[...] = out.astype(jnp.bfloat16)

    return pl.pallas_call(
        kernel,
        in_specs=[SMEM] * 2 + [VMEM] * (2 + grid_cols),
        out_specs=[VMEM] * 2,
        out_shape=[
            jax.ShapeDtypeStruct((orb, vectors), jnp.float32),
            jax.ShapeDtypeStruct((orb, vectors), jnp.bfloat16),
        ],
        compiler_params=pltpu.CompilerParams(vmem_limit_bytes=received.size * 4 + 2 * SPARE),
        name="backward_first",
    )(targets, halfwidth, received, base, *turned_panels)


def pick_blocks(targets, received, panel, grid_rows):
    _, orb, _ = received.shape
    grid_cols = targets.shape[0]

    def kernel(targets_ref, received_ref, panel_ref, *outs):
        for d, out in enumerate(outs, start=1):
            for c in range(grid_rows):
                out[c] = received_ref[c * grid_cols + targets_ref[d]]

    return pl.pallas_call(
        kernel,
        in_specs=[SMEM, VMEM, VMEM],
        out_specs=[VMEM] * (grid_cols - 1),
        out_shape=[jax.ShapeDtypeStruct((grid_rows, orb, orb), jnp.bfloat16)] * (grid_cols - 1),
        compiler_params=pltpu.CompilerParams(vmem_limit_bytes=received.size * 4 + SPARE),
        name="pick_blocks",
    )(targets, received, panel)


def merge_tile(sources, targets, dense, received, stacks):
    _, orb, _ = dense.shape
    grid_rows = sources.shape[0]
    grid_cols = targets.shape[0]

    def kernel(sources_ref, targets_ref, dense_ref, received_ref, *refs):
        *stack_refs, tile_ref = refs
        for k in range(grid_rows):
            source = sources_ref[k]
            for d in range(grid_cols):
                cell = source * grid_cols + targets_ref[d]
                turned = received_ref[cell] if d == 0 else stack_refs[d - 1][source]
                own = dense_ref[cell].astype(jnp.float32)
                block = (own + turned.T.astype(jnp.float32)).astype(jnp.bfloat16)
                tile_ref[d * orb : (d + 1) * orb, k * orb : (k + 1) * orb] = block

    return pl.pallas_call(
        kernel,
        in_specs=[SMEM] * 2 + [VMEM] * (1 + grid_cols),
        out_specs=VMEM,
        out_shape=jax.ShapeDtypeStruct((grid_cols * orb, grid_rows * orb), jnp.bfloat16),
        compiler_params=pltpu.CompilerParams(vmem_limit_bytes=dense.size * 8 + SPARE),
        name="merge_tile",
    )(sources, targets, dense, received, *stacks)


def apply_tile(tile, pieces, current, previous, center, halfwidth, grid_cols):
    height, _ = tile.shape
    orb = height // grid_cols
    vectors = current.shape[1]
    count = len(pieces)

    def kernel(center_ref, halfwidth_ref, tile_ref, current_ref, previous_ref, *refs):
        outs = refs[count:]
        total = None
        at = 0
        for ref in refs[:count]:
            depth = ref.shape[0]
            part = jnp.dot(
                tile_ref[:, at : at + depth], ref[...], preferred_element_type=jnp.float32
            )
            total = part if total is None else total + part
            at += depth
        base, scale = finish(
            total[:orb], False, current_ref, previous_ref, center_ref, halfwidth_ref
        )
        outs[0][...] = base
        for d in range(1, grid_cols):
            outs[d][...] = total[d * orb : (d + 1) * orb] * scale

    return pl.pallas_call(
        kernel,
        in_specs=[SMEM] * 2 + [VMEM] * (3 + count),
        out_specs=[VMEM] * grid_cols,
        out_shape=[jax.ShapeDtypeStruct((orb, vectors), jnp.float32)] * grid_cols,
        compiler_params=pltpu.CompilerParams(vmem_limit_bytes=tile.size * 2 + 2 * SPARE),
        name="apply_tile",
    )(center, halfwidth, tile, current, previous, *pieces)


def body(hamiltonian_blocks, block_rows, block_cols, block_counts, initial, center, halfwidth):
    grid_rows = lax.axis_size("row")
    grid_cols = lax.axis_size("col")
    strides = stage_strides(grid_rows)
    same = [strides, strides]
    turned = [strides, strides[::-1]]
    if [radix for _, radix in turned[0]] != [radix for _, radix in turned[1]]:
        turned = same

    def gather(parts, orders, first=0, last=None):
        for (stride, radix), (odd_stride, _) in list(zip(*orders))[first:last]:
            panel = jnp.concatenate(parts, axis=0)
            parts = [panel] + [
                swap_rows(panel, grid_rows, grid_cols, (k * stride, k * odd_stride))
                for k in range(1, radix)
            ]
        return parts

    row = lax.axis_index("row")
    col = lax.axis_index("col")
    early = arrival_order(strides)
    late = [arrival_order(order) for order in turned]
    early_sources = jnp.array(early, jnp.int32) ^ row
    sources = jnp.array(late, jnp.int32)[col % 2] ^ row
    targets = jnp.arange(grid_cols, dtype=jnp.int32) ^ col
    pieces = gather([initial.astype(jnp.bfloat16)], same, last=1)
    dense = build_tile(
        block_rows[0], block_cols[0], block_counts, hamiltonian_blocks[0, 0],
        grid_rows, grid_cols,
    )
    dense = after(dense, pieces[1:])
    received = lax.all_to_all(dense, "row", 0, 0, tiled=True)
    panel = jnp.concatenate(gather(pieces, same, first=1), axis=0)
    turned_panel = turn_panel(early_sources, panel, dense.shape[1])
    turned_panels = [turned_panel] + [
        swap(turned_panel, "col", grid_cols, d) for d in range(1, grid_cols)
    ]
    base, *others = forward_first(
        early_sources, targets, dense, panel, initial, center, halfwidth
    )
    for d, other in enumerate(others, start=1):
        base = base + swap(other, "col", grid_cols, d)

    previous = initial
    current, panel = backward_first(targets, turned_panels, received, base, halfwidth)
    stacks = []
    if grid_cols > 1:
        stacks = pick_blocks(targets, received, panel, grid_rows)
    stacks = [swap(stack, "col", grid_cols, d) for d, stack in enumerate(stacks, start=1)]
    tile = merge_tile(sources, targets, dense, received, stacks)
    for degree_step in range(1, DEGREE):
        pieces = gather([panel], turned)
        base, *others = apply_tile(tile, pieces, current, previous, center, halfwidth, grid_cols)
        following = base
        for d, other in enumerate(others, start=1):
            following = following + swap(other, "col", grid_cols, d)
        previous = current
        current = following
        panel = current.astype(jnp.bfloat16)
    return current


def solution(mesh):
    in_specs = (
        P("row", "col", None, None, None),
        P("row", "col", None),
        P("row", "col", None),
        P("row", "col"),
        P(("row", "col"), None),
        P(),
        P(),
    )
    out_specs = P(("row", "col"), None)
    return jax.shard_map(body, mesh=mesh, in_specs=in_specs, out_specs=out_specs, check_vma=False)
```

```python
import jax
import jax.numpy as jnp
from jax import lax
from jax.experimental import pallas as pl
from jax.experimental.pallas import tpu as pltpu
from jax.sharding import PartitionSpec as P

DEGREE = 3
RADIX = 4
CHUNK = 8
SPARE = 4 * 2**20
BUILD_VMEM = 62 * 2**20

VMEM = pl.BlockSpec(memory_space=pltpu.VMEM)
SMEM = pl.BlockSpec(memory_space=pltpu.SMEM)
HBM = pl.BlockSpec(memory_space=pltpu.HBM)


def stage_strides(size):
    found = []
    stride = 1
    while stride < size:
        radix = RADIX if size % (stride * RADIX) == 0 else size // stride
        found.append((stride, radix))
        stride *= radix
    return found[::-1]


def arrival_order(strides):
    order = [0]
    for stride, radix in strides:
        order = [k * stride ^ offset for k in range(radix) for offset in order]
    return order


def swap(x, axis, size, offset):
    return lax.ppermute(x, axis, [(source, source ^ offset) for source in range(size)])


def swap_rows(x, grid_rows, grid_cols, offsets):
    pairs = [
        (row * grid_cols + col, (row ^ offsets[col % 2]) * grid_cols + col)
        for row in range(grid_rows)
        for col in range(grid_cols)
    ]
    return lax.ppermute(x, ("row", "col"), pairs)


def build_tile(rows, cols, count, stacked, grid_rows, grid_cols):
    slots, orb, _ = stacked.shape
    chunk = CHUNK if slots % CHUNK == 0 else slots
    chunks = slots // chunk
    cells = grid_rows * grid_cols

    def kernel(
        rows_hbm, cols_hbm, count_ref, stack_ref, dense_ref,
        held_ref, acc_ref, rows_ref, cols_ref, sems, index_sems,
    ):
        indices = [
            pltpu.make_async_copy(source, target, index_sems.at[n])
            for n, (source, target) in enumerate([(rows_hbm, rows_ref), (cols_hbm, cols_ref)])
        ]
        for copy in indices:
            copy.start()
        copies = [
            pltpu.make_async_copy(
                stack_ref.at[pl.ds(n * chunk, chunk)], held_ref.at[pl.ds(n * chunk, chunk)], sems.at[n]
            )
            for n in range(chunks)
        ]
        for copy in copies:
            copy.start()
        acc_ref[...] = jnp.zeros_like(acc_ref)
        for copy in indices:
            copy.wait()
        count = count_ref[0, 0]
        for n, copy in enumerate(copies):
            copy.wait()
            for s in range(n * chunk, (n + 1) * chunk):
                cell = jnp.where(s < count, cols_ref[0, s] * grid_cols + rows_ref[0, s], cells)
                acc_ref[cell] += held_ref[s].astype(jnp.float32)

        def put(cell, carry):
            dense_ref[cell] = acc_ref[cell].astype(jnp.bfloat16)
            return carry

        lax.fori_loop(0, cells, put, 0, unroll=4 if cells % 4 == 0 else 1)

    return pl.pallas_call(
        kernel,
        in_specs=[HBM, HBM, SMEM, HBM],
        out_specs=VMEM,
        scratch_shapes=[
            pltpu.VMEM(stacked.shape, jnp.bfloat16),
            pltpu.VMEM((cells + 1, orb, orb), jnp.float32),
            pltpu.SMEM(rows.shape, jnp.int32),
            pltpu.SMEM(cols.shape, jnp.int32),
            pltpu.SemaphoreType.DMA((chunks,)),
            pltpu.SemaphoreType.DMA((2,)),
        ],
        out_shape=jax.ShapeDtypeStruct((cells, orb, orb), jnp.bfloat16),
        compiler_params=pltpu.CompilerParams(vmem_limit_bytes=BUILD_VMEM),
        name="build_tile",
    )(
        pltpu.with_memory_space_constraint(rows, pltpu.HBM),
        pltpu.with_memory_space_constraint(cols, pltpu.HBM),
        count,
        pltpu.with_memory_space_constraint(stacked, pltpu.HBM),
    )


def after(x, others):
    def kernel(*refs):
        pass

    return pl.pallas_call(
        kernel,
        in_specs=[HBM] + [VMEM] * len(others),
        out_specs=HBM,
        out_shape=pltpu.HBM(x.shape, x.dtype),
        input_output_aliases={0: 0},
        compiler_params=pltpu.CompilerParams(vmem_limit_bytes=SPARE),
        name="after",
    )(pltpu.with_memory_space_constraint(x, pltpu.HBM), *others)


def finish(own, first, current_ref, previous_ref, center_ref, halfwidth_ref):
    scale = (1.0 if first else 2.0) / jnp.full((1, own.shape[1]), halfwidth_ref[0])
    own = (own - center_ref[0] * current_ref[...]) * scale
    return own if first else own - previous_ref[...], scale


def forward_first(sources, targets, dense, panel, current, center, halfwidth):
    cells, orb, _ = dense.shape
    grid_rows = sources.shape[0]
    grid_cols = targets.shape[0]
    vectors = current.shape[1]

    def kernel(
        sources_ref, targets_ref, center_ref, halfwidth_ref,
        dense_hbm, panel_ref, current_ref, *refs,
    ):
        *outs, total_ref, dense_ref, sem = refs
        copy = pltpu.make_async_copy(dense_hbm, dense_ref, sem)
        copy.start()
        copy.wait()
        total = None
        for k in range(grid_rows):
            blocks = dense_ref[pl.ds(sources_ref[k] * grid_cols, grid_cols)]
            part = jnp.dot(
                blocks.reshape(grid_cols * orb, orb), panel_ref[k * orb : (k + 1) * orb],
                preferred_element_type=jnp.float32,
            )
            total = part if total is None else total + part
        total_ref[...] = total.reshape(grid_cols, orb, vectors)
        base, scale = finish(
            total_ref[targets_ref[0]], True, current_ref, None, center_ref, halfwidth_ref
        )
        outs[0][...] = base
        for d in range(1, grid_cols):
            outs[d][...] = total_ref[targets_ref[d]] * scale

    return pl.pallas_call(
        kernel,
        in_specs=[SMEM] * 4 + [HBM] + [VMEM] * 2,
        out_specs=[VMEM] * grid_cols,
        out_shape=[jax.ShapeDtypeStruct((orb, vectors), jnp.float32)] * grid_cols,
        scratch_shapes=[
            pltpu.VMEM((grid_cols, orb, vectors), jnp.float32),
            pltpu.VMEM(dense.shape, dense.dtype),
            pltpu.SemaphoreType.DMA,
        ],
        compiler_params=pltpu.CompilerParams(vmem_limit_bytes=dense.size * 2 + 2 * SPARE),
        name="forward_first",
    )(
        sources, targets, center, halfwidth,
        pltpu.with_memory_space_constraint(dense, pltpu.HBM), panel, current,
    )


def turn_panel(sources, panel, orb):
    grid_rows = sources.shape[0]
    vectors = panel.shape[1]

    def kernel(sources_ref, panel_ref, turned_ref):
        for k in range(grid_rows):
            turned = panel_ref[k * orb : (k + 1) * orb].T
            turned_ref[:, pl.ds(pl.multiple_of(sources_ref[k] * orb, orb), orb)] = turned

    return pl.pallas_call(
        kernel,
        in_specs=[SMEM, VMEM],
        out_specs=VMEM,
        out_shape=jax.ShapeDtypeStruct((vectors, grid_rows * orb), jnp.bfloat16),
        compiler_params=pltpu.CompilerParams(vmem_limit_bytes=panel.size * 4 + SPARE),
        name="turn_panel",
    )(sources, panel)


def lay_panels(targets, turned_panels, grid_rows):
    grid_cols = targets.shape[0]
    vectors, width = turned_panels[0].shape
    orb = width // grid_rows

    def kernel(targets_ref, *refs):
        *turned_refs, out_ref = refs
        for d, turned_ref in enumerate(turned_refs):
            for c in range(grid_rows):
                at = pl.multiple_of((c * grid_cols + targets_ref[d]) * orb, orb)
                out_ref[:, pl.ds(at, orb)] = turned_ref[:, c * orb : (c + 1) * orb]

    return pl.pallas_call(
        kernel,
        in_specs=[SMEM] + [VMEM] * grid_cols,
        out_specs=VMEM,
        out_shape=jax.ShapeDtypeStruct((vectors, grid_cols * width), jnp.bfloat16),
        compiler_params=pltpu.CompilerParams(vmem_limit_bytes=vectors * width * 4 * grid_cols + SPARE),
        name="lay_panels",
    )(targets, *turned_panels)


def backward_first(turned_panels, received, base, halfwidth):
    cells, orb, _ = received.shape
    vectors = base.shape[1]

    def kernel(halfwidth_ref, turned_ref, received_ref, base_ref, out_ref, panel_ref):
        blocks = received_ref[...].reshape(cells * orb, orb)
        total = jnp.dot(turned_ref[...], blocks, preferred_element_type=jnp.float32)
        out = base_ref[...] + total.T / jnp.full((1, vectors), halfwidth_ref[0])
        out_ref[...] = out
        panel_ref[...] = out.astype(jnp.bfloat16)

    return pl.pallas_call(
        kernel,
        in_specs=[SMEM] + [VMEM] * 3,
        out_specs=[VMEM] * 2,
        out_shape=[
            jax.ShapeDtypeStruct((orb, vectors), jnp.float32),
            jax.ShapeDtypeStruct((orb, vectors), jnp.bfloat16),
        ],
        compiler_params=pltpu.CompilerParams(vmem_limit_bytes=received.size * 4 + 2 * SPARE),
        name="backward_first",
    )(halfwidth, turned_panels, received, base)


def pick_blocks(targets, received, panel, grid_rows):
    _, orb, _ = received.shape
    grid_cols = targets.shape[0]

    def kernel(targets_ref, received_ref, panel_ref, *outs):
        for d, out in enumerate(outs, start=1):
            for c in range(grid_rows):
                out[c] = received_ref[c * grid_cols + targets_ref[d]]

    return pl.pallas_call(
        kernel,
        in_specs=[SMEM, VMEM, VMEM],
        out_specs=[VMEM] * (grid_cols - 1),
        out_shape=[jax.ShapeDtypeStruct((grid_rows, orb, orb), jnp.bfloat16)] * (grid_cols - 1),
        compiler_params=pltpu.CompilerParams(vmem_limit_bytes=received.size * 4 + SPARE),
        name="pick_blocks",
    )(targets, received, panel)


def merge_tile(sources, targets, dense, received, stacks):
    _, orb, _ = dense.shape
    grid_rows = sources.shape[0]
    grid_cols = targets.shape[0]

    def kernel(sources_ref, targets_ref, dense_hbm, received_ref, *refs):
        *stack_refs, tile_ref, dense_ref, sem = refs
        copy = pltpu.make_async_copy(dense_hbm, dense_ref, sem)
        copy.start()
        copy.wait()
        for k in range(grid_rows):
            source = sources_ref[k]
            for d in range(grid_cols):
                cell = source * grid_cols + targets_ref[d]
                turned = received_ref[cell] if d == 0 else stack_refs[d - 1][source]
                own = dense_ref[cell].astype(jnp.float32)
                block = (own + turned.T.astype(jnp.float32)).astype(jnp.bfloat16)
                tile_ref[d * orb : (d + 1) * orb, k * orb : (k + 1) * orb] = block

    return pl.pallas_call(
        kernel,
        in_specs=[SMEM] * 2 + [HBM] + [VMEM] * grid_cols,
        out_specs=VMEM,
        out_shape=jax.ShapeDtypeStruct((grid_cols * orb, grid_rows * orb), jnp.bfloat16),
        scratch_shapes=[pltpu.VMEM(dense.shape, dense.dtype), pltpu.SemaphoreType.DMA],
        compiler_params=pltpu.CompilerParams(vmem_limit_bytes=dense.size * 8 + SPARE),
        name="merge_tile",
    )(
        sources, targets, pltpu.with_memory_space_constraint(dense, pltpu.HBM), received, *stacks
    )


def apply_tile(tile, pieces, current, previous, center, halfwidth, grid_cols):
    height, _ = tile.shape
    orb = height // grid_cols
    vectors = current.shape[1]
    count = len(pieces)

    def kernel(center_ref, halfwidth_ref, tile_ref, current_ref, previous_ref, *refs):
        outs = refs[count:]
        total = None
        at = 0
        for ref in refs[:count]:
            depth = ref.shape[0]
            part = jnp.dot(
                tile_ref[:, at : at + depth], ref[...], preferred_element_type=jnp.float32
            )
            total = part if total is None else total + part
            at += depth
        base, scale = finish(
            total[:orb], False, current_ref, previous_ref, center_ref, halfwidth_ref
        )
        outs[0][...] = base
        for d in range(1, grid_cols):
            outs[d][...] = total[d * orb : (d + 1) * orb] * scale

    return pl.pallas_call(
        kernel,
        in_specs=[SMEM] * 2 + [VMEM] * (3 + count),
        out_specs=[VMEM] * grid_cols,
        out_shape=[jax.ShapeDtypeStruct((orb, vectors), jnp.float32)] * grid_cols,
        compiler_params=pltpu.CompilerParams(vmem_limit_bytes=tile.size * 2 + 2 * SPARE),
        name="apply_tile",
    )(center, halfwidth, tile, current, previous, *pieces)


def body(hamiltonian_blocks, block_rows, block_cols, block_counts, initial, center, halfwidth):
    grid_rows = lax.axis_size("row")
    grid_cols = lax.axis_size("col")
    strides = stage_strides(grid_rows)
    same = [strides, strides]
    turned = [strides, strides[::-1]]
    if [radix for _, radix in turned[0]] != [radix for _, radix in turned[1]]:
        turned = same

    def gather(parts, orders, first=0, last=None):
        for (stride, radix), (odd_stride, _) in list(zip(*orders))[first:last]:
            panel = jnp.concatenate(parts, axis=0)
            parts = [panel] + [
                swap_rows(panel, grid_rows, grid_cols, (k * stride, k * odd_stride))
                for k in range(1, radix)
            ]
        return parts

    row = lax.axis_index("row")
    col = lax.axis_index("col")
    early = arrival_order(strides)
    late = [arrival_order(order) for order in turned]
    early_sources = jnp.array(early, jnp.int32) ^ row
    sources = jnp.array(late, jnp.int32)[col % 2] ^ row
    targets = jnp.arange(grid_cols, dtype=jnp.int32) ^ col
    pieces = gather([initial.astype(jnp.bfloat16)], same, last=1)
    dense = build_tile(
        block_rows[0], block_cols[0], block_counts, hamiltonian_blocks[0, 0],
        grid_rows, grid_cols,
    )
    dense = after(dense, pieces[1:])
    received = lax.all_to_all(dense, "row", 0, 0, tiled=True)
    panel = jnp.concatenate(gather(pieces, same, first=1), axis=0)
    turned_panel = turn_panel(early_sources, panel, dense.shape[1])
    turned_panels = [turned_panel] + [
        swap(turned_panel, "col", grid_cols, d) for d in range(1, grid_cols)
    ]
    base, *others = forward_first(
        early_sources, targets, dense, panel, initial, center, halfwidth
    )
    for d, other in enumerate(others, start=1):
        base = base + swap(other, "col", grid_cols, d)

    previous = initial
    current, panel = backward_first(lay_panels(targets, turned_panels, grid_rows), received, base, halfwidth)
    pieces = gather([panel], turned, last=1)
    stacks = []
    if grid_cols > 1:
        stacks = pick_blocks(targets, received, pieces[-1], grid_rows)
    stacks = [swap(stack, "col", grid_cols, d) for d, stack in enumerate(stacks, start=1)]
    tile = merge_tile(sources, targets, dense, received, stacks)
    for degree_step in range(1, DEGREE):
        if degree_step > 1:
            pieces = gather([current.astype(jnp.bfloat16)], turned, last=1)
        pieces = gather(pieces, turned, first=1)
        base, *others = apply_tile(tile, pieces, current, previous, center, halfwidth, grid_cols)
        following = base
        for d, other in enumerate(others, start=1):
            following = following + swap(other, "col", grid_cols, d)
        previous = current
        current = following
    return current


def solution(mesh):
    in_specs = (
        P("row", "col", None, None, None),
        P("row", "col", None),
        P("row", "col", None),
        P("row", "col"),
        P(("row", "col"), None),
        P(),
        P(),
    )
    out_specs = P(("row", "col"), None)
    return jax.shard_map(body, mesh=mesh, in_specs=in_specs, out_specs=out_specs, check_vma=False)
```

```python
import jax
import jax.numpy as jnp
from jax import lax
from jax.experimental import pallas as pl
from jax.experimental.pallas import tpu as pltpu
from jax.sharding import PartitionSpec as P

DEGREE = 3
RADIX = 4
CHUNK = 8
SPARE = 4 * 2**20

VMEM = pl.BlockSpec(memory_space=pltpu.VMEM)
SMEM = pl.BlockSpec(memory_space=pltpu.SMEM)
HBM = pl.BlockSpec(memory_space=pltpu.HBM)


def stage_strides(size):
    found = []
    stride = 1
    while stride < size:
        radix = RADIX if size % (stride * RADIX) == 0 else size // stride
        found.append((stride, radix))
        stride *= radix
    return found[::-1]


def arrival_order(strides):
    order = [0]
    for stride, radix in strides:
        order = [k * stride ^ offset for k in range(radix) for offset in order]
    return order


def swap(x, axis, size, offset):
    return lax.ppermute(x, axis, [(source, source ^ offset) for source in range(size)])


def swap_rows(x, grid_rows, grid_cols, offsets):
    pairs = [
        (row * grid_cols + col, (row ^ offsets[col % 2]) * grid_cols + col)
        for row in range(grid_rows)
        for col in range(grid_cols)
    ]
    return lax.ppermute(x, ("row", "col"), pairs)


def build_tile(rows, cols, count, stacked, grid_rows, grid_cols):
    slots, orb, _ = stacked.shape
    cells = grid_rows * grid_cols
    parts = 4 if cells % 4 == 0 else 1
    chunk = CHUNK if slots % CHUNK == 0 else slots
    chunks = slots // chunk

    def kernel(
        rows_hbm, cols_hbm, count_ref, stack_hbm, out_hbm,
        stack_ref, acc_ref, dense_ref, rows_ref, cols_ref, index_sems, stack_sems, sems,
    ):
        indices = [
            pltpu.make_async_copy(source, target, index_sems.at[n])
            for n, (source, target) in enumerate([(rows_hbm, rows_ref), (cols_hbm, cols_ref)])
        ]
        for copy in indices:
            copy.start()
        arrivals = []
        for n in range(chunks):
            held = pl.ds(n * chunk, chunk)
            arrivals.append(
                pltpu.make_async_copy(stack_hbm.at[held], stack_ref.at[held], stack_sems.at[n])
            )
            arrivals[-1].start()
        acc_ref[...] = jnp.zeros_like(acc_ref)
        for copy in indices:
            copy.wait()
        count = count_ref[0, 0]
        for n, copy in enumerate(arrivals):
            copy.wait()
            for s in range(n * chunk, (n + 1) * chunk):
                cell = jnp.where(s < count, cols_ref[0, s] * grid_cols + rows_ref[0, s], cells)
                acc_ref[cell] += stack_ref[s].astype(jnp.float32)
        copies = []
        for n in range(parts):
            held = pl.ds(n * (cells // parts), cells // parts)
            dense_ref[held] = acc_ref[held].astype(jnp.bfloat16)
            copies.append(pltpu.make_async_copy(dense_ref.at[held], out_hbm.at[held], sems.at[n]))
            copies[-1].start()
        for copy in copies:
            copy.wait()

    return pl.pallas_call(
        kernel,
        in_specs=[HBM, HBM, SMEM, HBM],
        out_specs=HBM,
        scratch_shapes=[
            pltpu.VMEM(stacked.shape, jnp.bfloat16),
            pltpu.VMEM((cells + 1, orb, orb), jnp.float32),
            pltpu.VMEM((cells, orb, orb), jnp.bfloat16),
            pltpu.SMEM(rows.shape, jnp.int32),
            pltpu.SMEM(cols.shape, jnp.int32),
            pltpu.SemaphoreType.DMA((2,)),
            pltpu.SemaphoreType.DMA((chunks,)),
            pltpu.SemaphoreType.DMA((parts,)),
        ],
        out_shape=pltpu.HBM((cells, orb, orb), jnp.bfloat16),
        compiler_params=pltpu.CompilerParams(
            vmem_limit_bytes=(cells + 1) * orb * orb * 6 + stacked.size * 2 + SPARE
        ),
        name="build_tile",
    )(
        pltpu.with_memory_space_constraint(rows, pltpu.HBM),
        pltpu.with_memory_space_constraint(cols, pltpu.HBM),
        count,
        pltpu.with_memory_space_constraint(stacked, pltpu.HBM),
    )


def after(x, others):
    def kernel(*refs):
        pass

    return pl.pallas_call(
        kernel,
        in_specs=[HBM] + [VMEM] * len(others),
        out_specs=HBM,
        out_shape=pltpu.HBM(x.shape, x.dtype),
        input_output_aliases={0: 0},
        compiler_params=pltpu.CompilerParams(vmem_limit_bytes=SPARE),
        name="after",
    )(pltpu.with_memory_space_constraint(x, pltpu.HBM), *others)


def finish(own, first, current_ref, previous_ref, center_ref, halfwidth_ref):
    scale = (1.0 if first else 2.0) / jnp.full((1, own.shape[1]), halfwidth_ref[0])
    own = (own - center_ref[0] * current_ref[...]) * scale
    return own if first else own - previous_ref[...], scale


def forward_first(sources, targets, dense, panel, current, center, halfwidth):
    cells, orb, _ = dense.shape
    grid_rows = sources.shape[0]
    grid_cols = targets.shape[0]
    vectors = current.shape[1]

    def kernel(
        sources_ref, targets_ref, center_ref, halfwidth_ref,
        dense_hbm, panel_ref, current_ref, *refs,
    ):
        *outs, total_ref, dense_ref, sem = refs
        copy = pltpu.make_async_copy(dense_hbm, dense_ref, sem)
        copy.start()
        copy.wait()
        total = None
        for k in range(grid_rows):
            blocks = dense_ref[pl.ds(sources_ref[k] * grid_cols, grid_cols)]
            part = jnp.dot(
                blocks.reshape(grid_cols * orb, orb), panel_ref[k * orb : (k + 1) * orb],
                preferred_element_type=jnp.float32,
            )
            total = part if total is None else total + part
        total_ref[...] = total.reshape(grid_cols, orb, vectors)
        base, scale = finish(
            total_ref[targets_ref[0]], True, current_ref, None, center_ref, halfwidth_ref
        )
        outs[0][...] = base
        for d in range(1, grid_cols):
            outs[d][...] = total_ref[targets_ref[d]] * scale

    return pl.pallas_call(
        kernel,
        in_specs=[SMEM] * 4 + [HBM] + [VMEM] * 2,
        out_specs=[VMEM] * grid_cols,
        out_shape=[jax.ShapeDtypeStruct((orb, vectors), jnp.float32)] * grid_cols,
        scratch_shapes=[
            pltpu.VMEM((grid_cols, orb, vectors), jnp.float32),
            pltpu.VMEM(dense.shape, dense.dtype),
            pltpu.SemaphoreType.DMA,
        ],
        compiler_params=pltpu.CompilerParams(vmem_limit_bytes=dense.size * 2 + 2 * SPARE),
        name="forward_first",
    )(
        sources, targets, center, halfwidth,
        pltpu.with_memory_space_constraint(dense, pltpu.HBM), panel, current,
    )


def turn_panel(sources, panel, orb):
    grid_rows = sources.shape[0]
    vectors = panel.shape[1]

    def kernel(sources_ref, panel_ref, turned_ref):
        for k in range(grid_rows):
            turned = panel_ref[k * orb : (k + 1) * orb].T
            turned_ref[:, pl.ds(pl.multiple_of(sources_ref[k] * orb, orb), orb)] = turned

    return pl.pallas_call(
        kernel,
        in_specs=[SMEM, VMEM],
        out_specs=VMEM,
        out_shape=jax.ShapeDtypeStruct((vectors, grid_rows * orb), jnp.bfloat16),
        compiler_params=pltpu.CompilerParams(vmem_limit_bytes=panel.size * 4 + SPARE),
        name="turn_panel",
    )(sources, panel)


def lay_panels(targets, turned_panels, grid_rows):
    grid_cols = targets.shape[0]
    vectors, width = turned_panels[0].shape
    orb = width // grid_rows

    def kernel(targets_ref, *refs):
        *turned_refs, out_ref = refs
        for d, turned_ref in enumerate(turned_refs):
            for c in range(grid_rows):
                at = pl.multiple_of((c * grid_cols + targets_ref[d]) * orb, orb)
                out_ref[:, pl.ds(at, orb)] = turned_ref[:, c * orb : (c + 1) * orb]

    return pl.pallas_call(
        kernel,
        in_specs=[SMEM] + [VMEM] * grid_cols,
        out_specs=VMEM,
        out_shape=jax.ShapeDtypeStruct((vectors, grid_cols * width), jnp.bfloat16),
        compiler_params=pltpu.CompilerParams(vmem_limit_bytes=vectors * width * 4 * grid_cols + SPARE),
        name="lay_panels",
    )(targets, *turned_panels)


def backward_first(turned_panels, received, base, halfwidth):
    cells, orb, _ = received.shape
    vectors = base.shape[1]

    def kernel(halfwidth_ref, turned_ref, received_ref, base_ref, out_ref, panel_ref):
        blocks = received_ref[...].reshape(cells * orb, orb)
        total = jnp.dot(turned_ref[...], blocks, preferred_element_type=jnp.float32)
        out = base_ref[...] + total.T / jnp.full((1, vectors), halfwidth_ref[0])
        out_ref[...] = out
        panel_ref[...] = out.astype(jnp.bfloat16)

    return pl.pallas_call(
        kernel,
        in_specs=[SMEM] + [VMEM] * 3,
        out_specs=[VMEM] * 2,
        out_shape=[
            jax.ShapeDtypeStruct((orb, vectors), jnp.float32),
            jax.ShapeDtypeStruct((orb, vectors), jnp.bfloat16),
        ],
        compiler_params=pltpu.CompilerParams(vmem_limit_bytes=received.size * 4 + 2 * SPARE),
        name="backward_first",
    )(halfwidth, turned_panels, received, base)


def pick_blocks(targets, received, panel, grid_rows):
    _, orb, _ = received.shape
    grid_cols = targets.shape[0]

    def kernel(targets_ref, received_ref, panel_ref, *outs):
        for d, out in enumerate(outs, start=1):
            for c in range(grid_rows):
                out[c] = received_ref[c * grid_cols + targets_ref[d]]

    return pl.pallas_call(
        kernel,
        in_specs=[SMEM, VMEM, VMEM],
        out_specs=[VMEM] * (grid_cols - 1),
        out_shape=[jax.ShapeDtypeStruct((grid_rows, orb, orb), jnp.bfloat16)] * (grid_cols - 1),
        compiler_params=pltpu.CompilerParams(vmem_limit_bytes=received.size * 4 + SPARE),
        name="pick_blocks",
    )(targets, received, panel)


def merge_tile(sources, targets, dense, received, stacks):
    _, orb, _ = dense.shape
    grid_rows = sources.shape[0]
    grid_cols = targets.shape[0]

    def kernel(sources_ref, targets_ref, dense_hbm, received_ref, *refs):
        *stack_refs, tile_ref, dense_ref, sem = refs
        copy = pltpu.make_async_copy(dense_hbm, dense_ref, sem)
        copy.start()
        copy.wait()
        for k in range(grid_rows):
            source = sources_ref[k]
            for d in range(grid_cols):
                cell = source * grid_cols + targets_ref[d]
                turned = received_ref[cell] if d == 0 else stack_refs[d - 1][source]
                own = dense_ref[cell].astype(jnp.float32)
                block = (own + turned.T.astype(jnp.float32)).astype(jnp.bfloat16)
                tile_ref[d * orb : (d + 1) * orb, k * orb : (k + 1) * orb] = block

    return pl.pallas_call(
        kernel,
        in_specs=[SMEM] * 2 + [HBM] + [VMEM] * grid_cols,
        out_specs=VMEM,
        out_shape=jax.ShapeDtypeStruct((grid_cols * orb, grid_rows * orb), jnp.bfloat16),
        scratch_shapes=[pltpu.VMEM(dense.shape, dense.dtype), pltpu.SemaphoreType.DMA],
        compiler_params=pltpu.CompilerParams(vmem_limit_bytes=dense.size * 8 + SPARE),
        name="merge_tile",
    )(
        sources, targets, pltpu.with_memory_space_constraint(dense, pltpu.HBM), received, *stacks
    )


def apply_tile(tile, pieces, current, previous, center, halfwidth, grid_cols):
    height, _ = tile.shape
    orb = height // grid_cols
    vectors = current.shape[1]
    count = len(pieces)

    def kernel(center_ref, halfwidth_ref, tile_ref, current_ref, previous_ref, *refs):
        outs = refs[count:]
        total = None
        at = 0
        for ref in refs[:count]:
            depth = ref.shape[0]
            part = jnp.dot(
                tile_ref[:, at : at + depth], ref[...], preferred_element_type=jnp.float32
            )
            total = part if total is None else total + part
            at += depth
        base, scale = finish(
            total[:orb], False, current_ref, previous_ref, center_ref, halfwidth_ref
        )
        outs[0][...] = base
        for d in range(1, grid_cols):
            outs[d][...] = total[d * orb : (d + 1) * orb] * scale

    return pl.pallas_call(
        kernel,
        in_specs=[SMEM] * 2 + [VMEM] * (3 + count),
        out_specs=[VMEM] * grid_cols,
        out_shape=[jax.ShapeDtypeStruct((orb, vectors), jnp.float32)] * grid_cols,
        compiler_params=pltpu.CompilerParams(vmem_limit_bytes=tile.size * 2 + 2 * SPARE),
        name="apply_tile",
    )(center, halfwidth, tile, current, previous, *pieces)


def body(hamiltonian_blocks, block_rows, block_cols, block_counts, initial, center, halfwidth):
    grid_rows = lax.axis_size("row")
    grid_cols = lax.axis_size("col")
    strides = stage_strides(grid_rows)
    same = [strides, strides]
    turned = [strides, strides[::-1]]
    if [radix for _, radix in turned[0]] != [radix for _, radix in turned[1]]:
        turned = same

    def gather(parts, orders, first=0, last=None):
        for (stride, radix), (odd_stride, _) in list(zip(*orders))[first:last]:
            panel = jnp.concatenate(parts, axis=0)
            parts = [panel] + [
                swap_rows(panel, grid_rows, grid_cols, (k * stride, k * odd_stride))
                for k in range(1, radix)
            ]
        return parts

    row = lax.axis_index("row")
    col = lax.axis_index("col")
    early = arrival_order(strides)
    late = [arrival_order(order) for order in turned]
    early_sources = jnp.array(early, jnp.int32) ^ row
    sources = jnp.array(late, jnp.int32)[col % 2] ^ row
    targets = jnp.arange(grid_cols, dtype=jnp.int32) ^ col
    pieces = gather([initial.astype(jnp.bfloat16)], same, last=1)
    dense = build_tile(
        block_rows[0], block_cols[0], block_counts, hamiltonian_blocks[0, 0],
        grid_rows, grid_cols,
    )
    dense = after(dense, pieces[1:])
    received = lax.all_to_all(dense, "row", 0, 0, tiled=True)
    panel = jnp.concatenate(gather(pieces, same, first=1), axis=0)
    turned_panel = turn_panel(early_sources, panel, dense.shape[1])
    turned_panels = [turned_panel] + [
        swap(turned_panel, "col", grid_cols, d) for d in range(1, grid_cols)
    ]
    base, *others = forward_first(
        early_sources, targets, dense, panel, initial, center, halfwidth
    )
    for d, other in enumerate(others, start=1):
        base = base + swap(other, "col", grid_cols, d)

    previous = initial
    current, panel = backward_first(lay_panels(targets, turned_panels, grid_rows), received, base, halfwidth)
    pieces = gather([panel], turned, last=1)
    stacks = []
    if grid_cols > 1:
        stacks = pick_blocks(targets, received, pieces[-1], grid_rows)
    stacks = [swap(stack, "col", grid_cols, d) for d, stack in enumerate(stacks, start=1)]
    tile = merge_tile(sources, targets, dense, received, stacks)
    for degree_step in range(1, DEGREE):
        if degree_step > 1:
            pieces = gather([current.astype(jnp.bfloat16)], turned, last=1)
        pieces = gather(pieces, turned, first=1)
        base, *others = apply_tile(tile, pieces, current, previous, center, halfwidth, grid_cols)
        following = base
        for d, other in enumerate(others, start=1):
            following = following + swap(other, "col", grid_cols, d)
        previous = current
        current = following
    return current


def solution(mesh):
    in_specs = (
        P("row", "col", None, None, None),
        P("row", "col", None),
        P("row", "col", None),
        P("row", "col"),
        P(("row", "col"), None),
        P(),
        P(),
    )
    out_specs = P(("row", "col"), None)
    return jax.shard_map(body, mesh=mesh, in_specs=in_specs, out_specs=out_specs, check_vma=False)
```

```python
import jax
import jax.numpy as jnp
from jax import lax
from jax.experimental import pallas as pl
from jax.experimental.pallas import tpu as pltpu
from jax.sharding import PartitionSpec as P

DEGREE = 3
RADIX = 4
CHUNK = 8
SPARE = 4 * 2**20

VMEM = pl.BlockSpec(memory_space=pltpu.VMEM)
SMEM = pl.BlockSpec(memory_space=pltpu.SMEM)
HBM = pl.BlockSpec(memory_space=pltpu.HBM)


def stage_strides(size):
    found = []
    stride = 1
    while stride < size:
        radix = RADIX if size % (stride * RADIX) == 0 else size // stride
        found.append((stride, radix))
        stride *= radix
    return found[::-1]


def arrival_order(strides):
    order = [0]
    for stride, radix in strides:
        order = [k * stride ^ offset for k in range(radix) for offset in order]
    return order


def swap(x, axis, size, offset):
    return lax.ppermute(x, axis, [(source, source ^ offset) for source in range(size)])


def swap_rows(x, grid_rows, grid_cols, offsets):
    pairs = [
        (row * grid_cols + col, (row ^ offsets[col % 2]) * grid_cols + col)
        for row in range(grid_rows)
        for col in range(grid_cols)
    ]
    return lax.ppermute(x, ("row", "col"), pairs)


def build_tile(rows, cols, count, stacked, grid_rows, grid_cols):
    slots, orb, _ = stacked.shape
    cells = grid_rows * grid_cols
    parts = 4 if cells % 4 == 0 else 1
    chunk = CHUNK if slots % CHUNK == 0 else slots
    chunks = slots // chunk

    def kernel(
        rows_hbm, cols_hbm, count_ref, stack_hbm, out_hbm,
        stack_ref, even_ref, odd_ref, dense_ref, rows_ref, cols_ref, index_sems, stack_sems, sems,
    ):
        indices = [
            pltpu.make_async_copy(source, target, index_sems.at[n])
            for n, (source, target) in enumerate([(rows_hbm, rows_ref), (cols_hbm, cols_ref)])
        ]
        for copy in indices:
            copy.start()
        arrivals = []
        for n in range(chunks):
            held = pl.ds(n * chunk, chunk)
            arrivals.append(
                pltpu.make_async_copy(stack_hbm.at[held], stack_ref.at[held], stack_sems.at[n])
            )
            arrivals[-1].start()
        even_ref[...] = jnp.zeros_like(even_ref)
        odd_ref[...] = jnp.zeros_like(odd_ref)
        for copy in indices:
            copy.wait()
        count = count_ref[0, 0]
        for n, copy in enumerate(arrivals):
            copy.wait()
            for s in range(n * chunk, (n + 1) * chunk):
                cell = jnp.where(s < count, cols_ref[0, s] * grid_cols + rows_ref[0, s], cells)
                acc_ref = odd_ref if s % 2 else even_ref
                acc_ref[cell] += stack_ref[s].astype(jnp.float32)
        copies = []
        for n in range(parts):
            held = pl.ds(n * (cells // parts), cells // parts)
            dense_ref[held] = (even_ref[held] + odd_ref[held]).astype(jnp.bfloat16)
            copies.append(pltpu.make_async_copy(dense_ref.at[held], out_hbm.at[held], sems.at[n]))
            copies[-1].start()
        for copy in copies:
            copy.wait()

    return pl.pallas_call(
        kernel,
        in_specs=[HBM, HBM, SMEM, HBM],
        out_specs=HBM,
        scratch_shapes=[
            pltpu.VMEM(stacked.shape, jnp.bfloat16),
            pltpu.VMEM((cells + 1, orb, orb), jnp.float32),
            pltpu.VMEM((cells + 1, orb, orb), jnp.float32),
            pltpu.VMEM((cells, orb, orb), jnp.bfloat16),
            pltpu.SMEM(rows.shape, jnp.int32),
            pltpu.SMEM(cols.shape, jnp.int32),
            pltpu.SemaphoreType.DMA((2,)),
            pltpu.SemaphoreType.DMA((chunks,)),
            pltpu.SemaphoreType.DMA((parts,)),
        ],
        out_shape=pltpu.HBM((cells, orb, orb), jnp.bfloat16),
        compiler_params=pltpu.CompilerParams(
            vmem_limit_bytes=(cells + 1) * orb * orb * 10 + stacked.size * 2 + SPARE
        ),
        name="build_tile",
    )(
        pltpu.with_memory_space_constraint(rows, pltpu.HBM),
        pltpu.with_memory_space_constraint(cols, pltpu.HBM),
        count,
        pltpu.with_memory_space_constraint(stacked, pltpu.HBM),
    )


def after(x, others):
    def kernel(*refs):
        pass

    return pl.pallas_call(
        kernel,
        in_specs=[HBM] + [VMEM] * len(others),
        out_specs=HBM,
        out_shape=pltpu.HBM(x.shape, x.dtype),
        input_output_aliases={0: 0},
        compiler_params=pltpu.CompilerParams(vmem_limit_bytes=SPARE),
        name="after",
    )(pltpu.with_memory_space_constraint(x, pltpu.HBM), *others)


def finish(own, first, current_ref, previous_ref, center_ref, halfwidth_ref):
    scale = (1.0 if first else 2.0) / jnp.full((1, own.shape[1]), halfwidth_ref[0])
    own = (own - center_ref[0] * current_ref[...]) * scale
    return own if first else own - previous_ref[...], scale


def forward_first(sources, targets, dense, panel, current, center, halfwidth):
    cells, orb, _ = dense.shape
    grid_rows = sources.shape[0]
    grid_cols = targets.shape[0]
    vectors = current.shape[1]

    def kernel(
        sources_ref, targets_ref, center_ref, halfwidth_ref,
        dense_hbm, panel_ref, current_ref, *refs,
    ):
        *outs, total_ref, dense_ref, sem = refs
        copy = pltpu.make_async_copy(dense_hbm, dense_ref, sem)
        copy.start()
        copy.wait()
        total = None
        for k in range(grid_rows):
            blocks = dense_ref[pl.ds(sources_ref[k] * grid_cols, grid_cols)]
            part = jnp.dot(
                blocks.reshape(grid_cols * orb, orb), panel_ref[k * orb : (k + 1) * orb],
                preferred_element_type=jnp.float32,
            )
            total = part if total is None else total + part
        total_ref[...] = total.reshape(grid_cols, orb, vectors)
        base, scale = finish(
            total_ref[targets_ref[0]], True, current_ref, None, center_ref, halfwidth_ref
        )
        outs[0][...] = base
        for d in range(1, grid_cols):
            outs[d][...] = total_ref[targets_ref[d]] * scale

    return pl.pallas_call(
        kernel,
        in_specs=[SMEM] * 4 + [HBM] + [VMEM] * 2,
        out_specs=[VMEM] * grid_cols,
        out_shape=[jax.ShapeDtypeStruct((orb, vectors), jnp.float32)] * grid_cols,
        scratch_shapes=[
            pltpu.VMEM((grid_cols, orb, vectors), jnp.float32),
            pltpu.VMEM(dense.shape, dense.dtype),
            pltpu.SemaphoreType.DMA,
        ],
        compiler_params=pltpu.CompilerParams(vmem_limit_bytes=dense.size * 2 + 2 * SPARE),
        name="forward_first",
    )(
        sources, targets, center, halfwidth,
        pltpu.with_memory_space_constraint(dense, pltpu.HBM), panel, current,
    )


def turn_panel(sources, panel, orb):
    grid_rows = sources.shape[0]
    vectors = panel.shape[1]

    def kernel(sources_ref, panel_ref, turned_ref):
        for k in range(grid_rows):
            turned = panel_ref[k * orb : (k + 1) * orb].T
            turned_ref[:, pl.ds(pl.multiple_of(sources_ref[k] * orb, orb), orb)] = turned

    return pl.pallas_call(
        kernel,
        in_specs=[SMEM, VMEM],
        out_specs=VMEM,
        out_shape=jax.ShapeDtypeStruct((vectors, grid_rows * orb), jnp.bfloat16),
        compiler_params=pltpu.CompilerParams(vmem_limit_bytes=panel.size * 4 + SPARE),
        name="turn_panel",
    )(sources, panel)


def lay_panels(targets, turned_panels, grid_rows):
    grid_cols = targets.shape[0]
    vectors, width = turned_panels[0].shape
    orb = width // grid_rows

    def kernel(targets_ref, *refs):
        *turned_refs, out_ref = refs
        for d, turned_ref in enumerate(turned_refs):
            for c in range(grid_rows):
                at = pl.multiple_of((c * grid_cols + targets_ref[d]) * orb, orb)
                out_ref[:, pl.ds(at, orb)] = turned_ref[:, c * orb : (c + 1) * orb]

    return pl.pallas_call(
        kernel,
        in_specs=[SMEM] + [VMEM] * grid_cols,
        out_specs=VMEM,
        out_shape=jax.ShapeDtypeStruct((vectors, grid_cols * width), jnp.bfloat16),
        compiler_params=pltpu.CompilerParams(vmem_limit_bytes=vectors * width * 4 * grid_cols + SPARE),
        name="lay_panels",
    )(targets, *turned_panels)


def backward_first(turned_panels, received, base, halfwidth):
    cells, orb, _ = received.shape
    vectors = base.shape[1]

    def kernel(halfwidth_ref, turned_ref, received_ref, base_ref, out_ref, panel_ref):
        blocks = received_ref[...].reshape(cells * orb, orb)
        total = jnp.dot(turned_ref[...], blocks, preferred_element_type=jnp.float32)
        out = base_ref[...] + total.T / jnp.full((1, vectors), halfwidth_ref[0])
        out_ref[...] = out
        panel_ref[...] = out.astype(jnp.bfloat16)

    return pl.pallas_call(
        kernel,
        in_specs=[SMEM] + [VMEM] * 3,
        out_specs=[VMEM] * 2,
        out_shape=[
            jax.ShapeDtypeStruct((orb, vectors), jnp.float32),
            jax.ShapeDtypeStruct((orb, vectors), jnp.bfloat16),
        ],
        compiler_params=pltpu.CompilerParams(vmem_limit_bytes=received.size * 4 + 2 * SPARE),
        name="backward_first",
    )(halfwidth, turned_panels, received, base)


def pick_blocks(targets, received, panel, grid_rows):
    _, orb, _ = received.shape
    grid_cols = targets.shape[0]

    def kernel(targets_ref, received_ref, panel_ref, *outs):
        for d, out in enumerate(outs, start=1):
            for c in range(grid_rows):
                out[c] = received_ref[c * grid_cols + targets_ref[d]]

    return pl.pallas_call(
        kernel,
        in_specs=[SMEM, VMEM, VMEM],
        out_specs=[VMEM] * (grid_cols - 1),
        out_shape=[jax.ShapeDtypeStruct((grid_rows, orb, orb), jnp.bfloat16)] * (grid_cols - 1),
        compiler_params=pltpu.CompilerParams(vmem_limit_bytes=received.size * 4 + SPARE),
        name="pick_blocks",
    )(targets, received, panel)


def merge_tile(sources, targets, dense, received, stacks):
    _, orb, _ = dense.shape
    grid_rows = sources.shape[0]
    grid_cols = targets.shape[0]

    def kernel(sources_ref, targets_ref, dense_hbm, received_ref, *refs):
        *stack_refs, tile_ref, dense_ref, sem = refs
        copy = pltpu.make_async_copy(dense_hbm, dense_ref, sem)
        copy.start()
        copy.wait()
        for k in range(grid_rows):
            source = sources_ref[k]
            for d in range(grid_cols):
                cell = source * grid_cols + targets_ref[d]
                turned = received_ref[cell] if d == 0 else stack_refs[d - 1][source]
                own = dense_ref[cell].astype(jnp.float32)
                block = (own + turned.T.astype(jnp.float32)).astype(jnp.bfloat16)
                tile_ref[d * orb : (d + 1) * orb, k * orb : (k + 1) * orb] = block

    return pl.pallas_call(
        kernel,
        in_specs=[SMEM] * 2 + [HBM] + [VMEM] * grid_cols,
        out_specs=VMEM,
        out_shape=jax.ShapeDtypeStruct((grid_cols * orb, grid_rows * orb), jnp.bfloat16),
        scratch_shapes=[pltpu.VMEM(dense.shape, dense.dtype), pltpu.SemaphoreType.DMA],
        compiler_params=pltpu.CompilerParams(vmem_limit_bytes=dense.size * 8 + SPARE),
        name="merge_tile",
    )(
        sources, targets, pltpu.with_memory_space_constraint(dense, pltpu.HBM), received, *stacks
    )


def apply_tile(tile, pieces, current, previous, center, halfwidth, grid_cols):
    height, _ = tile.shape
    orb = height // grid_cols
    vectors = current.shape[1]
    count = len(pieces)

    def kernel(center_ref, halfwidth_ref, tile_ref, current_ref, previous_ref, *refs):
        outs = refs[count:]
        total = None
        at = 0
        for ref in refs[:count]:
            depth = ref.shape[0]
            part = jnp.dot(
                tile_ref[:, at : at + depth], ref[...], preferred_element_type=jnp.float32
            )
            total = part if total is None else total + part
            at += depth
        base, scale = finish(
            total[:orb], False, current_ref, previous_ref, center_ref, halfwidth_ref
        )
        outs[0][...] = base
        for d in range(1, grid_cols):
            outs[d][...] = total[d * orb : (d + 1) * orb] * scale

    return pl.pallas_call(
        kernel,
        in_specs=[SMEM] * 2 + [VMEM] * (3 + count),
        out_specs=[VMEM] * grid_cols,
        out_shape=[jax.ShapeDtypeStruct((orb, vectors), jnp.float32)] * grid_cols,
        compiler_params=pltpu.CompilerParams(vmem_limit_bytes=tile.size * 2 + 2 * SPARE),
        name="apply_tile",
    )(center, halfwidth, tile, current, previous, *pieces)


def body(hamiltonian_blocks, block_rows, block_cols, block_counts, initial, center, halfwidth):
    grid_rows = lax.axis_size("row")
    grid_cols = lax.axis_size("col")
    strides = stage_strides(grid_rows)
    same = [strides, strides]
    turned = [strides, strides[::-1]]
    if [radix for _, radix in turned[0]] != [radix for _, radix in turned[1]]:
        turned = same

    def gather(parts, orders, first=0, last=None):
        for (stride, radix), (odd_stride, _) in list(zip(*orders))[first:last]:
            panel = jnp.concatenate(parts, axis=0)
            parts = [panel] + [
                swap_rows(panel, grid_rows, grid_cols, (k * stride, k * odd_stride))
                for k in range(1, radix)
            ]
        return parts

    row = lax.axis_index("row")
    col = lax.axis_index("col")
    early = arrival_order(strides)
    late = [arrival_order(order) for order in turned]
    early_sources = jnp.array(early, jnp.int32) ^ row
    sources = jnp.array(late, jnp.int32)[col % 2] ^ row
    targets = jnp.arange(grid_cols, dtype=jnp.int32) ^ col
    pieces = gather([initial.astype(jnp.bfloat16)], same, last=1)
    dense = build_tile(
        block_rows[0], block_cols[0], block_counts, hamiltonian_blocks[0, 0],
        grid_rows, grid_cols,
    )
    dense = after(dense, pieces[1:])
    received = lax.all_to_all(dense, "row", 0, 0, tiled=True)
    panel = jnp.concatenate(gather(pieces, same, first=1), axis=0)
    turned_panel = turn_panel(early_sources, panel, dense.shape[1])
    turned_panels = [turned_panel] + [
        swap(turned_panel, "col", grid_cols, d) for d in range(1, grid_cols)
    ]
    base, *others = forward_first(
        early_sources, targets, dense, panel, initial, center, halfwidth
    )
    for d, other in enumerate(others, start=1):
        base = base + swap(other, "col", grid_cols, d)

    previous = initial
    current, panel = backward_first(lay_panels(targets, turned_panels, grid_rows), received, base, halfwidth)
    pieces = gather([panel], turned, last=1)
    stacks = []
    if grid_cols > 1:
        stacks = pick_blocks(targets, received, pieces[-1], grid_rows)
    stacks = [swap(stack, "col", grid_cols, d) for d, stack in enumerate(stacks, start=1)]
    tile = merge_tile(sources, targets, dense, received, stacks)
    for degree_step in range(1, DEGREE):
        if degree_step > 1:
            pieces = gather([current.astype(jnp.bfloat16)], turned, last=1)
        pieces = gather(pieces, turned, first=1)
        base, *others = apply_tile(tile, pieces, current, previous, center, halfwidth, grid_cols)
        following = base
        for d, other in enumerate(others, start=1):
            following = following + swap(other, "col", grid_cols, d)
        previous = current
        current = following
    return current


def solution(mesh):
    in_specs = (
        P("row", "col", None, None, None),
        P("row", "col", None),
        P("row", "col", None),
        P("row", "col"),
        P(("row", "col"), None),
        P(),
        P(),
    )
    out_specs = P(("row", "col"), None)
    return jax.shard_map(body, mesh=mesh, in_specs=in_specs, out_specs=out_specs, check_vma=False)
```

```python
import jax
import jax.numpy as jnp
from jax import lax
from jax.experimental import pallas as pl
from jax.experimental.pallas import tpu as pltpu
from jax.sharding import PartitionSpec as P

DEGREE = 3
RADIX = 4
CHUNK = 8
SPARE = 4 * 2**20

VMEM = pl.BlockSpec(memory_space=pltpu.VMEM)
SMEM = pl.BlockSpec(memory_space=pltpu.SMEM)
HBM = pl.BlockSpec(memory_space=pltpu.HBM)


def stage_strides(size):
    found = []
    stride = 1
    while stride < size:
        radix = RADIX if size % (stride * RADIX) == 0 else size // stride
        found.append((stride, radix))
        stride *= radix
    return found[::-1]


def arrival_order(strides):
    order = [0]
    for stride, radix in strides:
        order = [k * stride ^ offset for k in range(radix) for offset in order]
    return order


def swap(x, axis, size, offset):
    return lax.ppermute(x, axis, [(source, source ^ offset) for source in range(size)])


def swap_rows(x, grid_rows, grid_cols, offsets):
    pairs = [
        (row * grid_cols + col, (row ^ offsets[col % 2]) * grid_cols + col)
        for row in range(grid_rows)
        for col in range(grid_cols)
    ]
    return lax.ppermute(x, ("row", "col"), pairs)


def build_tile(rows, cols, count, stacked, grid_rows, grid_cols):
    slots, orb, _ = stacked.shape
    cells = grid_rows * grid_cols
    parts = 4 if cells % 4 == 0 else 1
    chunk = CHUNK if slots % CHUNK == 0 else slots
    chunks = slots // chunk

    def kernel(
        rows_hbm, cols_hbm, count_ref, stack_hbm, out_hbm,
        stack_ref, acc_ref, dense_ref, rows_ref, cols_ref, index_sems, stack_sems, sems,
    ):
        indices = [
            pltpu.make_async_copy(source, target, index_sems.at[n])
            for n, (source, target) in enumerate([(rows_hbm, rows_ref), (cols_hbm, cols_ref)])
        ]
        for copy in indices:
            copy.start()
        arrivals = []
        for n in range(chunks):
            held = pl.ds(n * chunk, chunk)
            arrivals.append(
                pltpu.make_async_copy(stack_hbm.at[held], stack_ref.at[held], stack_sems.at[n])
            )
            arrivals[-1].start()
        acc_ref[...] = jnp.zeros_like(acc_ref)
        for copy in indices:
            copy.wait()
        count = count_ref[0, 0]
        for n, copy in enumerate(arrivals):
            copy.wait()
            for s in range(n * chunk, (n + 1) * chunk):
                cell = jnp.where(s < count, cols_ref[0, s] * grid_cols + rows_ref[0, s], cells)
                acc_ref[cell] += stack_ref[s].astype(jnp.float32)
        copies = []
        for n in range(parts):
            held = pl.ds(n * (cells // parts), cells // parts)
            dense_ref[held] = acc_ref[held].astype(jnp.bfloat16)
            copies.append(pltpu.make_async_copy(dense_ref.at[held], out_hbm.at[held], sems.at[n]))
            copies[-1].start()
        for copy in copies:
            copy.wait()

    return pl.pallas_call(
        kernel,
        in_specs=[HBM, HBM, SMEM, HBM],
        out_specs=HBM,
        scratch_shapes=[
            pltpu.VMEM(stacked.shape, jnp.bfloat16),
            pltpu.VMEM((cells + 1, orb, orb), jnp.float32),
            pltpu.VMEM((cells, orb, orb), jnp.bfloat16),
            pltpu.SMEM(rows.shape, jnp.int32),
            pltpu.SMEM(cols.shape, jnp.int32),
            pltpu.SemaphoreType.DMA((2,)),
            pltpu.SemaphoreType.DMA((chunks,)),
            pltpu.SemaphoreType.DMA((parts,)),
        ],
        out_shape=pltpu.HBM((cells, orb, orb), jnp.bfloat16),
        compiler_params=pltpu.CompilerParams(
            vmem_limit_bytes=(cells + 1) * orb * orb * 6 + stacked.size * 2 + SPARE
        ),
        name="build_tile",
    )(
        pltpu.with_memory_space_constraint(rows, pltpu.HBM),
        pltpu.with_memory_space_constraint(cols, pltpu.HBM),
        count,
        pltpu.with_memory_space_constraint(stacked, pltpu.HBM),
    )


def after(x, others):
    def kernel(*refs):
        pass

    return pl.pallas_call(
        kernel,
        in_specs=[HBM] + [VMEM] * len(others),
        out_specs=HBM,
        out_shape=pltpu.HBM(x.shape, x.dtype),
        input_output_aliases={0: 0},
        compiler_params=pltpu.CompilerParams(vmem_limit_bytes=SPARE),
        name="after",
    )(pltpu.with_memory_space_constraint(x, pltpu.HBM), *others)


def finish(own, first, current_ref, previous_ref, center_ref, halfwidth_ref):
    scale = (1.0 if first else 2.0) / jnp.full((1, own.shape[1]), halfwidth_ref[0])
    own = (own - center_ref[0] * current_ref[...]) * scale
    return own if first else own - previous_ref[...], scale


def forward_first(sources, targets, dense, panel, current, center, halfwidth):
    cells, orb, _ = dense.shape
    grid_rows = sources.shape[0]
    grid_cols = targets.shape[0]
    vectors = current.shape[1]

    def kernel(
        sources_ref, targets_ref, center_ref, halfwidth_ref,
        dense_hbm, panel_ref, current_ref, *refs,
    ):
        *outs, total_ref, dense_ref, sem = refs
        copy = pltpu.make_async_copy(dense_hbm, dense_ref, sem)
        copy.start()
        copy.wait()
        total = None
        for k in range(grid_rows):
            blocks = dense_ref[pl.ds(sources_ref[k] * grid_cols, grid_cols)]
            part = jnp.dot(
                blocks.reshape(grid_cols * orb, orb), panel_ref[k * orb : (k + 1) * orb],
                preferred_element_type=jnp.float32,
            )
            total = part if total is None else total + part
        total_ref[...] = total.reshape(grid_cols, orb, vectors)
        base, scale = finish(
            total_ref[targets_ref[0]], True, current_ref, None, center_ref, halfwidth_ref
        )
        outs[0][...] = base
        for d in range(1, grid_cols):
            outs[d][...] = total_ref[targets_ref[d]] * scale

    return pl.pallas_call(
        kernel,
        in_specs=[SMEM] * 4 + [HBM] + [VMEM] * 2,
        out_specs=[VMEM] * grid_cols,
        out_shape=[jax.ShapeDtypeStruct((orb, vectors), jnp.float32)] * grid_cols,
        scratch_shapes=[
            pltpu.VMEM((grid_cols, orb, vectors), jnp.float32),
            pltpu.VMEM(dense.shape, dense.dtype),
            pltpu.SemaphoreType.DMA,
        ],
        compiler_params=pltpu.CompilerParams(vmem_limit_bytes=dense.size * 2 + 2 * SPARE),
        name="forward_first",
    )(
        sources, targets, center, halfwidth,
        pltpu.with_memory_space_constraint(dense, pltpu.HBM), panel, current,
    )


def turn_panel(sources, panel, orb):
    grid_rows = sources.shape[0]
    vectors = panel.shape[1]

    def kernel(sources_ref, panel_ref, turned_ref):
        for k in range(grid_rows):
            turned = panel_ref[k * orb : (k + 1) * orb].T
            turned_ref[:, pl.ds(pl.multiple_of(sources_ref[k] * orb, orb), orb)] = turned

    return pl.pallas_call(
        kernel,
        in_specs=[SMEM, VMEM],
        out_specs=VMEM,
        out_shape=jax.ShapeDtypeStruct((vectors, grid_rows * orb), jnp.bfloat16),
        compiler_params=pltpu.CompilerParams(vmem_limit_bytes=panel.size * 4 + SPARE),
        name="turn_panel",
    )(sources, panel)


def lay_panels(targets, turned_panels, grid_rows):
    grid_cols = targets.shape[0]
    vectors, width = turned_panels[0].shape
    orb = width // grid_rows

    def kernel(targets_ref, *refs):
        *turned_refs, out_ref = refs
        for d, turned_ref in enumerate(turned_refs):
            for c in range(grid_rows):
                at = pl.multiple_of((c * grid_cols + targets_ref[d]) * orb, orb)
                out_ref[:, pl.ds(at, orb)] = turned_ref[:, c * orb : (c + 1) * orb]

    return pl.pallas_call(
        kernel,
        in_specs=[SMEM] + [VMEM] * grid_cols,
        out_specs=VMEM,
        out_shape=jax.ShapeDtypeStruct((vectors, grid_cols * width), jnp.bfloat16),
        compiler_params=pltpu.CompilerParams(vmem_limit_bytes=vectors * width * 4 * grid_cols + SPARE),
        name="lay_panels",
    )(targets, *turned_panels)


def backward_first(targets, turned_panels, received, base, halfwidth):
    cells, orb, _ = received.shape
    grid_cols = targets.shape[0]
    grid_rows = cells // grid_cols
    vectors = base.shape[1]

    def kernel(targets_ref, halfwidth_ref, turned_ref, received_ref, base_ref, out_ref, panel_ref, *picked):
        blocks = received_ref[...].reshape(cells * orb, orb)
        total = jnp.dot(turned_ref[...], blocks, preferred_element_type=jnp.float32)
        for d, picked_ref in enumerate(picked, start=1):
            for c in range(grid_rows):
                picked_ref[c] = received_ref[c * grid_cols + targets_ref[d]]
        out = base_ref[...] + total.T / jnp.full((1, vectors), halfwidth_ref[0])
        out_ref[...] = out
        panel_ref[...] = out.astype(jnp.bfloat16)

    return pl.pallas_call(
        kernel,
        in_specs=[SMEM] * 2 + [VMEM] * 3,
        out_specs=[VMEM] * (1 + grid_cols),
        out_shape=[
            jax.ShapeDtypeStruct((orb, vectors), jnp.float32),
            jax.ShapeDtypeStruct((orb, vectors), jnp.bfloat16),
        ]
        + [jax.ShapeDtypeStruct((grid_rows, orb, orb), jnp.bfloat16)] * (grid_cols - 1),
        compiler_params=pltpu.CompilerParams(vmem_limit_bytes=received.size * 6 + 2 * SPARE),
        name="backward_first",
    )(targets, halfwidth, turned_panels, received, base)


def merge_tile(sources, targets, dense, received, stacks):
    _, orb, _ = dense.shape
    grid_rows = sources.shape[0]
    grid_cols = targets.shape[0]

    def kernel(sources_ref, targets_ref, dense_hbm, received_ref, *refs):
        *stack_refs, tile_ref, dense_ref, sem = refs
        copy = pltpu.make_async_copy(dense_hbm, dense_ref, sem)
        copy.start()
        copy.wait()
        for k in range(grid_rows):
            source = sources_ref[k]
            for d in range(grid_cols):
                cell = source * grid_cols + targets_ref[d]
                turned = received_ref[cell] if d == 0 else stack_refs[d - 1][source]
                own = dense_ref[cell].astype(jnp.float32)
                block = (own + turned.T.astype(jnp.float32)).astype(jnp.bfloat16)
                tile_ref[d * orb : (d + 1) * orb, k * orb : (k + 1) * orb] = block

    return pl.pallas_call(
        kernel,
        in_specs=[SMEM] * 2 + [HBM] + [VMEM] * grid_cols,
        out_specs=VMEM,
        out_shape=jax.ShapeDtypeStruct((grid_cols * orb, grid_rows * orb), jnp.bfloat16),
        scratch_shapes=[pltpu.VMEM(dense.shape, dense.dtype), pltpu.SemaphoreType.DMA],
        compiler_params=pltpu.CompilerParams(vmem_limit_bytes=dense.size * 8 + SPARE),
        name="merge_tile",
    )(
        sources, targets, pltpu.with_memory_space_constraint(dense, pltpu.HBM), received, *stacks
    )


def apply_tile(tile, pieces, current, previous, center, halfwidth, grid_cols):
    height, _ = tile.shape
    orb = height // grid_cols
    vectors = current.shape[1]
    count = len(pieces)

    def kernel(center_ref, halfwidth_ref, tile_ref, current_ref, previous_ref, *refs):
        outs = refs[count:]
        total = None
        at = 0
        for ref in refs[:count]:
            depth = ref.shape[0]
            part = jnp.dot(
                tile_ref[:, at : at + depth], ref[...], preferred_element_type=jnp.float32
            )
            total = part if total is None else total + part
            at += depth
        base, scale = finish(
            total[:orb], False, current_ref, previous_ref, center_ref, halfwidth_ref
        )
        outs[0][...] = base
        for d in range(1, grid_cols):
            outs[d][...] = total[d * orb : (d + 1) * orb] * scale

    return pl.pallas_call(
        kernel,
        in_specs=[SMEM] * 2 + [VMEM] * (3 + count),
        out_specs=[VMEM] * grid_cols,
        out_shape=[jax.ShapeDtypeStruct((orb, vectors), jnp.float32)] * grid_cols,
        compiler_params=pltpu.CompilerParams(vmem_limit_bytes=tile.size * 2 + 2 * SPARE),
        name="apply_tile",
    )(center, halfwidth, tile, current, previous, *pieces)


def body(hamiltonian_blocks, block_rows, block_cols, block_counts, initial, center, halfwidth):
    grid_rows = lax.axis_size("row")
    grid_cols = lax.axis_size("col")
    strides = stage_strides(grid_rows)
    same = [strides, strides]
    turned = [strides, strides[::-1]]
    if [radix for _, radix in turned[0]] != [radix for _, radix in turned[1]]:
        turned = same

    def gather(parts, orders, first=0, last=None):
        for (stride, radix), (odd_stride, _) in list(zip(*orders))[first:last]:
            panel = jnp.concatenate(parts, axis=0)
            parts = [panel] + [
                swap_rows(panel, grid_rows, grid_cols, (k * stride, k * odd_stride))
                for k in range(1, radix)
            ]
        return parts

    row = lax.axis_index("row")
    col = lax.axis_index("col")
    early = arrival_order(strides)
    late = [arrival_order(order) for order in turned]
    early_sources = jnp.array(early, jnp.int32) ^ row
    sources = jnp.array(late, jnp.int32)[col % 2] ^ row
    targets = jnp.arange(grid_cols, dtype=jnp.int32) ^ col
    pieces = gather([initial.astype(jnp.bfloat16)], same, last=1)
    dense = build_tile(
        block_rows[0], block_cols[0], block_counts, hamiltonian_blocks[0, 0],
        grid_rows, grid_cols,
    )
    dense = after(dense, pieces[1:])
    received = lax.all_to_all(dense, "row", 0, 0, tiled=True)
    panel = jnp.concatenate(gather(pieces, same, first=1), axis=0)
    turned_panel = turn_panel(early_sources, panel, dense.shape[1])
    turned_panels = [turned_panel] + [
        swap(turned_panel, "col", grid_cols, d) for d in range(1, grid_cols)
    ]
    base, *others = forward_first(
        early_sources, targets, dense, panel, initial, center, halfwidth
    )
    for d, other in enumerate(others, start=1):
        base = base + swap(other, "col", grid_cols, d)

    previous = initial
    current, panel, *stacks = backward_first(
        targets, lay_panels(targets, turned_panels, grid_rows), received, base, halfwidth
    )
    pieces = gather([panel], turned, last=1)
    stacks = [swap(stack, "col", grid_cols, d) for d, stack in enumerate(stacks, start=1)]
    tile = merge_tile(sources, targets, dense, received, stacks)
    for degree_step in range(1, DEGREE):
        if degree_step > 1:
            pieces = gather([current.astype(jnp.bfloat16)], turned, last=1)
        pieces = gather(pieces, turned, first=1)
        base, *others = apply_tile(tile, pieces, current, previous, center, halfwidth, grid_cols)
        following = base
        for d, other in enumerate(others, start=1):
            following = following + swap(other, "col", grid_cols, d)
        previous = current
        current = following
    return current


def solution(mesh):
    in_specs = (
        P("row", "col", None, None, None),
        P("row", "col", None),
        P("row", "col", None),
        P("row", "col"),
        P(("row", "col"), None),
        P(),
        P(),
    )
    out_specs = P(("row", "col"), None)
    return jax.shard_map(body, mesh=mesh, in_specs=in_specs, out_specs=out_specs, check_vma=False)
```

```python
import jax
import jax.numpy as jnp
from jax import lax
from jax.experimental import pallas as pl
from jax.experimental.pallas import tpu as pltpu
from jax.sharding import PartitionSpec as P

DEGREE = 3
RADIX = 4
CHUNK = 8
SPARE = 4 * 2**20

VMEM = pl.BlockSpec(memory_space=pltpu.VMEM)
SMEM = pl.BlockSpec(memory_space=pltpu.SMEM)
HBM = pl.BlockSpec(memory_space=pltpu.HBM)


def stage_strides(size):
    found = []
    stride = 1
    while stride < size:
        radix = RADIX if size % (stride * RADIX) == 0 else size // stride
        found.append((stride, radix))
        stride *= radix
    return found[::-1]


def arrival_order(strides):
    order = [0]
    for stride, radix in strides:
        order = [k * stride ^ offset for k in range(radix) for offset in order]
    return order


def swap(x, axis, size, offset):
    return lax.ppermute(x, axis, [(source, source ^ offset) for source in range(size)])


def swap_rows(x, grid_rows, grid_cols, offsets):
    pairs = [
        (row * grid_cols + col, (row ^ offsets[col % 2]) * grid_cols + col)
        for row in range(grid_rows)
        for col in range(grid_cols)
    ]
    return lax.ppermute(x, ("row", "col"), pairs)


def build_tile(rows, cols, count, stacked, grid_rows, grid_cols):
    slots, orb, _ = stacked.shape
    cells = grid_rows * grid_cols
    parts = 4 if cells % 4 == 0 else 1
    chunk = CHUNK if slots % CHUNK == 0 else slots
    chunks = slots // chunk

    def kernel(
        rows_hbm, cols_hbm, count_ref, stack_hbm, out_hbm,
        stack_ref, acc_ref, dense_ref, rows_ref, cols_ref, index_sems, stack_sems, sems,
    ):
        indices = [
            pltpu.make_async_copy(source, target, index_sems.at[n])
            for n, (source, target) in enumerate([(rows_hbm, rows_ref), (cols_hbm, cols_ref)])
        ]
        for copy in indices:
            copy.start()
        arrivals = []
        for n in range(chunks):
            held = pl.ds(n * chunk, chunk)
            arrivals.append(
                pltpu.make_async_copy(stack_hbm.at[held], stack_ref.at[held], stack_sems.at[n])
            )
            arrivals[-1].start()
        acc_ref[...] = jnp.zeros_like(acc_ref)
        for copy in indices:
            copy.wait()
        count = count_ref[0, 0]
        for n, copy in enumerate(arrivals):
            copy.wait()
            for s in range(n * chunk, (n + 1) * chunk):
                cell = jnp.where(s < count, cols_ref[0, s] * grid_cols + rows_ref[0, s], cells)
                acc_ref[cell] += stack_ref[s].astype(jnp.float32)
        copies = []
        for n in range(parts):
            held = pl.ds(n * (cells // parts), cells // parts)
            dense_ref[held] = acc_ref[held].astype(jnp.bfloat16)
            copies.append(pltpu.make_async_copy(dense_ref.at[held], out_hbm.at[held], sems.at[n]))
            copies[-1].start()
        for copy in copies:
            copy.wait()

    return pl.pallas_call(
        kernel,
        in_specs=[HBM, HBM, SMEM, HBM],
        out_specs=HBM,
        scratch_shapes=[
            pltpu.VMEM(stacked.shape, jnp.bfloat16),
            pltpu.VMEM((cells + 1, orb, orb), jnp.float32),
            pltpu.VMEM((cells, orb, orb), jnp.bfloat16),
            pltpu.SMEM(rows.shape, jnp.int32),
            pltpu.SMEM(cols.shape, jnp.int32),
            pltpu.SemaphoreType.DMA((2,)),
            pltpu.SemaphoreType.DMA((chunks,)),
            pltpu.SemaphoreType.DMA((parts,)),
        ],
        out_shape=pltpu.HBM((cells, orb, orb), jnp.bfloat16),
        compiler_params=pltpu.CompilerParams(
            vmem_limit_bytes=(cells + 1) * orb * orb * 6 + stacked.size * 2 + SPARE
        ),
        name="build_tile",
    )(
        pltpu.with_memory_space_constraint(rows, pltpu.HBM),
        pltpu.with_memory_space_constraint(cols, pltpu.HBM),
        count,
        pltpu.with_memory_space_constraint(stacked, pltpu.HBM),
    )


def after(x, others):
    def kernel(*refs):
        pass

    return pl.pallas_call(
        kernel,
        in_specs=[HBM] + [VMEM] * len(others),
        out_specs=HBM,
        out_shape=pltpu.HBM(x.shape, x.dtype),
        input_output_aliases={0: 0},
        compiler_params=pltpu.CompilerParams(vmem_limit_bytes=SPARE),
        name="after",
    )(pltpu.with_memory_space_constraint(x, pltpu.HBM), *others)


def finish(own, first, current_ref, previous_ref, center_ref, halfwidth_ref):
    scale = (1.0 if first else 2.0) / jnp.full((1, own.shape[1]), halfwidth_ref[0])
    own = (own - center_ref[0] * current_ref[...]) * scale
    return own if first else own - previous_ref[...], scale


def forward_first(sources, targets, dense, panel, current, center, halfwidth):
    cells, orb, _ = dense.shape
    grid_rows = sources.shape[0]
    grid_cols = targets.shape[0]
    vectors = current.shape[1]

    def kernel(
        sources_ref, targets_ref, center_ref, halfwidth_ref,
        dense_hbm, panel_ref, current_ref, *refs,
    ):
        *outs, total_ref, dense_ref, sem = refs
        copy = pltpu.make_async_copy(dense_hbm, dense_ref, sem)
        copy.start()
        copy.wait()
        total = None
        for k in range(grid_rows):
            blocks = dense_ref[pl.ds(sources_ref[k] * grid_cols, grid_cols)]
            part = jnp.dot(
                blocks.reshape(grid_cols * orb, orb), panel_ref[k * orb : (k + 1) * orb],
                preferred_element_type=jnp.float32,
            )
            total = part if total is None else total + part
        total_ref[...] = total.reshape(grid_cols, orb, vectors)
        base, scale = finish(
            total_ref[targets_ref[0]], True, current_ref, None, center_ref, halfwidth_ref
        )
        outs[0][...] = base
        for d in range(1, grid_cols):
            outs[d][...] = total_ref[targets_ref[d]] * scale

    return pl.pallas_call(
        kernel,
        in_specs=[SMEM] * 4 + [HBM] + [VMEM] * 2,
        out_specs=[VMEM] * grid_cols,
        out_shape=[jax.ShapeDtypeStruct((orb, vectors), jnp.float32)] * grid_cols,
        scratch_shapes=[
            pltpu.VMEM((grid_cols, orb, vectors), jnp.float32),
            pltpu.VMEM(dense.shape, dense.dtype),
            pltpu.SemaphoreType.DMA,
        ],
        compiler_params=pltpu.CompilerParams(vmem_limit_bytes=dense.size * 2 + 2 * SPARE),
        name="forward_first",
    )(
        sources, targets, center, halfwidth,
        pltpu.with_memory_space_constraint(dense, pltpu.HBM), panel, current,
    )


def turn_panel(sources, panel, orb):
    grid_rows = sources.shape[0]
    vectors = panel.shape[1]

    def kernel(sources_ref, panel_ref, turned_ref):
        for k in range(grid_rows):
            turned = panel_ref[k * orb : (k + 1) * orb].T
            turned_ref[:, pl.ds(pl.multiple_of(sources_ref[k] * orb, orb), orb)] = turned

    return pl.pallas_call(
        kernel,
        in_specs=[SMEM, VMEM],
        out_specs=VMEM,
        out_shape=jax.ShapeDtypeStruct((vectors, grid_rows * orb), jnp.bfloat16),
        compiler_params=pltpu.CompilerParams(vmem_limit_bytes=panel.size * 4 + SPARE),
        name="turn_panel",
    )(sources, panel)


def lay_panels(targets, turned_panels, grid_rows):
    grid_cols = targets.shape[0]
    vectors, width = turned_panels[0].shape
    orb = width // grid_rows

    def kernel(targets_ref, *refs):
        *turned_refs, out_ref = refs
        for d, turned_ref in enumerate(turned_refs):
            for c in range(grid_rows):
                at = pl.multiple_of((c * grid_cols + targets_ref[d]) * orb, orb)
                out_ref[:, pl.ds(at, orb)] = turned_ref[:, c * orb : (c + 1) * orb]

    return pl.pallas_call(
        kernel,
        in_specs=[SMEM] + [VMEM] * grid_cols,
        out_specs=VMEM,
        out_shape=jax.ShapeDtypeStruct((vectors, grid_cols * width), jnp.bfloat16),
        compiler_params=pltpu.CompilerParams(vmem_limit_bytes=vectors * width * 4 * grid_cols + SPARE),
        name="lay_panels",
    )(targets, *turned_panels)


def backward_first(targets, turned_panels, received, base, halfwidth):
    cells, orb, _ = received.shape
    grid_cols = targets.shape[0]
    grid_rows = cells // grid_cols
    vectors = base.shape[1]

    def kernel(
        targets_ref, halfwidth_ref, turned_ref, received_ref, base_ref, out_ref, panel_ref, *refs
    ):
        *picked, sems = refs
        copies = [
            pltpu.make_async_copy(received_ref.at[:, targets_ref[d]], picked_ref, sems.at[d - 1])
            for d, picked_ref in enumerate(picked, start=1)
        ]
        for copy in copies:
            copy.start()
        blocks = received_ref[...].reshape(cells * orb, orb)
        total = jnp.dot(turned_ref[...], blocks, preferred_element_type=jnp.float32)
        out = base_ref[...] + total.T / jnp.full((1, vectors), halfwidth_ref[0])
        out_ref[...] = out
        panel_ref[...] = out.astype(jnp.bfloat16)
        for copy in copies:
            copy.wait()

    return pl.pallas_call(
        kernel,
        in_specs=[SMEM] * 2 + [VMEM] * 3,
        out_specs=[VMEM] * (1 + grid_cols),
        scratch_shapes=[pltpu.SemaphoreType.DMA((max(grid_cols - 1, 1),))],
        out_shape=[
            jax.ShapeDtypeStruct((orb, vectors), jnp.float32),
            jax.ShapeDtypeStruct((orb, vectors), jnp.bfloat16),
        ]
        + [jax.ShapeDtypeStruct((grid_rows, orb, orb), jnp.bfloat16)] * (grid_cols - 1),
        compiler_params=pltpu.CompilerParams(vmem_limit_bytes=received.size * 6 + 2 * SPARE),
        name="backward_first",
    )(targets, halfwidth, turned_panels, received.reshape(grid_rows, grid_cols, orb, orb), base)


def merge_tile(sources, targets, dense, received, stacks):
    _, orb, _ = dense.shape
    grid_rows = sources.shape[0]
    grid_cols = targets.shape[0]

    def kernel(sources_ref, targets_ref, dense_hbm, received_ref, *refs):
        *stack_refs, tile_ref, dense_ref, sem = refs
        copy = pltpu.make_async_copy(dense_hbm, dense_ref, sem)
        copy.start()
        copy.wait()
        for k in range(grid_rows):
            source = sources_ref[k]
            for d in range(grid_cols):
                cell = source * grid_cols + targets_ref[d]
                turned = received_ref[cell] if d == 0 else stack_refs[d - 1][source]
                own = dense_ref[cell].astype(jnp.float32)
                block = (own + turned.T.astype(jnp.float32)).astype(jnp.bfloat16)
                tile_ref[d * orb : (d + 1) * orb, k * orb : (k + 1) * orb] = block

    return pl.pallas_call(
        kernel,
        in_specs=[SMEM] * 2 + [HBM] + [VMEM] * grid_cols,
        out_specs=VMEM,
        out_shape=jax.ShapeDtypeStruct((grid_cols * orb, grid_rows * orb), jnp.bfloat16),
        scratch_shapes=[pltpu.VMEM(dense.shape, dense.dtype), pltpu.SemaphoreType.DMA],
        compiler_params=pltpu.CompilerParams(vmem_limit_bytes=dense.size * 8 + SPARE),
        name="merge_tile",
    )(
        sources, targets, pltpu.with_memory_space_constraint(dense, pltpu.HBM), received, *stacks
    )


def apply_tile(tile, pieces, current, previous, center, halfwidth, grid_cols):
    height, _ = tile.shape
    orb = height // grid_cols
    vectors = current.shape[1]
    count = len(pieces)

    def kernel(center_ref, halfwidth_ref, tile_ref, current_ref, previous_ref, *refs):
        outs = refs[count:]
        total = None
        at = 0
        for ref in refs[:count]:
            depth = ref.shape[0]
            part = jnp.dot(
                tile_ref[:, at : at + depth], ref[...], preferred_element_type=jnp.float32
            )
            total = part if total is None else total + part
            at += depth
        base, scale = finish(
            total[:orb], False, current_ref, previous_ref, center_ref, halfwidth_ref
        )
        outs[0][...] = base
        for d in range(1, grid_cols):
            outs[d][...] = total[d * orb : (d + 1) * orb] * scale

    return pl.pallas_call(
        kernel,
        in_specs=[SMEM] * 2 + [VMEM] * (3 + count),
        out_specs=[VMEM] * grid_cols,
        out_shape=[jax.ShapeDtypeStruct((orb, vectors), jnp.float32)] * grid_cols,
        compiler_params=pltpu.CompilerParams(vmem_limit_bytes=tile.size * 2 + 2 * SPARE),
        name="apply_tile",
    )(center, halfwidth, tile, current, previous, *pieces)


def body(hamiltonian_blocks, block_rows, block_cols, block_counts, initial, center, halfwidth):
    grid_rows = lax.axis_size("row")
    grid_cols = lax.axis_size("col")
    strides = stage_strides(grid_rows)
    same = [strides, strides]
    turned = [strides, strides[::-1]]
    if [radix for _, radix in turned[0]] != [radix for _, radix in turned[1]]:
        turned = same

    def gather(parts, orders, first=0, last=None):
        for (stride, radix), (odd_stride, _) in list(zip(*orders))[first:last]:
            panel = jnp.concatenate(parts, axis=0)
            parts = [panel] + [
                swap_rows(panel, grid_rows, grid_cols, (k * stride, k * odd_stride))
                for k in range(1, radix)
            ]
        return parts

    row = lax.axis_index("row")
    col = lax.axis_index("col")
    early = arrival_order(strides)
    late = [arrival_order(order) for order in turned]
    early_sources = jnp.array(early, jnp.int32) ^ row
    sources = jnp.array(late, jnp.int32)[col % 2] ^ row
    targets = jnp.arange(grid_cols, dtype=jnp.int32) ^ col
    pieces = gather([initial.astype(jnp.bfloat16)], same, last=1)
    dense = build_tile(
        block_rows[0], block_cols[0], block_counts, hamiltonian_blocks[0, 0],
        grid_rows, grid_cols,
    )
    dense = after(dense, pieces[1:])
    received = lax.all_to_all(dense, "row", 0, 0, tiled=True)
    panel = jnp.concatenate(gather(pieces, same, first=1), axis=0)
    turned_panel = turn_panel(early_sources, panel, dense.shape[1])
    turned_panels = [turned_panel] + [
        swap(turned_panel, "col", grid_cols, d) for d in range(1, grid_cols)
    ]
    base, *others = forward_first(
        early_sources, targets, dense, panel, initial, center, halfwidth
    )
    for d, other in enumerate(others, start=1):
        base = base + swap(other, "col", grid_cols, d)

    previous = initial
    current, panel, *stacks = backward_first(
        targets, lay_panels(targets, turned_panels, grid_rows), received, base, halfwidth
    )
    pieces = gather([panel], turned, last=1)
    stacks = [swap(stack, "col", grid_cols, d) for d, stack in enumerate(stacks, start=1)]
    tile = merge_tile(sources, targets, dense, received, stacks)
    for degree_step in range(1, DEGREE):
        if degree_step > 1:
            pieces = gather([current.astype(jnp.bfloat16)], turned, last=1)
        pieces = gather(pieces, turned, first=1)
        base, *others = apply_tile(tile, pieces, current, previous, center, halfwidth, grid_cols)
        following = base
        for d, other in enumerate(others, start=1):
            following = following + swap(other, "col", grid_cols, d)
        previous = current
        current = following
    return current


def solution(mesh):
    in_specs = (
        P("row", "col", None, None, None),
        P("row", "col", None),
        P("row", "col", None),
        P("row", "col"),
        P(("row", "col"), None),
        P(),
        P(),
    )
    out_specs = P(("row", "col"), None)
    return jax.shard_map(body, mesh=mesh, in_specs=in_specs, out_specs=out_specs, check_vma=False)
```

```python
import jax
import jax.numpy as jnp
from jax import lax
from jax.experimental import pallas as pl
from jax.experimental.pallas import tpu as pltpu
from jax.sharding import PartitionSpec as P

DEGREE = 3
RADIX = 4
CHUNK = 8
SPARE = 4 * 2**20

VMEM = pl.BlockSpec(memory_space=pltpu.VMEM)
SMEM = pl.BlockSpec(memory_space=pltpu.SMEM)
HBM = pl.BlockSpec(memory_space=pltpu.HBM)


def stage_strides(size):
    found = []
    stride = 1
    while stride < size:
        radix = RADIX if size % (stride * RADIX) == 0 else size // stride
        found.append((stride, radix))
        stride *= radix
    return found[::-1]


def arrival_order(strides):
    order = [0]
    for stride, radix in strides:
        order = [k * stride ^ offset for k in range(radix) for offset in order]
    return order


def swap(x, axis, size, offset):
    return lax.ppermute(x, axis, [(source, source ^ offset) for source in range(size)])


def swap_rows(x, grid_rows, grid_cols, offsets):
    pairs = [
        (row * grid_cols + col, (row ^ offsets[col % 2]) * grid_cols + col)
        for row in range(grid_rows)
        for col in range(grid_cols)
    ]
    return lax.ppermute(x, ("row", "col"), pairs)


def build_tile(rows, cols, count, stacked, grid_rows, grid_cols):
    slots, orb, _ = stacked.shape
    cells = grid_rows * grid_cols
    parts = 4 if cells % 4 == 0 else 1
    chunk = CHUNK if slots % CHUNK == 0 else slots
    chunks = slots // chunk

    def kernel(
        rows_hbm, cols_hbm, count_ref, stack_hbm, out_hbm,
        stack_ref, acc_ref, dense_ref, rows_ref, cols_ref, index_sems, stack_sems, sems,
    ):
        indices = [
            pltpu.make_async_copy(source, target, index_sems.at[n])
            for n, (source, target) in enumerate([(rows_hbm, rows_ref), (cols_hbm, cols_ref)])
        ]
        for copy in indices:
            copy.start()
        arrivals = []
        for n in range(chunks):
            held = pl.ds(n * chunk, chunk)
            arrivals.append(
                pltpu.make_async_copy(stack_hbm.at[held], stack_ref.at[held], stack_sems.at[n])
            )
            arrivals[-1].start()
        acc_ref[...] = jnp.zeros_like(acc_ref)
        for copy in indices:
            copy.wait()
        count = count_ref[0, 0]
        for n, copy in enumerate(arrivals):
            copy.wait()
            for s in range(n * chunk, (n + 1) * chunk):
                cell = jnp.where(s < count, cols_ref[0, s] * grid_cols + rows_ref[0, s], cells)
                acc_ref[cell] += stack_ref[s].astype(jnp.float32)
        copies = []
        for n in range(parts):
            held = pl.ds(n * (cells // parts), cells // parts)
            dense_ref[held] = acc_ref[held].astype(jnp.bfloat16)
            copies.append(pltpu.make_async_copy(dense_ref.at[held], out_hbm.at[held], sems.at[n]))
            copies[-1].start()
        for copy in copies:
            copy.wait()

    return pl.pallas_call(
        kernel,
        in_specs=[HBM, HBM, SMEM, HBM],
        out_specs=HBM,
        scratch_shapes=[
            pltpu.VMEM(stacked.shape, jnp.bfloat16),
            pltpu.VMEM((cells + 1, orb, orb), jnp.float32),
            pltpu.VMEM((cells, orb, orb), jnp.bfloat16),
            pltpu.SMEM(rows.shape, jnp.int32),
            pltpu.SMEM(cols.shape, jnp.int32),
            pltpu.SemaphoreType.DMA((2,)),
            pltpu.SemaphoreType.DMA((chunks,)),
            pltpu.SemaphoreType.DMA((parts,)),
        ],
        out_shape=pltpu.HBM((cells, orb, orb), jnp.bfloat16),
        compiler_params=pltpu.CompilerParams(
            vmem_limit_bytes=(cells + 1) * orb * orb * 6 + stacked.size * 2 + SPARE
        ),
        name="build_tile",
    )(
        pltpu.with_memory_space_constraint(rows, pltpu.HBM),
        pltpu.with_memory_space_constraint(cols, pltpu.HBM),
        count,
        pltpu.with_memory_space_constraint(stacked, pltpu.HBM),
    )


def after(x, others):
    def kernel(*refs):
        pass

    return pl.pallas_call(
        kernel,
        in_specs=[HBM] + [VMEM] * len(others),
        out_specs=HBM,
        out_shape=pltpu.HBM(x.shape, x.dtype),
        input_output_aliases={0: 0},
        compiler_params=pltpu.CompilerParams(vmem_limit_bytes=SPARE),
        name="after",
    )(pltpu.with_memory_space_constraint(x, pltpu.HBM), *others)


def finish(own, first, current_ref, previous_ref, center_ref, halfwidth_ref):
    scale = (1.0 if first else 2.0) / jnp.full((1, own.shape[1]), halfwidth_ref[0])
    own = (own - center_ref[0] * current_ref[...]) * scale
    return own if first else own - previous_ref[...], scale


def forward_first(sources, targets, dense, panel, current, center, halfwidth):
    cells, orb, _ = dense.shape
    grid_rows = sources.shape[0]
    grid_cols = targets.shape[0]
    vectors = current.shape[1]

    def kernel(
        sources_ref, targets_ref, center_ref, halfwidth_ref,
        dense_hbm, panel_ref, current_ref, *refs,
    ):
        *outs, total_ref, dense_ref, sem = refs
        copy = pltpu.make_async_copy(dense_hbm, dense_ref, sem)
        copy.start()
        copy.wait()
        total = None
        for k in range(grid_rows):
            blocks = dense_ref[pl.ds(sources_ref[k] * grid_cols, grid_cols)]
            part = jnp.dot(
                blocks.reshape(grid_cols * orb, orb), panel_ref[k * orb : (k + 1) * orb],
                preferred_element_type=jnp.float32,
            )
            total = part if total is None else total + part
        total_ref[...] = total.reshape(grid_cols, orb, vectors)
        base, scale = finish(
            total_ref[targets_ref[0]], True, current_ref, None, center_ref, halfwidth_ref
        )
        outs[0][...] = base
        for d in range(1, grid_cols):
            outs[d][...] = total_ref[targets_ref[d]] * scale

    return pl.pallas_call(
        kernel,
        in_specs=[SMEM] * 4 + [HBM] + [VMEM] * 2,
        out_specs=[VMEM] * grid_cols,
        out_shape=[jax.ShapeDtypeStruct((orb, vectors), jnp.float32)] * grid_cols,
        scratch_shapes=[
            pltpu.VMEM((grid_cols, orb, vectors), jnp.float32),
            pltpu.VMEM(dense.shape, dense.dtype),
            pltpu.SemaphoreType.DMA,
        ],
        compiler_params=pltpu.CompilerParams(vmem_limit_bytes=dense.size * 2 + 2 * SPARE),
        name="forward_first",
    )(
        sources, targets, center, halfwidth,
        pltpu.with_memory_space_constraint(dense, pltpu.HBM), panel, current,
    )


def turn_panel(sources, panel, orb):
    grid_rows = sources.shape[0]
    vectors = panel.shape[1]

    def kernel(sources_ref, panel_ref, turned_ref):
        for k in range(grid_rows):
            turned = panel_ref[k * orb : (k + 1) * orb].T
            turned_ref[:, pl.ds(pl.multiple_of(sources_ref[k] * orb, orb), orb)] = turned

    return pl.pallas_call(
        kernel,
        in_specs=[SMEM, VMEM],
        out_specs=VMEM,
        out_shape=jax.ShapeDtypeStruct((vectors, grid_rows * orb), jnp.bfloat16),
        compiler_params=pltpu.CompilerParams(vmem_limit_bytes=panel.size * 4 + SPARE),
        name="turn_panel",
    )(sources, panel)


def lay_panels(targets, turned_panels, grid_rows):
    grid_cols = targets.shape[0]
    vectors, width = turned_panels[0].shape
    orb = width // grid_rows

    def kernel(targets_ref, *refs):
        *turned_refs, out_ref = refs
        for d, turned_ref in enumerate(turned_refs):
            for c in range(grid_rows):
                at = pl.multiple_of((c * grid_cols + targets_ref[d]) * orb, orb)
                out_ref[:, pl.ds(at, orb)] = turned_ref[:, c * orb : (c + 1) * orb]

    return pl.pallas_call(
        kernel,
        in_specs=[SMEM] + [VMEM] * grid_cols,
        out_specs=VMEM,
        out_shape=jax.ShapeDtypeStruct((vectors, grid_cols * width), jnp.bfloat16),
        compiler_params=pltpu.CompilerParams(vmem_limit_bytes=vectors * width * 4 * grid_cols + SPARE),
        name="lay_panels",
    )(targets, *turned_panels)


def backward_first(turned_panels, received, base, halfwidth):
    cells, orb, _ = received.shape
    vectors = base.shape[1]

    def kernel(halfwidth_ref, turned_ref, received_ref, base_ref, out_ref, panel_ref):
        blocks = received_ref[...].reshape(cells * orb, orb)
        total = jnp.dot(turned_ref[...], blocks, preferred_element_type=jnp.float32)
        out = base_ref[...] + total.T / jnp.full((1, vectors), halfwidth_ref[0])
        out_ref[...] = out
        panel_ref[...] = out.astype(jnp.bfloat16)

    return pl.pallas_call(
        kernel,
        in_specs=[SMEM] + [VMEM] * 3,
        out_specs=[VMEM] * 2,
        out_shape=[
            jax.ShapeDtypeStruct((orb, vectors), jnp.float32),
            jax.ShapeDtypeStruct((orb, vectors), jnp.bfloat16),
        ],
        compiler_params=pltpu.CompilerParams(vmem_limit_bytes=received.size * 4 + 2 * SPARE),
        name="backward_first",
    )(halfwidth, turned_panels, received, base)


def pick_blocks(targets, received, panel, grid_rows):
    _, orb, _ = received.shape
    grid_cols = targets.shape[0]

    def kernel(targets_ref, received_ref, panel_ref, *outs):
        for d, out in enumerate(outs, start=1):
            for c in range(grid_rows):
                out[c] = received_ref[c * grid_cols + targets_ref[d]]

    return pl.pallas_call(
        kernel,
        in_specs=[SMEM, VMEM, VMEM],
        out_specs=[VMEM] * (grid_cols - 1),
        out_shape=[jax.ShapeDtypeStruct((grid_rows, orb, orb), jnp.bfloat16)] * (grid_cols - 1),
        compiler_params=pltpu.CompilerParams(vmem_limit_bytes=received.size * 4 + SPARE),
        name="pick_blocks",
    )(targets, received, panel)


def merge_tile(sources, targets, dense, received, stacks):
    _, orb, _ = dense.shape
    grid_rows = sources.shape[0]
    grid_cols = targets.shape[0]

    def kernel(sources_ref, targets_ref, dense_hbm, received_ref, *refs):
        *stack_refs, tile_ref, dense_ref, sem = refs
        copy = pltpu.make_async_copy(dense_hbm, dense_ref, sem)
        copy.start()
        copy.wait()
        for k in range(grid_rows):
            source = sources_ref[k]
            for d in range(grid_cols):
                cell = source * grid_cols + targets_ref[d]
                turned = received_ref[cell] if d == 0 else stack_refs[d - 1][source]
                own = dense_ref[cell].astype(jnp.float32)
                block = (own + turned.T.astype(jnp.float32)).astype(jnp.bfloat16)
                tile_ref[d * orb : (d + 1) * orb, k * orb : (k + 1) * orb] = block

    return pl.pallas_call(
        kernel,
        in_specs=[SMEM] * 2 + [HBM] + [VMEM] * grid_cols,
        out_specs=VMEM,
        out_shape=jax.ShapeDtypeStruct((grid_cols * orb, grid_rows * orb), jnp.bfloat16),
        scratch_shapes=[pltpu.VMEM(dense.shape, dense.dtype), pltpu.SemaphoreType.DMA],
        compiler_params=pltpu.CompilerParams(vmem_limit_bytes=dense.size * 8 + SPARE),
        name="merge_tile",
    )(
        sources, targets, pltpu.with_memory_space_constraint(dense, pltpu.HBM), received, *stacks
    )


def apply_tile(tile, pieces, current, previous, center, halfwidth, grid_cols):
    height, _ = tile.shape
    orb = height // grid_cols
    vectors = current.shape[1]
    count = len(pieces)

    def kernel(center_ref, halfwidth_ref, tile_ref, current_ref, previous_ref, *refs):
        outs = refs[count:]
        total = None
        at = 0
        for ref in refs[:count]:
            depth = ref.shape[0]
            part = jnp.dot(
                tile_ref[:, at : at + depth], ref[...], preferred_element_type=jnp.float32
            )
            total = part if total is None else total + part
            at += depth
        base, scale = finish(
            total[:orb], False, current_ref, previous_ref, center_ref, halfwidth_ref
        )
        outs[0][...] = base
        for d in range(1, grid_cols):
            outs[d][...] = total[d * orb : (d + 1) * orb] * scale

    return pl.pallas_call(
        kernel,
        in_specs=[SMEM] * 2 + [VMEM] * (3 + count),
        out_specs=[VMEM] * grid_cols,
        out_shape=[jax.ShapeDtypeStruct((orb, vectors), jnp.float32)] * grid_cols,
        compiler_params=pltpu.CompilerParams(vmem_limit_bytes=tile.size * 2 + 2 * SPARE),
        name="apply_tile",
    )(center, halfwidth, tile, current, previous, *pieces)


def body(hamiltonian_blocks, block_rows, block_cols, block_counts, initial, center, halfwidth):
    grid_rows = lax.axis_size("row")
    grid_cols = lax.axis_size("col")
    strides = stage_strides(grid_rows)
    same = [strides, strides]
    turned = [strides, strides[::-1]]
    if [radix for _, radix in turned[0]] != [radix for _, radix in turned[1]]:
        turned = same

    def gather(parts, orders, first=0, last=None):
        for (stride, radix), (odd_stride, _) in list(zip(*orders))[first:last]:
            panel = jnp.concatenate(parts, axis=0)
            digits = range(radix - 1, 0, -1) if len(parts) > 1 else range(1, radix)
            found = {
                k: swap_rows(panel, grid_rows, grid_cols, (k * stride, k * odd_stride))
                for k in digits
            }
            parts = [panel] + [found[k] for k in range(1, radix)]
        return parts

    row = lax.axis_index("row")
    col = lax.axis_index("col")
    early = arrival_order(strides)
    late = [arrival_order(order) for order in turned]
    early_sources = jnp.array(early, jnp.int32) ^ row
    sources = jnp.array(late, jnp.int32)[col % 2] ^ row
    targets = jnp.arange(grid_cols, dtype=jnp.int32) ^ col
    pieces = gather([initial.astype(jnp.bfloat16)], same, last=1)
    dense = build_tile(
        block_rows[0], block_cols[0], block_counts, hamiltonian_blocks[0, 0],
        grid_rows, grid_cols,
    )
    dense = after(dense, pieces[1:])
    received = lax.all_to_all(dense, "row", 0, 0, tiled=True)
    panel = jnp.concatenate(gather(pieces, same, first=1), axis=0)
    turned_panel = turn_panel(early_sources, panel, dense.shape[1])
    turned_panels = [turned_panel] + [
        swap(turned_panel, "col", grid_cols, d) for d in range(1, grid_cols)
    ]
    base, *others = forward_first(
        early_sources, targets, dense, panel, initial, center, halfwidth
    )
    for d, other in enumerate(others, start=1):
        base = base + swap(other, "col", grid_cols, d)

    previous = initial
    current, panel = backward_first(lay_panels(targets, turned_panels, grid_rows), received, base, halfwidth)
    pieces = gather([panel], turned, last=1)
    stacks = []
    if grid_cols > 1:
        stacks = pick_blocks(targets, received, pieces[-1], grid_rows)
    stacks = [swap(stack, "col", grid_cols, d) for d, stack in enumerate(stacks, start=1)]
    tile = merge_tile(sources, targets, dense, received, stacks)
    for degree_step in range(1, DEGREE):
        if degree_step > 1:
            pieces = gather([current.astype(jnp.bfloat16)], turned, last=1)
        pieces = gather(pieces, turned, first=1)
        base, *others = apply_tile(tile, pieces, current, previous, center, halfwidth, grid_cols)
        following = base
        for d, other in enumerate(others, start=1):
            following = following + swap(other, "col", grid_cols, d)
        previous = current
        current = following
    return current


def solution(mesh):
    in_specs = (
        P("row", "col", None, None, None),
        P("row", "col", None),
        P("row", "col", None),
        P("row", "col"),
        P(("row", "col"), None),
        P(),
        P(),
    )
    out_specs = P(("row", "col"), None)
    return jax.shard_map(body, mesh=mesh, in_specs=in_specs, out_specs=out_specs, check_vma=False)
```

```python
import jax
import jax.numpy as jnp
from jax import lax
from jax.experimental import pallas as pl
from jax.experimental.pallas import tpu as pltpu
from jax.sharding import PartitionSpec as P

DEGREE = 3
RADIX = 4
CHUNK = 16
SPARE = 4 * 2**20

VMEM = pl.BlockSpec(memory_space=pltpu.VMEM)
SMEM = pl.BlockSpec(memory_space=pltpu.SMEM)
HBM = pl.BlockSpec(memory_space=pltpu.HBM)


def stage_strides(size):
    found = []
    stride = 1
    while stride < size:
        radix = RADIX if size % (stride * RADIX) == 0 else size // stride
        found.append((stride, radix))
        stride *= radix
    return found[::-1]


def arrival_order(strides):
    order = [0]
    for stride, radix in strides:
        order = [k * stride ^ offset for k in range(radix) for offset in order]
    return order


def swap(x, axis, size, offset):
    return lax.ppermute(x, axis, [(source, source ^ offset) for source in range(size)])


def swap_rows(x, grid_rows, grid_cols, offsets):
    pairs = [
        (row * grid_cols + col, (row ^ offsets[col % 2]) * grid_cols + col)
        for row in range(grid_rows)
        for col in range(grid_cols)
    ]
    return lax.ppermute(x, ("row", "col"), pairs)


def build_tile(rows, cols, count, stacked, grid_rows, grid_cols):
    slots, orb, _ = stacked.shape
    cells = grid_rows * grid_cols
    parts = 4 if cells % 4 == 0 else 1
    chunk = CHUNK if slots % CHUNK == 0 else slots
    chunks = slots // chunk

    def kernel(
        rows_hbm, cols_hbm, count_ref, stack_hbm, out_hbm,
        stack_ref, acc_ref, dense_ref, rows_ref, cols_ref, index_sems, stack_sems, sems,
    ):
        indices = [
            pltpu.make_async_copy(source, target, index_sems.at[n])
            for n, (source, target) in enumerate([(rows_hbm, rows_ref), (cols_hbm, cols_ref)])
        ]
        for copy in indices:
            copy.start()
        arrivals = []
        for n in range(chunks):
            held = pl.ds(n * chunk, chunk)
            arrivals.append(
                pltpu.make_async_copy(stack_hbm.at[held], stack_ref.at[held], stack_sems.at[n])
            )
            arrivals[-1].start()
        acc_ref[...] = jnp.zeros_like(acc_ref)
        for copy in indices:
            copy.wait()
        count = count_ref[0, 0]
        for n, copy in enumerate(arrivals):
            copy.wait()
            for s in range(n * chunk, (n + 1) * chunk):
                cell = jnp.where(s < count, cols_ref[0, s] * grid_cols + rows_ref[0, s], cells)
                acc_ref[cell] += stack_ref[s].astype(jnp.float32)
        copies = []
        for n in range(parts):
            held = pl.ds(n * (cells // parts), cells // parts)
            dense_ref[held] = acc_ref[held].astype(jnp.bfloat16)
            copies.append(pltpu.make_async_copy(dense_ref.at[held], out_hbm.at[held], sems.at[n]))
            copies[-1].start()
        for copy in copies:
            copy.wait()

    return pl.pallas_call(
        kernel,
        in_specs=[HBM, HBM, SMEM, HBM],
        out_specs=HBM,
        scratch_shapes=[
            pltpu.VMEM(stacked.shape, jnp.bfloat16),
            pltpu.VMEM((cells + 1, orb, orb), jnp.float32),
            pltpu.VMEM((cells, orb, orb), jnp.bfloat16),
            pltpu.SMEM(rows.shape, jnp.int32),
            pltpu.SMEM(cols.shape, jnp.int32),
            pltpu.SemaphoreType.DMA((2,)),
            pltpu.SemaphoreType.DMA((chunks,)),
            pltpu.SemaphoreType.DMA((parts,)),
        ],
        out_shape=pltpu.HBM((cells, orb, orb), jnp.bfloat16),
        compiler_params=pltpu.CompilerParams(
            vmem_limit_bytes=(cells + 1) * orb * orb * 6 + stacked.size * 2 + SPARE
        ),
        name="build_tile",
    )(
        pltpu.with_memory_space_constraint(rows, pltpu.HBM),
        pltpu.with_memory_space_constraint(cols, pltpu.HBM),
        count,
        pltpu.with_memory_space_constraint(stacked, pltpu.HBM),
    )


def after(x, others):
    def kernel(*refs):
        pass

    return pl.pallas_call(
        kernel,
        in_specs=[HBM] + [VMEM] * len(others),
        out_specs=HBM,
        out_shape=pltpu.HBM(x.shape, x.dtype),
        input_output_aliases={0: 0},
        compiler_params=pltpu.CompilerParams(vmem_limit_bytes=SPARE),
        name="after",
    )(pltpu.with_memory_space_constraint(x, pltpu.HBM), *others)


def finish(own, first, current_ref, previous_ref, center_ref, halfwidth_ref):
    scale = (1.0 if first else 2.0) / jnp.full((1, own.shape[1]), halfwidth_ref[0])
    own = (own - center_ref[0] * current_ref[...]) * scale
    return own if first else own - previous_ref[...], scale


def forward_first(sources, targets, dense, panel, current, center, halfwidth):
    cells, orb, _ = dense.shape
    grid_rows = sources.shape[0]
    grid_cols = targets.shape[0]
    vectors = current.shape[1]

    def kernel(
        sources_ref, targets_ref, center_ref, halfwidth_ref,
        dense_hbm, panel_ref, current_ref, *refs,
    ):
        *outs, total_ref, dense_ref, sem = refs
        copy = pltpu.make_async_copy(dense_hbm, dense_ref, sem)
        copy.start()
        copy.wait()
        total = None
        for k in range(grid_rows):
            blocks = dense_ref[pl.ds(sources_ref[k] * grid_cols, grid_cols)]
            part = jnp.dot(
                blocks.reshape(grid_cols * orb, orb), panel_ref[k * orb : (k + 1) * orb],
                preferred_element_type=jnp.float32,
            )
            total = part if total is None else total + part
        total_ref[...] = total.reshape(grid_cols, orb, vectors)
        base, scale = finish(
            total_ref[targets_ref[0]], True, current_ref, None, center_ref, halfwidth_ref
        )
        outs[0][...] = base
        for d in range(1, grid_cols):
            outs[d][...] = total_ref[targets_ref[d]] * scale

    return pl.pallas_call(
        kernel,
        in_specs=[SMEM] * 4 + [HBM] + [VMEM] * 2,
        out_specs=[VMEM] * grid_cols,
        out_shape=[jax.ShapeDtypeStruct((orb, vectors), jnp.float32)] * grid_cols,
        scratch_shapes=[
            pltpu.VMEM((grid_cols, orb, vectors), jnp.float32),
            pltpu.VMEM(dense.shape, dense.dtype),
            pltpu.SemaphoreType.DMA,
        ],
        compiler_params=pltpu.CompilerParams(vmem_limit_bytes=dense.size * 2 + 2 * SPARE),
        name="forward_first",
    )(
        sources, targets, center, halfwidth,
        pltpu.with_memory_space_constraint(dense, pltpu.HBM), panel, current,
    )


def turn_panel(sources, panel, orb):
    grid_rows = sources.shape[0]
    vectors = panel.shape[1]

    def kernel(sources_ref, panel_ref, turned_ref):
        for k in range(grid_rows):
            turned = panel_ref[k * orb : (k + 1) * orb].T
            turned_ref[:, pl.ds(pl.multiple_of(sources_ref[k] * orb, orb), orb)] = turned

    return pl.pallas_call(
        kernel,
        in_specs=[SMEM, VMEM],
        out_specs=VMEM,
        out_shape=jax.ShapeDtypeStruct((vectors, grid_rows * orb), jnp.bfloat16),
        compiler_params=pltpu.CompilerParams(vmem_limit_bytes=panel.size * 4 + SPARE),
        name="turn_panel",
    )(sources, panel)


def lay_panels(targets, turned_panels, grid_rows):
    grid_cols = targets.shape[0]
    vectors, width = turned_panels[0].shape
    orb = width // grid_rows

    def kernel(targets_ref, *refs):
        *turned_refs, out_ref = refs
        for d, turned_ref in enumerate(turned_refs):
            for c in range(grid_rows):
                at = pl.multiple_of((c * grid_cols + targets_ref[d]) * orb, orb)
                out_ref[:, pl.ds(at, orb)] = turned_ref[:, c * orb : (c + 1) * orb]

    return pl.pallas_call(
        kernel,
        in_specs=[SMEM] + [VMEM] * grid_cols,
        out_specs=VMEM,
        out_shape=jax.ShapeDtypeStruct((vectors, grid_cols * width), jnp.bfloat16),
        compiler_params=pltpu.CompilerParams(vmem_limit_bytes=vectors * width * 4 * grid_cols + SPARE),
        name="lay_panels",
    )(targets, *turned_panels)


def backward_first(turned_panels, received, base, halfwidth):
    cells, orb, _ = received.shape
    vectors = base.shape[1]

    def kernel(halfwidth_ref, turned_ref, received_ref, base_ref, out_ref, panel_ref):
        blocks = received_ref[...].reshape(cells * orb, orb)
        total = jnp.dot(turned_ref[...], blocks, preferred_element_type=jnp.float32)
        out = base_ref[...] + total.T / jnp.full((1, vectors), halfwidth_ref[0])
        out_ref[...] = out
        panel_ref[...] = out.astype(jnp.bfloat16)

    return pl.pallas_call(
        kernel,
        in_specs=[SMEM] + [VMEM] * 3,
        out_specs=[VMEM] * 2,
        out_shape=[
            jax.ShapeDtypeStruct((orb, vectors), jnp.float32),
            jax.ShapeDtypeStruct((orb, vectors), jnp.bfloat16),
        ],
        compiler_params=pltpu.CompilerParams(vmem_limit_bytes=received.size * 4 + 2 * SPARE),
        name="backward_first",
    )(halfwidth, turned_panels, received, base)


def pick_blocks(targets, received, panel, grid_rows):
    _, orb, _ = received.shape
    grid_cols = targets.shape[0]

    def kernel(targets_ref, received_ref, panel_ref, *outs):
        for d, out in enumerate(outs, start=1):
            for c in range(grid_rows):
                out[c] = received_ref[c * grid_cols + targets_ref[d]]

    return pl.pallas_call(
        kernel,
        in_specs=[SMEM, VMEM, VMEM],
        out_specs=[VMEM] * (grid_cols - 1),
        out_shape=[jax.ShapeDtypeStruct((grid_rows, orb, orb), jnp.bfloat16)] * (grid_cols - 1),
        compiler_params=pltpu.CompilerParams(vmem_limit_bytes=received.size * 4 + SPARE),
        name="pick_blocks",
    )(targets, received, panel)


def merge_tile(sources, targets, dense, received, stacks):
    _, orb, _ = dense.shape
    grid_rows = sources.shape[0]
    grid_cols = targets.shape[0]

    def kernel(sources_ref, targets_ref, dense_hbm, received_ref, *refs):
        *stack_refs, tile_ref, dense_ref, sem = refs
        copy = pltpu.make_async_copy(dense_hbm, dense_ref, sem)
        copy.start()
        copy.wait()
        for k in range(grid_rows):
            source = sources_ref[k]
            for d in range(grid_cols):
                cell = source * grid_cols + targets_ref[d]
                turned = received_ref[cell] if d == 0 else stack_refs[d - 1][source]
                own = dense_ref[cell].astype(jnp.float32)
                block = (own + turned.T.astype(jnp.float32)).astype(jnp.bfloat16)
                tile_ref[d * orb : (d + 1) * orb, k * orb : (k + 1) * orb] = block

    return pl.pallas_call(
        kernel,
        in_specs=[SMEM] * 2 + [HBM] + [VMEM] * grid_cols,
        out_specs=VMEM,
        out_shape=jax.ShapeDtypeStruct((grid_cols * orb, grid_rows * orb), jnp.bfloat16),
        scratch_shapes=[pltpu.VMEM(dense.shape, dense.dtype), pltpu.SemaphoreType.DMA],
        compiler_params=pltpu.CompilerParams(vmem_limit_bytes=dense.size * 8 + SPARE),
        name="merge_tile",
    )(
        sources, targets, pltpu.with_memory_space_constraint(dense, pltpu.HBM), received, *stacks
    )


def apply_tile(tile, pieces, current, previous, center, halfwidth, grid_cols):
    height, _ = tile.shape
    orb = height // grid_cols
    vectors = current.shape[1]
    count = len(pieces)

    def kernel(center_ref, halfwidth_ref, tile_ref, current_ref, previous_ref, *refs):
        outs = refs[count:]
        total = None
        at = 0
        for ref in refs[:count]:
            depth = ref.shape[0]
            part = jnp.dot(
                tile_ref[:, at : at + depth], ref[...], preferred_element_type=jnp.float32
            )
            total = part if total is None else total + part
            at += depth
        base, scale = finish(
            total[:orb], False, current_ref, previous_ref, center_ref, halfwidth_ref
        )
        outs[0][...] = base
        for d in range(1, grid_cols):
            outs[d][...] = total[d * orb : (d + 1) * orb] * scale

    return pl.pallas_call(
        kernel,
        in_specs=[SMEM] * 2 + [VMEM] * (3 + count),
        out_specs=[VMEM] * grid_cols,
        out_shape=[jax.ShapeDtypeStruct((orb, vectors), jnp.float32)] * grid_cols,
        compiler_params=pltpu.CompilerParams(vmem_limit_bytes=tile.size * 2 + 2 * SPARE),
        name="apply_tile",
    )(center, halfwidth, tile, current, previous, *pieces)


def body(hamiltonian_blocks, block_rows, block_cols, block_counts, initial, center, halfwidth):
    grid_rows = lax.axis_size("row")
    grid_cols = lax.axis_size("col")
    strides = stage_strides(grid_rows)
    same = [strides, strides]
    turned = [strides, strides[::-1]]
    if [radix for _, radix in turned[0]] != [radix for _, radix in turned[1]]:
        turned = same

    def gather(parts, orders, first=0, last=None):
        for (stride, radix), (odd_stride, _) in list(zip(*orders))[first:last]:
            panel = jnp.concatenate(parts, axis=0)
            parts = [panel] + [
                swap_rows(panel, grid_rows, grid_cols, (k * stride, k * odd_stride))
                for k in range(1, radix)
            ]
        return parts

    row = lax.axis_index("row")
    col = lax.axis_index("col")
    early = arrival_order(strides)
    late = [arrival_order(order) for order in turned]
    early_sources = jnp.array(early, jnp.int32) ^ row
    sources = jnp.array(late, jnp.int32)[col % 2] ^ row
    targets = jnp.arange(grid_cols, dtype=jnp.int32) ^ col
    pieces = gather([initial.astype(jnp.bfloat16)], same, last=1)
    dense = build_tile(
        block_rows[0], block_cols[0], block_counts, hamiltonian_blocks[0, 0],
        grid_rows, grid_cols,
    )
    dense = after(dense, pieces[1:])
    received = lax.all_to_all(dense, "row", 0, 0, tiled=True)
    panel = jnp.concatenate(gather(pieces, same, first=1), axis=0)
    turned_panel = turn_panel(early_sources, panel, dense.shape[1])
    turned_panels = [turned_panel] + [
        swap(turned_panel, "col", grid_cols, d) for d in range(1, grid_cols)
    ]
    base, *others = forward_first(
        early_sources, targets, dense, panel, initial, center, halfwidth
    )
    for d, other in enumerate(others, start=1):
        base = base + swap(other, "col", grid_cols, d)

    previous = initial
    current, panel = backward_first(lay_panels(targets, turned_panels, grid_rows), received, base, halfwidth)
    pieces = gather([panel], turned, last=1)
    stacks = []
    if grid_cols > 1:
        stacks = pick_blocks(targets, received, pieces[-1], grid_rows)
    stacks = [swap(stack, "col", grid_cols, d) for d, stack in enumerate(stacks, start=1)]
    tile = merge_tile(sources, targets, dense, received, stacks)
    for degree_step in range(1, DEGREE):
        if degree_step > 1:
            pieces = gather([current.astype(jnp.bfloat16)], turned, last=1)
        pieces = gather(pieces, turned, first=1)
        base, *others = apply_tile(tile, pieces, current, previous, center, halfwidth, grid_cols)
        following = base
        for d, other in enumerate(others, start=1):
            following = following + swap(other, "col", grid_cols, d)
        previous = current
        current = following
    return current


def solution(mesh):
    in_specs = (
        P("row", "col", None, None, None),
        P("row", "col", None),
        P("row", "col", None),
        P("row", "col"),
        P(("row", "col"), None),
        P(),
        P(),
    )
    out_specs = P(("row", "col"), None)
    return jax.shard_map(body, mesh=mesh, in_specs=in_specs, out_specs=out_specs, check_vma=False)
```
